32 devices in a mesh: seq: 16 (over z, x, core), mp: 2 (over y).
Axes of the slice: x: 2, y: 2, z: 4, core: 2. Of those that a mesh axis runs over, the one named last changes fastest.
Arguments:
- stream_one: float32 [2048, 1024], P('seq'), may hold values from -6 to 6
- stream_two: float32 [2048, 1024], P('seq'), may hold values from -6 to 6
- cotangent_one: float32 [2048, 1024], P('seq'), may hold values from -6 to 6
- cotangent_two: float32 [2048, 1024], P('seq'), may hold values from -6 to 6
- bucket_numbers: int32 [2, 4, 8, 2048], P(None, None, 'mp'), may hold values from 0 to 31, as said below
- query_weight: bfloat16 [2, 1024, 1024], P(None, None, 'mp'), may hold values from -0.25 to 0.25
- value_weight: bfloat16 [2, 1024, 1024], P(None, None, 'mp'), may hold values from -0.1875 to 0.1875
- mixing_weight: bfloat16 [2, 1024, 1024], P(None, 'mp'), may hold values from -0.75 to 0.75
- mixing_bias: float32 [2, 1024], replicated, may hold values from -3 to 3
- expand_weight: bfloat16 [2, 1024, 4096], P(None, None, 'mp'), may hold values from -0.1875 to 0.1875
- expand_bias: float32 [2, 4096], P(None, 'mp'), may hold values from -3 to 3
- shrink_weight: bfloat16 [2, 4096, 1024], P(None, 'mp'), may hold values from -0.125 to 0.125
- shrink_bias: float32 [2, 1024], replicated, may hold values from -3 to 3
- attention_gain: float32 [2, 1024], replicated, may hold values from 0.1 to 1.9
- attention_shift: float32 [2, 1024], replicated, may hold values from -3 to 3
- forward_gain: float32 [2, 1024], replicated, may hold values from 0.1 to 1.9
- forward_shift: float32 [2, 1024], replicated, may hold values from -3 to 3
Outputs:
- result_one: float32 [2048, 1024], P('seq')
- result_two: float32 [2048, 1024], P('seq')
- gradient_one: float32 [2048, 1024], P('seq')
- gradient_two: float32 [2048, 1024], P('seq')
- weight_query: float32 [2, 1024, 1024], P(None, 'seq', 'mp')
- weight_value: float32 [2, 1024, 1024], P(None, 'seq', 'mp')
- weight_mixing: float32 [2, 1024, 1024], P(None, ('mp', 'seq'))
- bias_mixing: float32 [2, 1024], P(None, 'seq')
- weight_expand: float32 [2, 1024, 4096], P(None, 'seq', 'mp')
- bias_expand: float32 [2, 4096], P(None, ('mp', 'seq'))
- weight_shrink: float32 [2, 4096, 1024], P(None, ('mp', 'seq'))
- bias_shrink: float32 [2, 1024], P(None, 'seq')
- gain_attention: float32 [2, 1024], P(None, 'seq')
- shift_attention: float32 [2, 1024], P(None, 'seq')
- gain_forward: float32 [2, 1024], P(None, 'seq')
- shift_forward: float32 [2, 1024], P(None, 'seq')
The draws below stay inside these ranges and needn't reach their ends.
Inputs may be any that keep to these rules, and one draw needn't show every extreme that they name: `bucket_numbers`: for every layer, round and head, the tokens whose bucket number lies in bucket numbers p * (2) to (p + 1) * 2 - 1 are exactly 128 for every p, so that sorted rows p * 128 to (p + 1) * 128 - 1 are these tokens; of one block of 128 consecutive positions at most 16 lie in one such range. Buckets hold uneven numbers of tokens.
All inputs are finite; a program needn't handle non-finite values.
Results may differ from the reference program's by a relative error of at most 0.014.
Values may be sent and summed in bfloat16 or wider, within the bound.
A program may use at most 192 MiB of HBM per device.

```python
import math
import jax
import jax.numpy as jnp
from jax import lax

D = 1024
HEADS = 8
DH = 128
FF = 4096
SPAN = 64
ROUNDS = 4
LAYERS = 2
TOK_DEV = 128
TOKENS = 2048


def draw_bucket_numbers(key, part):
    key = jax.random.fold_in(key, 7)
    groups = TOKENS // TOK_DEV
    unit = TOK_DEV // groups
    per_owner = TOK_DEV // SPAN
    list_count = LAYERS * ROUNDS * HEADS

    def one_list(subkey):
        perm_key, amount_key, label_key, bucket_key = jax.random.split(subkey, 4)
        offsets = jax.random.permutation(perm_key, groups)
        amounts = jax.random.randint(amount_key, (groups // 2,), 0, unit + 1).astype(jnp.int32)
        amounts = amounts.at[0].set(unit)
        paired = jnp.stack([unit + amounts, unit - amounts], axis=1).reshape(groups)
        weights = jnp.zeros((groups,), jnp.int32).at[offsets].set(paired)
        bounds = jnp.cumsum(weights)
        labels = jnp.searchsorted(bounds, jnp.arange(TOK_DEV, dtype=jnp.int32), side='right').astype(jnp.int32)
        shuffled = jax.vmap(lambda label_sub: jax.random.permutation(label_sub, labels))(jax.random.split(label_key, groups))
        owners = (jnp.arange(groups, dtype=jnp.int32)[:, None] + shuffled) % groups
        inner = jax.random.randint(bucket_key, (groups, TOK_DEV), 0, per_owner).astype(jnp.int32)
        return (owners * per_owner + inner).reshape(TOKENS)
    buckets = jax.vmap(one_list)(jax.random.split(key, list_count))
    return buckets.reshape(LAYERS, ROUNDS, HEADS, TOKENS).astype(jnp.int32)


def with_spikes(entries, stream_key, source, target, parts, factor):
    owner, partner = [(jnp.arange(entries.shape[dim]) // (entries.shape[dim] // parts)).reshape([-1 if axis == dim else 1 for axis in range(entries.ndim)]) for dim in (source, target)]
    chosen = jax.random.permutation(stream_key, parts)[partner]
    strong = (owner == chosen) | (owner == (partner + parts // 2) % parts)
    return jnp.where(strong, factor * entries, entries)


def block_scale(rng, shape, cuts, least, top_value):
    level = 1.0
    for dim, shards_of in cuts:
        steps = jax.random.uniform(jax.random.fold_in(jax.random.fold_in(rng, 6), dim), (shards_of,), jnp.float32, least / len(cuts), top_value / len(cuts))
        level = level * jnp.repeat(jnp.exp(steps), shape[dim] // shards_of).reshape((-1,) + (1,) * (len(shape) - 1 - dim))
    return level


def bell_draw(rng, extent, width, limit, shards=(), kind=jnp.bfloat16):
    factor_of = block_scale(rng, extent, shards, -0.22, 0.18) if shards else 1.0
    values = jax.random.normal(rng, extent, jnp.float32) * width * factor_of
    return jnp.minimum(jnp.maximum(values, -limit), limit).astype(kind)


def gaussian_with(key, shape, width, limit, cuts, heavy, kind=jnp.bfloat16):
    entries = width * jax.random.normal(key, shape, jnp.float32)
    if cuts:
        entries = entries * block_scale(key, shape, cuts, -0.22, 0.18)
    return jnp.clip(with_spikes(entries, jax.random.fold_in(key, 3), *heavy), -limit, limit).astype(kind)


def setup_inputs(seed: int = 0) -> dict:
    keys = jax.random.split(jax.random.key(seed), 18)
    stream_one = bell_draw(keys[0], (TOKENS, D), 1.0, 6.0, ((0, 16),), jnp.float32)
    stream_two = bell_draw(keys[1], (TOKENS, D), 1.0, 6.0, ((0, 16),), jnp.float32)
    cotangent_one = gaussian_with(keys[2], (TOKENS, D), 1.0, 6.0, ((0, 16),), (0, 1, 16, 2.0), jnp.float32)
    cotangent_two = gaussian_with(keys[3], (TOKENS, D), 1.0, 6.0, ((0, 16),), (0, 1, 16, 2.0), jnp.float32)
    bucket_numbers = draw_bucket_numbers(jax.random.fold_in(keys[17], 71), 0)
    query_weight = bell_draw(keys[5], (LAYERS, D, HEADS * DH), (D // 2) ** -0.5, 0.25, ((2, 2),))
    value_weight = bell_draw(keys[6], (LAYERS, D, HEADS * DH), D ** -0.5, 0.1875, ((2, 2),))
    mixing_weight = bell_draw(keys[7], (LAYERS, HEADS * DH, D), (HEADS * DH // 16) ** -0.5, 0.75, ((1, 2),))
    mixing_bias = bell_draw(keys[8], (LAYERS, D), 0.5, 3.0, (), jnp.float32)
    expand_weight = bell_draw(keys[9], (LAYERS, D, FF), D ** -0.5, 0.1875, ((2, 2),))
    expand_bias = bell_draw(keys[10], (LAYERS, FF), 0.5, 3.0, ((1, 2),), jnp.float32)
    shrink_weight = bell_draw(keys[11], (LAYERS, FF, D), (FF // 2) ** -0.5, 0.125, ((1, 2),))
    shrink_bias = bell_draw(keys[12], (LAYERS, D), 0.5, 3.0, (), jnp.float32)
    attention_gain = jnp.clip(1.0 + 0.18 * jax.random.normal(keys[13], (LAYERS, D), jnp.float32), 0.1, 1.9)
    attention_shift = bell_draw(keys[14], (LAYERS, D), 0.5, 3.0, (), jnp.float32)
    forward_gain = jnp.clip(1.0 + 0.18 * jax.random.normal(keys[15], (LAYERS, D), jnp.float32), 0.1, 1.9)
    forward_shift = bell_draw(keys[16], (LAYERS, D), 0.5, 3.0, (), jnp.float32)
    return {"stream_one": stream_one, "stream_two": stream_two, "cotangent_one": cotangent_one, "cotangent_two": cotangent_two, "bucket_numbers": bucket_numbers, "query_weight": query_weight, "value_weight": value_weight, "mixing_weight": mixing_weight, "mixing_bias": mixing_bias, "expand_weight": expand_weight, "expand_bias": expand_bias, "shrink_weight": shrink_weight, "shrink_bias": shrink_bias, "attention_gain": attention_gain, "attention_shift": attention_shift, "forward_gain": forward_gain, "forward_shift": forward_shift}


@jax.custom_vjp
def low(v):
    return lax.optimization_barrier(v.astype(jnp.bfloat16)).astype(jnp.float32)

@jax.custom_vjp
def low_back(v):
    return v

def low_keep(v):
    return (low(v), None)

def low_pass(kept, grad):
    return (grad,)

def back_keep(v):
    return (v, None)

def back_low(kept, grad):
    return (low(grad),)
low.defvjp(low_keep, low_pass)
low_back.defvjp(back_keep, back_low)
precise = lax.Precision.HIGHEST

def matmul(left_side, right_side):
    return jnp.dot(left_side, right_side, preferred_element_type=jnp.float32, precision=precise)

def layer_norm(values, scale_row, shift_row):
    center = values - lax.optimization_barrier(jnp.mean(values, axis=-1, keepdims=True))
    spread = lax.optimization_barrier(jnp.mean(center * center, axis=-1, keepdims=True))
    return center * lax.rsqrt(spread + 1e-05) * scale_row + shift_row

def normalize(key_rows):
    return key_rows * lax.rsqrt(lax.optimization_barrier(jnp.mean(key_rows * key_rows, axis=-1, keepdims=True)) + 1e-06)

def combine(outputs, logsums):
    highest = lax.optimization_barrier(jnp.max(logsums, axis=0, keepdims=True))
    powers = jnp.exp(logsums - highest)
    shares = powers / lax.optimization_barrier(jnp.sum(powers, axis=0, keepdims=True))
    return lax.optimization_barrier(jnp.sum(shares[..., None] * outputs, axis=0))

def span_attend(queries, values):
    span_count = queries.shape[0] // SPAN
    blocks = queries.reshape(span_count, SPAN, DH)
    value_blocks = values.reshape(span_count, SPAN, DH)
    key_rows = jnp.concatenate([blocks, jnp.roll(blocks, 1, axis=0)], axis=1)
    key_values = jnp.concatenate([value_blocks, jnp.roll(value_blocks, 1, axis=0)], axis=1)
    normed = low(normalize(key_rows))
    scores = jnp.einsum('cid,cjd->cij', blocks, normed, precision=precise) / math.sqrt(DH)
    diagonal = jnp.arange(SPAN)[:, None] == jnp.arange(2 * SPAN)[None, :]
    scores = jnp.where(diagonal, -1000000000.0, scores)
    highest = lax.optimization_barrier(jnp.max(scores, axis=-1, keepdims=True))
    powers = jnp.exp(scores - highest)
    summed = lax.optimization_barrier(jnp.sum(powers, axis=-1, keepdims=True))
    weights = low(powers / summed)
    output = jnp.einsum('cij,cjd->cid', weights, key_values, precision=precise)
    return (output.reshape(-1, DH), (highest + jnp.log(summed)).reshape(-1))

def lsh_attention(normed, query_weight, value_weight, buckets):
    queries = low(low_back(matmul(normed, query_weight)))
    values = low(low_back(matmul(normed, value_weight)))
    head_queries = queries.reshape(-1, HEADS, DH).transpose(1, 0, 2)
    head_values = values.reshape(-1, HEADS, DH).transpose(1, 0, 2)
    flat_buckets = buckets.reshape(ROUNDS * HEADS, -1)

    def single(member_index):
        row_order = jnp.argsort(flat_buckets[member_index], stable=True).astype(jnp.int32)
        inverse = jnp.argsort(row_order).astype(jnp.int32)
        head_index = member_index % HEADS
        output, logsum = span_attend(head_queries[head_index][row_order], head_values[head_index][row_order])
        return (output[inverse], logsum[inverse])
    outputs, logsums = lax.map(jax.checkpoint(single), jnp.arange(ROUNDS * HEADS, dtype=jnp.int32))
    outputs = low_back(outputs).reshape(ROUNDS, HEADS, -1, DH)
    logsums = logsums.reshape(ROUNDS, HEADS, -1)
    combined = combine(outputs, logsums)
    return low(combined.transpose(1, 0, 2).reshape(-1, HEADS * DH))

def reversible_block(first_stream, second_stream, weights, buckets):
    query_weight, value_weight, mixing_weight, mixing_bias, expand_weight, expand_bias, shrink_weight, shrink_bias, attention_gain, attention_shift, forward_gain, forward_shift = weights
    normed = low(layer_norm(second_stream, attention_gain, attention_shift))
    combined = lsh_attention(normed, query_weight, value_weight, buckets)
    mixed_stream = first_stream + low_back(matmul(combined, mixing_weight) + mixing_bias)
    normed_two = low(layer_norm(mixed_stream, forward_gain, forward_shift))
    hidden = low_back(matmul(normed_two, expand_weight) + expand_bias)
    active = low(jax.nn.gelu(hidden, approximate=False))
    renewed = second_stream + low_back(matmul(active, shrink_weight) + shrink_bias)
    return (mixed_stream, renewed)

def reference(stream_one, stream_two, cotangent_one, cotangent_two, bucket_numbers, query_weight, value_weight, mixing_weight, mixing_bias, expand_weight, expand_bias, shrink_weight, shrink_bias, attention_gain, attention_shift, forward_gain, forward_shift):
    params = tuple((member.astype(jnp.float32) for member in (query_weight, value_weight, mixing_weight, mixing_bias, expand_weight, expand_bias, shrink_weight, shrink_bias, attention_gain, attention_shift, forward_gain, forward_shift)))

    def forward(first_stream, second_stream, weights):
        for number in range(LAYERS):
            first_stream, second_stream = reversible_block(first_stream, second_stream, tuple((member[number] for member in weights)), bucket_numbers[number])
        return (first_stream, second_stream)
    results, pullback = jax.vjp(forward, stream_one.astype(jnp.float32), stream_two.astype(jnp.float32), params)
    gradients = pullback((cotangent_one.astype(jnp.float32), cotangent_two.astype(jnp.float32)))
    param_grads = gradients[2]
    return (results[0], results[1], gradients[0], gradients[1], param_grads[0], param_grads[1], param_grads[2], param_grads[3], param_grads[4], param_grads[5], param_grads[6], param_grads[7], param_grads[8], param_grads[9], param_grads[10], param_grads[11])
```

```python
import functools
import math
from types import SimpleNamespace
from typing import NamedTuple

import jax
import jax.numpy as jnp
from jax import lax
from jax.experimental import pallas as pl
from jax.experimental.pallas import tpu as pltpu
from jax.sharding import PartitionSpec as P

DH = 128
SPAN = 64
ROUNDS = 4
LAYERS = 2
LANES = 128
CHUNK = 128
MESH = pl.DeviceIdType.MESH
F32 = jnp.float32
BF16 = jnp.bfloat16
AWAY = -1e30
VMEM_LIMIT = 60 << 20


class Sizes(NamedTuple):
    seq: int
    tok: int
    heads: int
    plane: int
    bits: int
    parts: int
    total: int
    rows: int
    ext: int
    buckets: int
    feats: int
    width: int
    hid: int


def sizes_of(seq, stream, query_weight, expand_weight):
    tok, feats = stream.shape
    width = query_weight.shape[2]
    heads = width // DH
    plane = seq // heads
    parts = plane // ROUNDS
    total = seq * tok
    rows = total // parts
    return Sizes(
        seq,
        tok,
        heads,
        plane,
        plane.bit_length() - 1,
        parts,
        total,
        rows,
        rows + CHUNK,
        total // SPAN,
        feats,
        width,
        expand_weight.shape[2],
    )


def dot(left, right):
    return lax.dot_general(left, right, (((1,), (0,)), ((), ())), preferred_element_type=F32)


def dot_nt(left, right):
    return lax.dot_general(left, right, (((1,), (1,)), ((), ())), preferred_element_type=F32)


def dot_tn(left, right):
    return lax.dot_general(left, right, (((0,), (0,)), ((), ())), preferred_element_type=F32)


def norm_parts(values):
    center = values - jnp.mean(values, axis=-1, keepdims=True)
    scale = lax.rsqrt(jnp.mean(center * center, axis=-1, keepdims=True) + 1e-05)
    return center * scale, scale


def norm_back(xhat, scale, gain, grad):
    t = grad * gain
    inner = t - jnp.mean(t, axis=-1, keepdims=True) - xhat * jnp.mean(t * xhat, axis=-1, keepdims=True)
    return scale * inner


def key_scale(keys):
    return lax.rsqrt(jnp.mean(keys * keys, axis=-1, keepdims=True) + 1e-06)


def rows_to_columns(rows):
    return jnp.transpose(jnp.broadcast_to(rows, (LANES, rows.shape[1])))


def split_three(values):
    high = values.astype(BF16).astype(F32)
    rest = values - high
    middle = rest.astype(BF16).astype(F32)
    return high, middle, rest - middle


class Place:
    def __init__(self, cfg):
        self.cfg = cfg
        self.index = lax.axis_index("seq")
        self.half = lax.axis_index("mp")
        self.head = self.index // cfg.plane
        self.member = self.index % cfg.plane
        self.round = self.member // cfg.parts
        self.part = self.member % cfg.parts

    def bit(self, k):
        return (self.member // 2**k) % 2

    def z_peer(self, step):
        head = (self.head + step) % self.cfg.heads
        return head, (head * self.cfg.plane + self.member, self.half)

    def z_source(self, step):
        return (self.head + self.cfg.heads - step) % self.cfg.heads

    def bit_peer(self, k):
        return (self.index + (1 - 2 * self.bit(k)) * 2**k, self.half)

    def y_peer(self):
        return (self.index, 1 - self.half)

    def kept(self, k, i):
        return 2 ** (k + 1) * i + self.member % 2 ** (k + 1)

    def given(self, k, i):
        return 2 ** (k + 1) * i + (1 - self.bit(k)) * 2**k + self.member % 2**k

    def group(self, k):
        return self.cfg.plane // 2 ** (k + 1)

    def greet(self):
        barrier = pltpu.get_barrier_semaphore()
        peers = [self.z_peer(step)[1] for step in range(1, self.cfg.heads)]
        peers += [self.bit_peer(k) for k in range(self.cfg.bits)]
        peers += [self.y_peer()]
        for peer in peers:
            pl.semaphore_signal(barrier, inc=1, device_id=peer, device_id_type=MESH)
        pl.semaphore_wait(barrier, len(peers))


def remote(src, dst, send, recv, peer):
    return pltpu.make_async_remote_copy(
        src_ref=src, dst_ref=dst, send_sem=send, recv_sem=recv, device_id=peer, device_id_type=MESH
    )


def rank_rows(cfg, bucket_row, rank_ref):
    count = cfg.buckets
    ids = lax.broadcasted_iota(jnp.int32, (count, LANES), 0)
    ahead = (
        lax.broadcasted_iota(jnp.int32, (LANES, LANES), 0)
        < lax.broadcasted_iota(jnp.int32, (LANES, LANES), 1)
    ).astype(BF16)
    lower = (
        lax.broadcasted_iota(jnp.int32, (count, count), 1)
        < lax.broadcasted_iota(jnp.int32, (count, count), 0)
    ).astype(BF16)
    marks = [
        (bucket_row[:, p * LANES : (p + 1) * LANES] == ids).astype(F32) for p in range(cfg.seq)
    ]
    totals = sum(marks)
    totals = jnp.broadcast_to(jnp.sum(totals, axis=1, keepdims=True), (count, LANES))
    carry = dot(lower, totals.astype(BF16))
    for p in range(cfg.seq):
        within = dot(marks[p].astype(BF16), ahead)
        rank = jnp.sum(marks[p] * (within + carry), axis=0, keepdims=True)
        carry = carry + jnp.broadcast_to(jnp.sum(marks[p], axis=1, keepdims=True), (count, LANES))
        spot = (p % cfg.plane) * cfg.heads + p // cfg.plane
        rank_ref[:, spot * LANES : (spot + 1) * LANES] = jnp.broadcast_to(
            rank.astype(jnp.int32), (8, LANES)
        )


def sort_rows(cfg, rank_ref, source_ref, store, start, size, chunks):
    step = min(cfg.total, 2048)

    def body(c, _):
        spots = start + c * size + lax.broadcasted_iota(jnp.int32, (size, step), 0)
        spots = spots % cfg.total if cfg.parts > 1 else spots
        found = None
        for k in range(cfg.total // step):
            ranks = rank_ref[0:1, k * step : (k + 1) * step]
            pick = (spots == ranks).astype(BF16)
            part = dot(pick, source_ref[k * step : (k + 1) * step, :])
            found = part if found is None else found + part
        store(c, found)
        return 0

    lax.fori_loop(0, chunks, body, 0)


def window_mask():
    row = lax.broadcasted_iota(jnp.int32, (CHUNK, 2 * CHUNK), 0)
    column = lax.broadcasted_iota(jnp.int32, (CHUNK, 2 * CHUNK), 1)
    gap = column // SPAN - row // SPAN
    near = jnp.logical_or(gap == 1, gap == 2)
    return jnp.logical_and(near, column != row + CHUNK)


def z_exchange(cfg, place, source, target, send, recv):
    copies = []
    for step in range(1, cfg.heads):
        head, peer = place.z_peer(step)
        copy = remote(source(head), target(place.head), send.at[step], recv.at[step], peer)
        copy.start()
        copies.append(copy)
    return copies


def z_arrival(place, block, recv, step):
    return remote(block, block, recv.at[step], recv.at[step], place.z_peer(step)[1])


class Doubling:
    def __init__(self, place, keys, block, send, recv):
        self.place, self.keys, self.block = place, keys, block
        self.send, self.recv = send, recv

    def give(self, key, spot, k):
        return remote(
            self.block(key, spot),
            self.block(key, spot),
            self.send.at[k, key, spot],
            self.recv.at[key, spot],
            self.place.bit_peer(k),
        )

    def offer(self, key):
        for k in range(self.place.cfg.bits):
            self.give(key, self.place.member, k).start()

    def spots(self):
        for k in reversed(range(self.place.cfg.bits)):
            for key in self.keys:
                for i in range(self.place.group(k)):
                    yield k, key, self.place.given(k, i)

    def receive(self):
        for k, key, spot in self.spots():
            self.give(key, spot, k).wait_recv()
            for low in range(k):
                self.give(key, spot, low).start()

    def finish(self):
        for key in self.keys:
            for k in range(self.place.cfg.bits):
                self.give(key, self.place.member, k).wait_send()
        for k, key, spot in self.spots():
            for low in range(k):
                self.give(key, spot, low).wait_send()


class Params(NamedTuple):
    wq_hbm: jax.Array
    wv_hbm: jax.Array
    wm_hbm: jax.Array
    mix_bias: jax.Array
    we_hbm: jax.Array
    expand_bias: jax.Array
    ws_hbm: jax.Array
    shrink_bias: jax.Array
    attention_gain: jax.Array
    attention_shift: jax.Array
    forward_gain: jax.Array
    forward_shift: jax.Array


class Streams(NamedTuple):
    first: jax.Array
    second: jax.Array
    buckets: jax.Array


class Kept(NamedTuple):
    mixed: jax.Array
    sorted: jax.Array
    comb: jax.Array
    joint: jax.Array
    hidden: jax.Array
    rank: jax.Array
    normed_t: jax.Array
    normed_two_t: jax.Array
    active_t: jax.Array
    low_t: jax.Array
    second: jax.Array


class Grads(NamedTuple):
    first_out: jax.Array
    second_out: jax.Array
    out_wq: jax.Array
    out_wv: jax.Array
    out_wm: jax.Array
    out_we: jax.Array
    out_ws: jax.Array
    out_small: jax.Array


def gathered(*groups, **scratch):
    merged = {}
    for group in groups:
        merged.update(group._asdict())
    return SimpleNamespace(**merged, **scratch)


def forward_scratch(cfg):
    tok, heads, plane, bits = cfg.tok, cfg.heads, cfg.plane, cfg.bits
    band = heads * tok
    dma = pltpu.SemaphoreType.DMA
    return dict(
        wq=pltpu.VMEM((cfg.feats, cfg.width), BF16),
        wv=pltpu.VMEM((cfg.feats, cfg.width), BF16),
        wm=pltpu.VMEM((cfg.width, cfg.feats), BF16),
        we=pltpu.VMEM((cfg.feats, cfg.hid), BF16),
        ws=pltpu.VMEM((cfg.hid, cfg.feats), BF16),
        zs=pltpu.VMEM((heads, tok, 2 * DH), BF16),
        tokens=pltpu.VMEM((cfg.total, 2 * DH), BF16),
        keys=pltpu.VMEM((cfg.ext, DH), BF16),
        attended=pltpu.VMEM((cfg.rows, 3 * DH), BF16),
        part=pltpu.VMEM((plane, band, DH), F32),
        lrow=pltpu.VMEM((plane, 8, band), F32),
        part_in=pltpu.VMEM((bits, plane, band, DH), F32),
        lrow_in=pltpu.VMEM((bits, plane, 8, band), F32),
        low_out=pltpu.VMEM((heads, tok, DH), BF16),
        low_in=pltpu.VMEM((heads, tok, DH), BF16),
        ys=pltpu.VMEM((2, tok, cfg.feats), BF16),
        yr=pltpu.VMEM((2, tok, cfg.feats), BF16),
        wsem=dma((5,)),
        zsend=dma((heads,)),
        zrecv=dma((heads,)),
        gsend=dma((bits, heads, plane)),
        grecv=dma((heads, plane)),
        psend=dma((bits, plane, 2)),
        precv=dma((bits, plane, 2)),
        csend=dma((heads,)),
        crecv=dma((heads,)),
        ysend=dma((2,)),
        yrecv=dma((2,)),
    )


def y_sum(place, r, slot, partial, meanwhile=None):
    r.ys[slot] = partial.astype(BF16)
    copy = remote(r.ys.at[slot], r.yr.at[slot], r.ysend.at[slot], r.yrecv.at[slot], place.y_peer())
    copy.start()
    if meanwhile is not None:
        meanwhile()
    copy.wait()
    return r.ys[slot].astype(F32) + r.yr[slot].astype(F32)


def forward_kernel(cfg, layer, names, *refs):
    inputs, refs = refs[:IN_COUNT], refs[IN_COUNT:]
    streams, params = Streams(*inputs[:3]), Params(*inputs[3:])
    out, scratch = Kept(*refs[: len(Kept._fields)]), refs[len(Kept._fields) :]
    r = gathered(out, streams, params, **dict(zip(names, scratch, strict=True)))
    r.second, r.renewed = streams.second, out.second
    place = Place(cfg)
    tok, heads = cfg.tok, cfg.heads
    band = heads * tok
    one = slice(layer, layer + 1)
    loads = [
        pltpu.make_async_copy(src.at[layer], dst, r.wsem.at[i])
        for i, (src, dst) in enumerate(
            (
                (r.wq_hbm, r.wq),
                (r.wv_hbm, r.wv),
                (r.wm_hbm, r.wm),
                (r.we_hbm, r.we),
                (r.ws_hbm, r.ws),
            )
        )
    ]
    for load in loads:
        load.start()
    normed = norm_parts(r.second[...])[0] * r.attention_gain[one, :] + r.attention_shift[one, :]
    normed = normed.astype(BF16)
    loads[0].wait()
    loads[1].wait()
    queries = dot(normed, r.wq[...]).astype(BF16)
    values = dot(normed, r.wv[...]).astype(BF16)
    for head in range(heads):
        r.zs[head, :, :DH] = queries[:, head * DH : (head + 1) * DH]
        r.zs[head, :, DH:] = values[:, head * DH : (head + 1) * DH]

    def block(head, spot):
        return r.tokens.at[pl.ds(pl.multiple_of((spot * heads + head) * tok, tok), tok), :]

    place.greet()
    sent = z_exchange(
        cfg,
        place,
        lambda head: r.zs.at[head],
        lambda head: block(head, place.member),
        r.zsend,
        r.zrecv,
    )
    block(place.head, place.member)[...] = r.zs[place.head]
    rank_rows(cfg, r.buckets[layer, place.round, pl.ds(place.head, 1), :], r.rank)

    spread = Doubling(
        place, [place.z_source(step) for step in range(heads)], block, r.gsend, r.grecv
    )
    for step in range(heads):
        if step > 0:
            z_arrival(place, block(place.z_source(step), place.member), r.zrecv, step).wait_recv()
        spread.offer(place.z_source(step))
    spread.receive()
    base = place.part * cfg.rows

    def store_rows(c, found):
        r.sorted[pl.ds(pl.multiple_of(CHUNK + c * 512, CHUNK), 512), :] = found.astype(BF16)

    def store_halo(c, found):
        r.sorted[0:CHUNK, :] = found.astype(BF16)

    sort_rows(cfg, r.rank, r.tokens, store_rows, base, 512, cfg.rows // 512)
    if cfg.parts == 1:
        r.sorted[0:CHUNK, :] = r.sorted[cfg.rows : cfg.ext, :]
    else:
        sort_rows(cfg, r.rank, r.tokens, store_halo, base + cfg.total - CHUNK, CHUNK, 1)
    raw = r.sorted[:, :DH].astype(F32)
    r.keys[...] = (raw * key_scale(raw)).astype(BF16)
    mask = window_mask()
    lane = lax.broadcasted_iota(jnp.int32, (CHUNK, LANES), 1)

    def attend(c, _):
        at = pl.multiple_of(c * CHUNK, CHUNK)
        query = r.sorted[pl.ds(at + CHUNK, CHUNK), :DH]
        scores = dot_nt(query, r.keys[pl.ds(at, 2 * CHUNK), :]) / math.sqrt(DH)
        scores = jnp.where(mask, scores, -1000000000.0)
        peak = jnp.max(scores, axis=-1, keepdims=True)
        powers = jnp.exp(scores - peak)
        summed = jnp.sum(powers, axis=-1, keepdims=True)
        weights = (powers / summed).astype(BF16)
        output = dot(weights, r.sorted[pl.ds(at, 2 * CHUNK), DH:])
        high, middle, low = split_three(peak + jnp.log(summed))
        extra = jnp.where(lane == 0, high, 0.0)
        extra = jnp.where(lane == 1, middle, extra)
        extra = jnp.where(lane == 2, low, extra)
        extra = jnp.where(lane == 3, 1.0, extra)
        r.attended[pl.ds(at, CHUNK), :DH] = output.astype(BF16)
        r.attended[pl.ds(at, CHUNK), DH:2 * DH] = extra.astype(BF16)
        r.attended[pl.ds(at, CHUNK), 2 * DH :] = (output - output.astype(BF16).astype(F32)).astype(BF16)
        return 0

    lax.fori_loop(0, cfg.rows // CHUNK, attend, 0)

    def unsort(spot):
        found = dot(unsort_pick(cfg, r.rank, spot, base, cfg.rows), r.attended[...])
        r.part[spot] = found[:, :DH] + found[:, 2 * DH :]
        extra = jnp.transpose(found[:, DH:2 * DH])
        row = extra[0:1] + extra[1:2] + extra[2:3] + (1.0 - extra[3:4]) * AWAY
        r.lrow[spot] = jnp.broadcast_to(row, (8, band))

    def pass_part(k, spot):
        peer = place.bit_peer(k)
        return [
            remote(mine.at[spot], theirs.at[k, spot], r.psend.at[k, spot, i], r.precv.at[k, spot, i], peer)
            for i, (mine, theirs) in enumerate(((r.part, r.part_in), (r.lrow, r.lrow_in)))
        ]

    def first_half(i, _):
        unsort(place.given(0, i))
        for copy in pass_part(0, place.given(0, i)):
            copy.start()
        return 0

    def second_half(i, _):
        unsort(place.kept(0, i))
        return 0

    lax.fori_loop(0, place.group(0), first_half, 0)
    lax.fori_loop(0, place.group(0), second_half, 0)

    def merge(k, spot):
        for copy in pass_part(k, spot):
            copy.wait_recv()
        mine = rows_to_columns(r.lrow[spot][0:1])
        other = rows_to_columns(r.lrow_in[k, spot][0:1])
        highest = jnp.maximum(mine, other)
        share = jnp.exp(mine - highest)
        share_in = jnp.exp(other - highest)
        both = share + share_in
        merged = (r.part[spot].astype(F32) * share + r.part_in[k, spot].astype(F32) * share_in) / both
        return merged, jnp.transpose(highest + jnp.log(both))[0:8]

    for k in range(cfg.bits - 1):
        for giving in (True, False):
            for i in range(place.group(k + 1)):
                spot = place.given(k + 1, i) if giving else place.kept(k + 1, i)
                merged, joint = merge(k, spot)
                r.part[spot] = merged
                r.lrow[spot] = joint
                if giving:
                    for copy in pass_part(k + 1, spot):
                        copy.start()
    merged, joint = merge(cfg.bits - 1, place.member)
    r.comb[...] = merged
    r.joint[...] = joint
    for head in range(heads):
        r.low_out[head] = merged[head * tok : (head + 1) * tok].astype(BF16)
    back = z_exchange(
        cfg, place, lambda head: r.low_out.at[head], lambda head: r.low_in.at[head], r.csend, r.crecv
    )
    r.low_in[place.head] = r.low_out[place.head]
    loads[2].wait()
    for step in range(1, heads):
        z_arrival(place, r.low_in.at[place.z_source(step)], r.crecv, step).wait_recv()
    low = jnp.concatenate([r.low_in[head] for head in range(heads)], axis=1)

    def finish_sends():
        spread.finish()
        for copy in sent + back:
            copy.wait_send()
        for k in range(cfg.bits):
            for i in range(place.group(k)):
                for copy in pass_part(k, place.given(k, i)):
                    copy.wait_send()
        r.normed_t[...] = jnp.transpose(normed)
        r.low_t[...] = jnp.transpose(low)

    mixed = (
        r.first[...]
        + y_sum(place, r, 0, dot(low, r.wm[...]), finish_sends)
        + r.mix_bias[one, :]
    )
    r.mixed[...] = mixed
    normed_two = norm_parts(mixed)[0] * r.forward_gain[one, :] + r.forward_shift[one, :]
    normed_two = normed_two.astype(BF16)
    loads[3].wait()
    hidden = dot(normed_two, r.we[...]) + r.expand_bias[one, :]
    r.hidden[...] = hidden
    active = (hidden * (1.0 + lax.erf(hidden * math.sqrt(0.5))) * 0.5).astype(BF16)
    loads[4].wait()

    def turn():
        r.normed_two_t[...] = jnp.transpose(normed_two)
        r.active_t[...] = jnp.transpose(active)

    r.renewed[...] = (
        r.second[...] + y_sum(place, r, 1, dot(active, r.ws[...]), turn) + r.shrink_bias[one, :]
    )


def unsort_pick(cfg, rank_ref, spot, base, rows):
    band = cfg.heads * cfg.tok
    ranks = rank_ref[0:1, pl.ds(pl.multiple_of(spot * band, band), band)]
    ranks = rows_to_columns(ranks.astype(F32)).astype(jnp.int32)[:, 0:1]
    places = base + lax.broadcasted_iota(jnp.int32, (band, rows), 1)
    if cfg.parts > 1:
        places = places % cfg.total
    return (ranks == places).astype(BF16)


IN_COUNT = len(Streams._fields) + len(Params._fields)


def forward_call(cfg, layer, streams, params):
    scratch = forward_scratch(cfg)
    whole = pl.BlockSpec(memory_space=pltpu.VMEM)
    apart = pl.BlockSpec(memory_space=pl.ANY)
    specs = Params(*[whole] * len(params))._replace(
        wq_hbm=apart, wv_hbm=apart, wm_hbm=apart, we_hbm=apart, ws_hbm=apart
    )
    outs = pl.pallas_call(
        functools.partial(forward_kernel, cfg, layer, list(scratch)),
        out_shape=[jax.ShapeDtypeStruct(*shape) for shape in saved_shapes(cfg)],
        in_specs=[whole] * len(streams) + list(specs),
        out_specs=[whole] * len(Kept._fields),
        scratch_shapes=list(scratch.values()),
        compiler_params=pltpu.CompilerParams(
            collective_id=layer, has_side_effects=True, vmem_limit_bytes=VMEM_LIMIT
        ),
        name=f"forward_{layer}",
    )(*streams, *params)
    return Kept(*outs)


RING = 4


def saved_shapes(cfg):
    tok, feats, band = cfg.tok, cfg.feats, cfg.heads * cfg.tok
    return Kept(
        second=((tok, feats), F32),
        mixed=((tok, feats), F32),
        sorted=((cfg.ext, 2 * DH), BF16),
        comb=((band, DH), F32),
        joint=((8, band), F32),
        hidden=((tok, cfg.hid), F32),
        rank=((8, cfg.total), jnp.int32),
        normed_t=((feats, tok), BF16),
        normed_two_t=((feats, tok), BF16),
        active_t=((cfg.hid, tok), BF16),
        low_t=((cfg.width, tok), BF16),
    )


def backward_scratch(cfg):
    tok, heads, plane, bits = cfg.tok, cfg.heads, cfg.plane, cfg.bits
    band = heads * tok
    dma = pltpu.SemaphoreType.DMA
    share = cfg.feats // cfg.seq
    return dict(
        wq=pltpu.VMEM((cfg.feats, cfg.width), BF16),
        wv=pltpu.VMEM((cfg.feats, cfg.width), BF16),
        wm=pltpu.VMEM((cfg.width, cfg.feats), BF16),
        we=pltpu.VMEM((cfg.feats, cfg.hid), BF16),
        ws=pltpu.VMEM((cfg.hid, cfg.feats), BF16),
        gs=pltpu.VMEM((heads, tok, DH), BF16),
        gtokens=pltpu.VMEM((cfg.total, 2 * DH), BF16),
        arow=pltpu.VMEM((LAYERS, plane, 8, band), F32),
        gsorted=pltpu.VMEM((cfg.rows, DH), BF16),
        stats=pltpu.VMEM((cfg.rows, LANES), F32),
        keys=pltpu.VMEM((cfg.ext, DH), BF16),
        dq=pltpu.VMEM((cfg.ext, DH), F32),
        dk=pltpu.VMEM((cfg.ext, DH), F32),
        dv=pltpu.VMEM((cfg.ext, DH), F32),
        grads=pltpu.VMEM((cfg.ext, 2 * DH), BF16),
        part=pltpu.VMEM((plane, band, 2 * DH), BF16),
        part_in=pltpu.VMEM((plane, band, 2 * DH), BF16),
        home_out=pltpu.VMEM((heads, tok, 2 * DH), BF16),
        home_in=pltpu.VMEM((heads, tok, 2 * DH), BF16),
        ys=pltpu.VMEM((2, tok, cfg.feats), BF16),
        yr=pltpu.VMEM((2, tok, cfg.feats), BF16),
        vectors=pltpu.VMEM((8, cfg.feats), F32),
        ubuf=pltpu.VMEM((RING, plane, heads, share, 512), BF16),
        uin=pltpu.VMEM((RING, plane, heads, share, 512), BF16),
        uz=pltpu.VMEM((RING, heads, share, 512), BF16),
        vbuf=pltpu.VMEM((LAYERS, plane, heads, 8, LANES), F32),
        vin=pltpu.VMEM((LAYERS, plane, heads, 8, LANES), F32),
        vz=pltpu.VMEM((LAYERS, heads, 8, LANES), F32),
        wsem=dma((5,)),
        lsem=dma((LAYERS, len(Kept._fields))),
        zsend=dma((LAYERS, heads)),
        zrecv=dma((LAYERS, heads)),
        gsend=dma((LAYERS, bits, heads, plane)),
        grecv=dma((LAYERS, heads, plane)),
        asend=dma((LAYERS, bits, 1, plane)),
        arecv=dma((LAYERS, 1, plane)),
        psend=dma((LAYERS, bits, plane)),
        precv=dma((LAYERS, bits, plane)),
        csend=dma((LAYERS, heads)),
        crecv=dma((LAYERS, heads)),
        ysend=dma((2,)),
        yrecv=dma((2,)),
        usend=dma((RING, bits + heads)),
        urecv=dma((RING, bits + heads)),
        vsend=dma((LAYERS, bits + heads)),
        vrecv=dma((LAYERS, bits + heads)),
    )


class Unit:
    def __init__(self, place, fill, done, buf, arrive, zbuf, send, recv):
        self.place, self.fill, self.done = place, fill, done
        self.buf, self.arrive, self.zbuf, self.send, self.recv = buf, arrive, zbuf, send, recv
        self.stage = 0

    def halved(self, k):
        place, plane = self.place, self.place.cfg.plane
        group = place.group(k)
        start = plane - plane // 2**k
        shape = (group, 2 ** (k + 1)) + self.buf.shape[1:]
        spot = (1 - place.bit(k)) * 2**k + place.member % 2**k
        return remote(
            self.buf.reshape(*shape).at[:, spot],
            self.arrive.at[start : start + group],
            self.send.at[k],
            self.recv.at[k],
            place.bit_peer(k),
        )

    def across(self, step):
        place = self.place
        head, peer = place.z_peer(step)
        at = place.cfg.bits + step
        return remote(
            self.buf.at[place.member, head], self.zbuf.at[step], self.send.at[at], self.recv.at[at], peer
        )

    def advance(self):
        place, cfg = self.place, self.place.cfg
        k = self.stage - 1
        if self.stage == 0:
            self.fill(self.buf)
        elif k < cfg.bits:
            self.halved(k).wait_recv()
            start = cfg.plane - cfg.plane // 2**k
            for i in range(place.group(k)):
                spot = place.kept(k, i)
                both = self.buf[spot].astype(F32) + self.arrive[start + i].astype(F32)
                self.buf[spot] = both.astype(self.buf.dtype)
        else:
            total = self.buf[place.member, place.head].astype(F32)
            for step in range(1, cfg.heads):
                self.across(step).wait_recv()
                total = total + self.zbuf[step].astype(F32)
            self.done(total)
            for k in range(cfg.bits):
                self.halved(k).wait_send()
            for step in range(1, cfg.heads):
                self.across(step).wait_send()
        self.stage += 1
        if self.stage <= cfg.bits:
            self.halved(self.stage - 1).start()
        elif self.stage == cfg.bits + 1:
            for step in range(1, cfg.heads):
                self.across(step).start()
        return self.stage <= cfg.bits + 1


class Pump:
    def __init__(self):
        self.waiting, self.flying = [], []

    def tick(self, times=1):
        for _ in range(times):
            self.flying = [unit for unit in self.flying if unit.advance()]
            if self.waiting:
                unit = self.waiting.pop(0)()
                unit.advance()
                self.flying.append(unit)

    def drain(self):
        while self.waiting or self.flying:
            self.tick()


def backward_kernel(cfg, names, *refs):
    params, refs = Params(*refs[: len(Params._fields)]), refs[len(Params._fields) :]
    (first_cot, second_cot), refs = refs[:2], refs[2:]
    held = []
    for _ in range(2 * LAYERS):
        held.append(Kept(*refs[: len(Kept._fields)]))
        refs = refs[len(Kept._fields) :]
        if len(held) == LAYERS:
            out, refs = Grads(*refs[: len(Grads._fields)]), refs[len(Grads._fields) :]
    stored, held = held[:LAYERS], held[LAYERS:]
    r = gathered(params, out, **dict(zip(names, refs, strict=True)))
    place = Place(cfg)
    tok, heads, plane, width = cfg.tok, cfg.heads, cfg.plane, cfg.width
    band = heads * tok
    share = cfg.feats // cfg.seq
    base = place.part * cfg.rows
    pump = Pump()
    count = [0]

    def weight_load(i, layer):
        source = (r.ws_hbm, r.we_hbm, r.wm_hbm, r.wq_hbm, r.wv_hbm)[i]
        target = (r.ws, r.we, r.wm, r.wq, r.wv)[i]
        return pltpu.make_async_copy(source.at[layer], target, r.wsem.at[i])

    def saved_load(layer, ref):
        i = [ref is other for other in held[layer]].index(True)
        return pltpu.make_async_copy(stored[layer][i], ref, r.lsem.at[layer, i])

    def queue(fill, done):
        def make():
            slot = count[0] % RING
            count[0] += 1
            return Unit(
                place, fill, done, r.ubuf.at[slot], r.uin.at[slot], r.uz.at[slot], r.usend.at[slot], r.urecv.at[slot]
            )

        pump.waiting.append(make)

    def product(lines, right):
        def fill(buf):
            for head in range(heads):
                found = dot(lines(head), right)
                buf[:, head] = found.reshape(plane, share, 512).astype(BF16)

        return fill

    def queue_expand(layer, hidden_grad):
        lhs = held[layer].normed_two_t
        for j in range(cfg.hid // 512):

            def done(total, j=j):
                r.out_we[layer, :, j * 512 : (j + 1) * 512] = total

            queue(
                product(
                    lambda head: lhs[head * plane * share : (head + 1) * plane * share, :],
                    hidden_grad[:, j * 512 : (j + 1) * 512],
                ),
                done,
            )

    def queue_shrink(layer, branch):
        lhs = held[layer].active_t
        deep = cfg.hid // cfg.seq
        for h in range(deep // share):
            for j in range(cfg.feats // 512):

                def lines(head, h=h):
                    rows = lhs[head * plane * deep : (head + 1) * plane * deep, :]
                    rows = rows.reshape(plane, deep, tok)[:, h * share : (h + 1) * share]
                    return rows.reshape(plane * share, tok)

                def done(total, h=h, j=j):
                    r.out_ws[layer, h * share : (h + 1) * share, j * 512 : (j + 1) * 512] = total

                queue(product(lines, branch[:, j * 512 : (j + 1) * 512]), done)

    def queue_mixing(layer, mix_low):
        lhs = held[layer].low_t
        deep = width // cfg.seq
        folds = share // deep

        def fill(buf):
            for head in range(heads):
                rows = lhs[head * plane * deep : (head + 1) * plane * deep, :]
                pieces = [
                    dot(rows, mix_low[:, j * 512 : (j + 1) * 512]).reshape(plane, deep, 512)
                    for j in range(folds)
                ]
                buf[:, head] = jnp.concatenate(pieces, axis=1).astype(BF16)

        def done(total):
            for j in range(folds):
                r.out_wm[layer, :, j * 512 : (j + 1) * 512] = total[j * deep : (j + 1) * deep]

        queue(fill, done)

    def queue_attention(layer, grad, out):
        lhs = held[layer].normed_t

        def done(total):
            out[layer] = total

        queue(product(lambda head: lhs[head * plane * share : (head + 1) * plane * share, :], grad), done)

    def queue_vectors(layer):
        def fill(buf):
            deep = cfg.hid // cfg.seq
            for p in range(cfg.seq):
                at = p * share // LANES * LANES
                tile = r.vectors[:, at : at + LANES]
                at = p * deep // LANES * LANES
                line, at = 6 + at // cfg.feats, at % cfg.feats
                extra = r.vectors[line : line + 1, at : at + LANES]
                buf[p % plane, p // plane, 0:6] = tile[0:6]
                buf[p % plane, p // plane, 6:8] = jnp.broadcast_to(extra, (2, LANES))

        def done(total):
            r.out_small[layer] = total

        def make():
            return Unit(
                place, fill, done, r.vbuf.at[layer], r.vin.at[layer], r.vz.at[layer], r.vsend.at[layer], r.vrecv.at[layer]
            )

        pump.waiting.append(make)

    order = list(reversed(range(LAYERS)))
    for i in range(5):
        weight_load(i, order[0]).start()
    for layer in order:
        k = held[layer]
        for ref in (k.active_t, k.hidden, k.mixed, k.normed_two_t, k.comb, k.joint, k.sorted):
            saved_load(layer, ref).start()
        for ref in (k.rank, k.low_t, k.second, k.normed_t):
            saved_load(layer, ref).start()
    place.greet()

    for layer in order:
        one = slice(layer, layer + 1)
        after = layer - 1

        saved = held[layer]

        def arrived(*fields):
            for field in fields:
                saved_load(layer, field).wait()

        def next_weight(*numbers):
            if after >= 0:
                for i in numbers:
                    weight_load(i, after).start()

        second_grad = second_cot if layer == order[0] else r.second_out
        first_grad = first_cot if layer == order[0] else r.first_out
        branch = second_grad[...].astype(BF16)
        arrived(saved.active_t, saved.hidden)
        queue_shrink(layer, branch)
        pump.tick()
        r.vectors[0:1, :] = jnp.sum(branch.astype(F32), axis=0, keepdims=True)
        hidden = saved.hidden[...]
        slope = 0.5 * (1.0 + lax.erf(hidden * math.sqrt(0.5)))
        slope = slope + hidden * jnp.exp(-0.5 * hidden * hidden) * (1.0 / math.sqrt(2.0 * math.pi))
        weight_load(0, layer).wait()
        hidden_grad = (dot_nt(branch, r.ws[...]) * slope).astype(BF16)
        next_weight(0)
        weight_load(1, layer).wait()
        partial = dot_nt(hidden_grad, r.we[...])
        next_weight(1)
        arrived(saved.mixed, saved.normed_two_t)

        def during_two():
            summed = jnp.sum(hidden_grad.astype(F32), axis=0, keepdims=True)
            for i in range(cfg.hid // cfg.feats):
                r.vectors[6 + i : 7 + i, :] = summed[:, i * cfg.feats : (i + 1) * cfg.feats]
            queue_expand(layer, hidden_grad)
            pump.tick(2)

        two_grad = y_sum(place, r, 0, partial, during_two)
        xhat, scale = norm_parts(saved.mixed[...])
        mixed_grad = first_grad[...] + norm_back(xhat, scale, r.forward_gain[one, :], two_grad)
        r.first_out[...] = mixed_grad
        mix_low = mixed_grad.astype(BF16)
        weight_load(2, layer).wait()
        combined_grad = dot_nt(mix_low, r.wm[...]).astype(BF16)
        next_weight(2)
        for head in range(heads):
            r.gs[head] = combined_grad[:, head * DH : (head + 1) * DH]

        def rows_of(spot, head):
            return pl.ds(pl.multiple_of((spot * heads + head) * tok, tok), tok)

        def block(head, spot):
            return r.gtokens.at[rows_of(spot, head), :DH]

        sent = z_exchange(
            cfg,
            place,
            lambda head: r.gs.at[head],
            lambda head: block(head, place.member),
            r.zsend.at[layer],
            r.zrecv.at[layer],
        )
        block(place.head, place.member)[...] = r.gs[place.head]
        r.vectors[1:2, :] = jnp.sum(mix_low.astype(F32), axis=0, keepdims=True)
        r.vectors[2:3, :] = jnp.sum(two_grad * xhat, axis=0, keepdims=True)
        r.vectors[3:4, :] = jnp.sum(two_grad, axis=0, keepdims=True)
        arrived(saved.sorted, saved.rank, saved.comb, saved.joint, saved.low_t)
        rank = saved.rank
        rows = saved.sorted
        queue_mixing(layer, mix_low)
        raw = rows[:, :DH].astype(F32)
        r.keys[...] = (raw * key_scale(raw)).astype(BF16)
        pump.tick()
        spread = Doubling(
            place,
            [place.z_source(step) for step in range(heads)],
            block,
            r.gsend.at[layer],
            r.grecv.at[layer],
        )
        for step in range(heads):
            if step > 0:
                spot = block(place.z_source(step), place.member)
                z_arrival(place, spot, r.zrecv.at[layer], step).wait_recv()
            spread.offer(place.z_source(step))
        mine = r.gtokens[pl.ds(pl.multiple_of(place.member * band, band), band), :DH].astype(F32)
        inner = jnp.sum(jnp.transpose(mine * saved.comb[...]), axis=0, keepdims=True)
        line = lax.broadcasted_iota(jnp.int32, (8, band), 0)
        r.arow[layer, place.member] = jnp.where(
            line == 0, saved.joint[...], jnp.broadcast_to(inner, (8, band))
        )
        extras = Doubling(
            place,
            [0],
            lambda key, spot: r.arow.at[layer, spot],
            r.asend.at[layer],
            r.arecv.at[layer],
        )
        extras.offer(0)
        spread.receive()
        extras.receive()
        pump.tick()
        lines = lax.broadcasted_iota(jnp.int32, (LANES, band), 0)
        for spot in range(plane):
            pieces = split_three(r.arow[layer, spot][0:1]) + split_three(r.arow[layer, spot][1:2])
            table = jnp.zeros((LANES, band), F32)
            for i, piece in enumerate(pieces):
                table = jnp.where(lines == i, piece, table)
            r.gtokens[spot * band : (spot + 1) * band, DH:] = jnp.transpose(table).astype(BF16)

        def store_rows(c, found):
            at = pl.ds(pl.multiple_of(c * 512, 512), 512)
            r.gsorted[at, :] = found[:, :DH].astype(BF16)
            r.stats[at, :] = found[:, DH:]

        sort_rows(cfg, rank, r.gtokens, store_rows, base, 512, cfg.rows // 512)
        pump.tick()
        r.dk[...] = jnp.zeros((cfg.ext, DH), F32)
        r.dv[...] = jnp.zeros((cfg.ext, DH), F32)
        r.dq[0:CHUNK, :] = jnp.zeros((CHUNK, DH), F32)
        mask = window_mask()

        def attend(c, _):
            at = pl.multiple_of(c * CHUNK, CHUNK)
            own = pl.ds(at + CHUNK, CHUNK)
            window = pl.ds(at, 2 * CHUNK)
            query = rows[own, :DH]
            near = r.keys[window, :]
            grad = r.gsorted[pl.ds(at, CHUNK), :]
            stats = r.stats[pl.ds(at, CHUNK), :]
            joint = stats[:, 0:1] + stats[:, 1:2] + stats[:, 2:3]
            inner = stats[:, 3:4] + stats[:, 4:5] + stats[:, 5:6]
            scores = dot_nt(query, near) / math.sqrt(DH)
            scores = jnp.where(mask, scores, -1000000000.0)
            probs = jnp.exp(scores - joint)
            prob_grad = dot_nt(grad, rows[window, DH:])
            score_grad = (probs * (prob_grad - inner) / math.sqrt(DH)).astype(BF16)
            r.dq[own, :] = dot(score_grad, near)
            r.dk[window, :] = r.dk[window, :] + dot_tn(score_grad, query)
            r.dv[window, :] = r.dv[window, :] + dot_tn(probs.astype(BF16), grad)
            return 0

        half = cfg.rows // CHUNK // 2
        lax.fori_loop(0, half, attend, 0)
        pump.tick()
        lax.fori_loop(half, cfg.rows // CHUNK, attend, 0)
        if cfg.parts == 1:
            last = slice(cfg.rows, cfg.ext)
            r.dk[last, :] = r.dk[last, :] + r.dk[0:CHUNK, :]
            r.dv[last, :] = r.dv[last, :] + r.dv[0:CHUNK, :]
        raw = rows[:, :DH].astype(F32)
        scale = key_scale(raw)
        dk = r.dk[...]
        inner = jnp.mean(raw * dk, axis=-1, keepdims=True)
        r.grads[:, :DH] = (
            r.dq[...] + scale * dk - raw * (scale * scale * scale * inner)
        ).astype(BF16)
        r.grads[:, DH:] = r.dv[...].astype(BF16)
        pump.tick()
        skip = CHUNK if cfg.parts == 1 else 0

        def unsort(spot):
            start = base if cfg.parts == 1 else base + cfg.total - CHUNK
            pick = unsort_pick(cfg, rank, spot, start, cfg.ext - skip)
            r.part[spot] = dot(pick, r.grads[skip:, :]).astype(BF16)

        def pass_part(k, spot):
            return remote(
                r.part.at[spot],
                r.part_in.at[plane - plane // 2**k + spot // 2 ** (k + 1)],
                r.psend.at[layer, k, spot],
                r.precv.at[layer, k, spot // 2 ** (k + 1)],
                place.bit_peer(k),
            )

        def first_half(i, _):
            unsort(place.given(0, i))
            pass_part(0, place.given(0, i)).start()
            return 0

        def second_half(i, _):
            unsort(place.kept(0, i))
            return 0

        lax.fori_loop(0, place.group(0), first_half, 0)
        lax.fori_loop(0, place.group(0), second_half, 0)

        def merge(k, spot):
            pass_part(k, spot).wait_recv()
            other = r.part_in[plane - plane // 2**k + spot // 2 ** (k + 1)]
            return (r.part[spot].astype(F32) + other.astype(F32)).astype(BF16)

        for k in range(cfg.bits - 1):
            for giving in (True, False):
                for i in range(place.group(k + 1)):
                    spot = place.given(k + 1, i) if giving else place.kept(k + 1, i)
                    r.part[spot] = merge(k, spot)
                    if giving:
                        pass_part(k + 1, spot).start()
        pump.tick()
        merged = merge(cfg.bits - 1, place.member)
        for head in range(heads):
            r.home_out[head] = merged[head * tok : (head + 1) * tok]
        back = z_exchange(
            cfg,
            place,
            lambda head: r.home_out.at[head],
            lambda head: r.home_in.at[head],
            r.csend.at[layer],
            r.crecv.at[layer],
        )
        r.home_in[place.head] = r.home_out[place.head]
        arrived(saved.second, saved.normed_t)
        weight_load(3, layer).wait()
        weight_load(4, layer).wait()
        pump.tick()
        for step in range(1, heads):
            spot = r.home_in.at[place.z_source(step)]
            z_arrival(place, spot, r.crecv.at[layer], step).wait_recv()
        query_grad = jnp.concatenate([r.home_in[head][:, :DH] for head in range(heads)], axis=1)
        value_grad = jnp.concatenate([r.home_in[head][:, DH:] for head in range(heads)], axis=1)
        one_grad = dot_nt(query_grad, r.wq[...]) + dot_nt(value_grad, r.wv[...])
        next_weight(3, 4)

        def during_one():
            queue_attention(layer, query_grad, r.out_wq)
            queue_attention(layer, value_grad, r.out_wv)
            spread.finish()
            extras.finish()
            for copy in sent + back:
                copy.wait_send()
            for k in range(cfg.bits):
                for i in range(place.group(k)):
                    pass_part(k, place.given(k, i)).wait_send()
            pump.tick(2)

        one_grad = y_sum(place, r, 1, one_grad, during_one)
        xhat, scale = norm_parts(saved.second[...])
        dx = norm_back(xhat, scale, r.attention_gain[one, :], one_grad)
        r.second_out[...] = second_grad[...] + dx
        r.vectors[4:5, :] = jnp.sum(one_grad * xhat, axis=0, keepdims=True)
        r.vectors[5:6, :] = jnp.sum(one_grad, axis=0, keepdims=True)
        queue_vectors(layer)
        pump.waiting.insert(0, pump.waiting.pop())
        pump.tick()
    pump.drain()


def backward_call(cfg, params, cotangents, saved):
    scratch = backward_scratch(cfg)
    tok, feats = cfg.tok, cfg.feats
    share = feats // cfg.seq
    shapes = Grads(
        first_out=(tok, feats),
        second_out=(tok, feats),
        out_wq=(LAYERS, share, cfg.width),
        out_wv=(LAYERS, share, cfg.width),
        out_wm=(LAYERS, cfg.width // cfg.seq, feats),
        out_we=(LAYERS, share, cfg.hid),
        out_ws=(LAYERS, cfg.hid // cfg.seq, feats),
        out_small=(LAYERS, 8, LANES),
    )
    whole = pl.BlockSpec(memory_space=pltpu.VMEM)
    apart = pl.BlockSpec(memory_space=pl.ANY)
    specs = Params(*[apart] * len(params))._replace(attention_gain=whole, forward_gain=whole)
    held = [pltpu.VMEM(*shape) for shape in saved_shapes(cfg)] * LAYERS
    outs = pl.pallas_call(
        functools.partial(backward_kernel, cfg, list(scratch)),
        out_shape=[jax.ShapeDtypeStruct(shape, F32) for shape in shapes],
        in_specs=list(specs) + [whole] * 2 + [apart] * (LAYERS * len(Kept._fields)),
        out_specs=[whole] * len(shapes),
        scratch_shapes=held + list(scratch.values()),
        compiler_params=pltpu.CompilerParams(
            collective_id=LAYERS, has_side_effects=True, vmem_limit_bytes=VMEM_LIMIT
        ),
        name="backward",
    )(*params, *cotangents, *[array for kept in saved for array in kept])
    return Grads(*outs)


def shards(stream_one, stream_two, cotangent_one, cotangent_two, bucket_numbers, *params):
    cfg = sizes_of(lax.axis_size("seq"), stream_one, params[0], params[4])
    params = Params(*params)
    first, second = stream_one, stream_two
    saved = []
    for layer in range(LAYERS):
        kept = forward_call(cfg, layer, Streams(first, second, bucket_numbers), params)
        saved.append(kept._replace(second=second))
        first, second = kept.mixed, kept.second
    out = backward_call(cfg, params, (cotangent_one, cotangent_two), saved)
    index = lax.axis_index("seq")

    def columns(extent):
        share = extent // cfg.seq
        return lambda line: lax.dynamic_slice_in_dim(
            out.out_small[:, line], index * share % LANES, share, axis=1
        )

    small = columns(cfg.feats)
    return (
        first,
        second,
        out.first_out,
        out.second_out,
        out.out_wq,
        out.out_wv,
        out.out_wm,
        small(1),
        out.out_we,
        columns(cfg.hid)(6),
        out.out_ws,
        small(0),
        small(4),
        small(5),
        small(2),
        small(3),
    )


def solution(mesh):
    in_specs = (
        P("seq", None),
        P("seq", None),
        P("seq", None),
        P("seq", None),
        P(None, None, "mp", None),
        P(None, None, "mp"),
        P(None, None, "mp"),
        P(None, "mp", None),
        P(),
        P(None, None, "mp"),
        P(None, "mp"),
        P(None, "mp", None),
        P(),
        P(),
        P(),
        P(),
        P(),
    )
    out_specs = (
        P("seq", None),
        P("seq", None),
        P("seq", None),
        P("seq", None),
        P(None, "seq", "mp"),
        P(None, "seq", "mp"),
        P(None, ("mp", "seq"), None),
        P(None, "seq"),
        P(None, "seq", "mp"),
        P(None, ("mp", "seq")),
        P(None, ("mp", "seq"), None),
        P(None, "seq"),
        P(None, "seq"),
        P(None, "seq"),
        P(None, "seq"),
        P(None, "seq"),
    )
    return jax.shard_map(shards, mesh=mesh, in_specs=in_specs, out_specs=out_specs, check_vma=False)
```

```python
import functools
import math
from types import SimpleNamespace
from typing import NamedTuple

import jax
import jax.numpy as jnp
from jax import lax
from jax.experimental import pallas as pl
from jax.experimental.pallas import tpu as pltpu
from jax.sharding import PartitionSpec as P

DH = 128
SPAN = 64
ROUNDS = 4
LAYERS = 2
LANES = 128
CHUNK = 128
UNROLL = 8
MESH = pl.DeviceIdType.MESH
F32 = jnp.float32
BF16 = jnp.bfloat16
AWAY = -1e30
VMEM_LIMIT = 62 << 20


class Sizes(NamedTuple):
    seq: int
    tok: int
    heads: int
    plane: int
    bits: int
    parts: int
    total: int
    rows: int
    ext: int
    buckets: int
    feats: int
    width: int
    hid: int


def sizes_of(seq, stream, query_weight, expand_weight):
    tok, feats = stream.shape
    width = query_weight.shape[2]
    heads = width // DH
    plane = seq // heads
    parts = plane // ROUNDS
    total = seq * tok
    rows = total // parts
    return Sizes(
        seq,
        tok,
        heads,
        plane,
        plane.bit_length() - 1,
        parts,
        total,
        rows,
        rows + CHUNK,
        total // SPAN,
        feats,
        width,
        expand_weight.shape[2],
    )


def dot(left, right):
    return lax.dot_general(left, right, (((1,), (0,)), ((), ())), preferred_element_type=F32)


def dot_nt(left, right):
    return lax.dot_general(left, right, (((1,), (1,)), ((), ())), preferred_element_type=F32)


def dot_tn(left, right):
    return lax.dot_general(left, right, (((0,), (0,)), ((), ())), preferred_element_type=F32)


def norm_parts(values):
    center = values - jnp.mean(values, axis=-1, keepdims=True)
    scale = lax.rsqrt(jnp.mean(center * center, axis=-1, keepdims=True) + 1e-05)
    return center * scale, scale


def norm_back(xhat, scale, gain, grad):
    t = grad * gain
    inner = t - jnp.mean(t, axis=-1, keepdims=True) - xhat * jnp.mean(t * xhat, axis=-1, keepdims=True)
    return scale * inner


def key_scale(keys):
    return lax.rsqrt(jnp.mean(keys * keys, axis=-1, keepdims=True) + 1e-06)


def rows_to_columns(rows):
    return jnp.transpose(jnp.broadcast_to(rows, (LANES, rows.shape[1])))


def split_three(values):
    high = values.astype(BF16).astype(F32)
    rest = values - high
    middle = rest.astype(BF16).astype(F32)
    return high, middle, rest - middle


class Place:
    def __init__(self, cfg):
        self.cfg = cfg
        self.index = lax.axis_index("seq")
        self.half = lax.axis_index("mp")
        self.head = self.index // cfg.plane
        self.member = self.index % cfg.plane
        self.round = self.member // cfg.parts
        self.part = self.member % cfg.parts

    def bit(self, k):
        return (self.member // 2**k) % 2

    def z_peer(self, step):
        head = (self.head + step) % self.cfg.heads
        return head, (head * self.cfg.plane + self.member, self.half)

    def z_source(self, step):
        return (self.head + self.cfg.heads - step) % self.cfg.heads

    def bit_peer(self, k):
        return (self.index + (1 - 2 * self.bit(k)) * 2**k, self.half)

    def y_peer(self):
        return (self.index, 1 - self.half)

    def kept(self, k, i):
        return 2 ** (k + 1) * i + self.member % 2 ** (k + 1)

    def given(self, k, i):
        return 2 ** (k + 1) * i + (1 - self.bit(k)) * 2**k + self.member % 2**k

    def group(self, k):
        return self.cfg.plane // 2 ** (k + 1)

    def plane_peer(self, step):
        member = (self.member + step) % self.cfg.plane
        return member, (self.head * self.cfg.plane + member, self.half)

    def greet(self):
        barrier = pltpu.get_barrier_semaphore()
        peers = [self.z_peer(step)[1] for step in range(1, self.cfg.heads)]
        peers += [self.plane_peer(step)[1] for step in range(1, self.cfg.plane)]
        peers += [self.y_peer()]
        for peer in peers:
            pl.semaphore_signal(barrier, inc=1, device_id=peer, device_id_type=MESH)
        pl.semaphore_wait(barrier, len(peers))


def remote(src, dst, send, recv, peer):
    return pltpu.make_async_remote_copy(
        src_ref=src, dst_ref=dst, send_sem=send, recv_sem=recv, device_id=peer, device_id_type=MESH
    )


def rank_rows(cfg, bucket_row, rank_ref):
    count = cfg.buckets
    ids = lax.broadcasted_iota(jnp.int32, (count, LANES), 0)
    ahead = (
        lax.broadcasted_iota(jnp.int32, (LANES, LANES), 0)
        < lax.broadcasted_iota(jnp.int32, (LANES, LANES), 1)
    ).astype(BF16)
    lower = (
        lax.broadcasted_iota(jnp.int32, (count, count), 1)
        < lax.broadcasted_iota(jnp.int32, (count, count), 0)
    ).astype(BF16)
    marks = [
        (bucket_row[:, p * LANES : (p + 1) * LANES] == ids).astype(F32) for p in range(cfg.seq)
    ]
    totals = sum(marks)
    totals = jnp.broadcast_to(jnp.sum(totals, axis=1, keepdims=True), (count, LANES))
    carry = dot(lower, totals.astype(BF16))
    for p in range(cfg.seq):
        within = dot(marks[p].astype(BF16), ahead)
        rank = jnp.sum(marks[p] * (within + carry), axis=0, keepdims=True)
        carry = carry + jnp.broadcast_to(jnp.sum(marks[p], axis=1, keepdims=True), (count, LANES))
        spot = (p % cfg.plane) * cfg.heads + p // cfg.plane
        rank_ref[:, spot * LANES : (spot + 1) * LANES] = jnp.broadcast_to(
            rank.astype(jnp.int32), (8, LANES)
        )


def sort_rows(cfg, rank_ref, source_ref, store, start, size, chunks):
    step = min(cfg.total, 2048)

    def body(c, _):
        spots = start + c * size + lax.broadcasted_iota(jnp.int32, (size, step), 0)
        spots = spots % cfg.total if cfg.parts > 1 else spots
        found = None
        for k in range(cfg.total // step):
            ranks = rank_ref[0:1, k * step : (k + 1) * step]
            pick = (spots == ranks).astype(BF16)
            part = dot(pick, source_ref[k * step : (k + 1) * step, :])
            found = part if found is None else found + part
        store(c, found)
        return 0

    lax.fori_loop(0, chunks, body, 0)


def several(step, count):
    def body(c, _):
        for i in range(UNROLL):
            step(c * UNROLL + i)
        return 0

    lax.fori_loop(0, count // UNROLL, body, 0)


def window_mask():
    row = lax.broadcasted_iota(jnp.int32, (CHUNK, 2 * CHUNK), 0)
    column = lax.broadcasted_iota(jnp.int32, (CHUNK, 2 * CHUNK), 1)
    gap = column // SPAN - row // SPAN
    near = jnp.logical_or(gap == 1, gap == 2)
    return jnp.logical_and(near, column != row + CHUNK)


def z_exchange(cfg, place, source, target, send, recv):
    copies = []
    for step in range(1, cfg.heads):
        head, peer = place.z_peer(step)
        copy = remote(source(head), target(place.head), send.at[step], recv.at[step], peer)
        copy.start()
        copies.append(copy)
    return copies


def z_arrival(place, block, recv, step):
    return remote(block, block, recv.at[step], recv.at[step], place.z_peer(step)[1])


class Doubling:
    def __init__(self, place, keys, block, send, recv):
        self.place, self.keys, self.block = place, keys, block
        self.send, self.recv = send, recv

    def give(self, key, spot, k):
        return remote(
            self.block(key, spot),
            self.block(key, spot),
            self.send.at[k, key, spot],
            self.recv.at[key, spot],
            self.place.bit_peer(k),
        )

    def offer(self, key):
        for k in range(self.place.cfg.bits):
            self.give(key, self.place.member, k).start()

    def spots(self):
        for k in reversed(range(self.place.cfg.bits)):
            for key in self.keys:
                for i in range(self.place.group(k)):
                    yield k, key, self.place.given(k, i)

    def receive_bit(self, k):
        for key in self.keys:
            for i in range(self.place.group(k)):
                spot = self.place.given(k, i)
                self.give(key, spot, k).wait_recv()
                for low in range(k):
                    self.give(key, spot, low).start()

    def receive(self):
        for k in reversed(range(self.place.cfg.bits)):
            self.receive_bit(k)

    def finish(self):
        for key in self.keys:
            for k in range(self.place.cfg.bits):
                self.give(key, self.place.member, k).wait_send()
        for k, key, spot in self.spots():
            for low in range(k):
                self.give(key, spot, low).wait_send()


class Params(NamedTuple):
    wq_hbm: jax.Array
    wv_hbm: jax.Array
    wm_hbm: jax.Array
    mix_bias: jax.Array
    we_hbm: jax.Array
    expand_bias: jax.Array
    ws_hbm: jax.Array
    shrink_bias: jax.Array
    attention_gain: jax.Array
    attention_shift: jax.Array
    forward_gain: jax.Array
    forward_shift: jax.Array


class Streams(NamedTuple):
    first: jax.Array
    second: jax.Array
    buckets: jax.Array


class Kept(NamedTuple):
    mixed: jax.Array
    sorted: jax.Array
    comb: jax.Array
    joint: jax.Array
    hidden: jax.Array
    rank: jax.Array
    lhs_qv: jax.Array
    lhs_expand: jax.Array
    lhs_shrink: jax.Array
    lhs_mix: jax.Array
    second: jax.Array


class Grads(NamedTuple):
    first_out: jax.Array
    second_out: jax.Array
    out_wq: jax.Array
    out_wv: jax.Array
    out_wm: jax.Array
    out_we: jax.Array
    out_ws: jax.Array
    out_small: jax.Array


def gathered(*groups, **scratch):
    merged = {}
    for group in groups:
        merged.update(group._asdict())
    return SimpleNamespace(**merged, **scratch)


def forward_scratch(cfg):
    tok, heads, plane, bits = cfg.tok, cfg.heads, cfg.plane, cfg.bits
    band = heads * tok
    dma = pltpu.SemaphoreType.DMA
    return dict(
        wq=pltpu.VMEM((cfg.feats, cfg.width), BF16),
        wv=pltpu.VMEM((cfg.feats, cfg.width), BF16),
        wm=pltpu.VMEM((cfg.width, cfg.feats), BF16),
        we=pltpu.VMEM((cfg.feats, cfg.hid), BF16),
        ws=pltpu.VMEM((cfg.hid, cfg.feats), BF16),
        zs=pltpu.VMEM((heads, tok, 2 * DH), BF16),
        tokens=pltpu.VMEM((cfg.total, 2 * DH), BF16),
        keys=pltpu.VMEM((cfg.ext, DH), BF16),
        attended=pltpu.VMEM((cfg.rows, 3 * DH), BF16),
        part=pltpu.VMEM((plane, band, DH), F32),
        lrow=pltpu.VMEM((plane, 8, band), F32),
        part_in=pltpu.VMEM((bits, plane, band, DH), F32),
        lrow_in=pltpu.VMEM((bits, plane, 8, band), F32),
        low_out=pltpu.VMEM((heads, tok, DH), BF16),
        low_in=pltpu.VMEM((heads, tok, DH), BF16),
        ys=pltpu.VMEM((2, tok, cfg.feats), BF16),
        yr=pltpu.VMEM((2, tok, cfg.feats), BF16),
        wsem=dma((5,)),
        zsend=dma((heads,)),
        zrecv=dma((heads,)),
        gsend=dma((bits, heads, plane)),
        grecv=dma((heads, plane)),
        psend=dma((bits, plane, 2)),
        precv=dma((bits, plane, 2)),
        csend=dma((heads,)),
        crecv=dma((heads,)),
        ysend=dma((2,)),
        yrecv=dma((2,)),
        normed_t=pltpu.VMEM((cfg.feats, tok), BF16),
        nsend=dma((heads,)),
        nrecv=dma((heads,)),
        turned_expand=turned_of(cfg, cfg.feats),
        turned_shrink=turned_of(cfg, cfg.hid),
        turned_mix=turned_of(cfg, cfg.width),
        tsend=dma((4, plane)),
        trecv=dma((4, plane)),
    )


class Turned:
    def __init__(self, place, number, values, source, target, r):
        self.place, self.source, self.target = place, source, target
        self.send, self.recv = r.tsend.at[number], r.trecv.at[number]
        source[...] = jnp.transpose(values).reshape(source.shape).astype(source.dtype)

    def slot(self, member):
        tok = self.place.cfg.tok
        return self.target.at[:, :, pl.ds(pl.multiple_of(member * tok, tok), tok)]

    def copy(self, step):
        member, peer = self.place.plane_peer(step)
        return remote(
            self.source.at[:, member], self.slot(self.place.member), self.send.at[step], self.recv.at[step], peer
        )

    def start(self):
        for step in range(1, self.place.cfg.plane):
            self.copy(step).start()
        self.slot(self.place.member)[...] = self.source[:, self.place.member]

    def finish(self):
        cfg = self.place.cfg
        for step in range(1, cfg.plane):
            self.copy(step).wait_send()
            arrived = self.slot((self.place.member + cfg.plane - step) % cfg.plane)
            remote(arrived, arrived, self.send.at[step], self.recv.at[step], self.place.y_peer()).wait_recv()


def y_sum(place, r, slot, partial, meanwhile=None, first=()):
    r.ys[slot] = partial.astype(BF16)
    copy = remote(r.ys.at[slot], r.yr.at[slot], r.ysend.at[slot], r.yrecv.at[slot], place.y_peer())
    copy.start()
    for step in first:
        step()
    if meanwhile is not None:
        meanwhile()
    copy.wait()
    return r.ys[slot].astype(F32) + r.yr[slot].astype(F32)


def forward_kernel(cfg, layer, names, *refs):
    inputs, refs = refs[:IN_COUNT], refs[IN_COUNT:]
    streams, params = Streams(*inputs[:3]), Params(*inputs[3:])
    out, scratch = Kept(*refs[: len(Kept._fields)]), refs[len(Kept._fields) :]
    r = gathered(out, streams, params, **dict(zip(names, scratch, strict=True)))
    r.second, r.renewed = streams.second, out.second
    place = Place(cfg)
    tok, heads = cfg.tok, cfg.heads
    band = heads * tok
    one = slice(layer, layer + 1)
    loads = [
        pltpu.make_async_copy(src.at[layer], dst, r.wsem.at[i])
        for i, (src, dst) in enumerate(
            (
                (r.wq_hbm, r.wq),
                (r.wv_hbm, r.wv),
                (r.wm_hbm, r.wm),
                (r.we_hbm, r.we),
                (r.ws_hbm, r.ws),
            )
        )
    ]
    for load in loads:
        load.start()
    normed = norm_parts(r.second[...])[0] * r.attention_gain[one, :] + r.attention_shift[one, :]
    normed = normed.astype(BF16)
    loads[0].wait()
    loads[1].wait()
    queries = dot(normed, r.wq[...]).astype(BF16)
    values = dot(normed, r.wv[...]).astype(BF16)
    for head in range(heads):
        r.zs[head, :, :DH] = queries[:, head * DH : (head + 1) * DH]
        r.zs[head, :, DH:] = values[:, head * DH : (head + 1) * DH]

    def block(head, spot):
        return r.tokens.at[pl.ds(pl.multiple_of((spot * heads + head) * tok, tok), tok), :]

    place.greet()
    sent = z_exchange(
        cfg,
        place,
        lambda head: r.zs.at[head],
        lambda head: block(head, place.member),
        r.zsend,
        r.zrecv,
    )
    block(place.head, place.member)[...] = r.zs[place.head]
    r.normed_t[...] = jnp.transpose(normed)

    def column(head):
        return r.lhs_qv.at[:, pl.ds(pl.multiple_of(head * tok, tok), tok)]

    column(place.head)[...] = r.normed_t[...]
    rank_rows(cfg, r.buckets[layer, place.round, pl.ds(place.head, 1), :], r.rank)

    spread = Doubling(
        place, [place.z_source(step) for step in range(heads)], block, r.gsend, r.grecv
    )
    for step in range(heads):
        if step > 0:
            z_arrival(place, block(place.z_source(step), place.member), r.zrecv, step).wait_recv()
        spread.offer(place.z_source(step))
    spread.receive()
    sent += z_exchange(cfg, place, lambda head: r.normed_t, column, r.nsend, r.nrecv)
    base = place.part * cfg.rows

    def store_rows(c, found):
        r.sorted[pl.ds(pl.multiple_of(CHUNK + c * 512, CHUNK), 512), :] = found.astype(BF16)

    def store_halo(c, found):
        r.sorted[0:CHUNK, :] = found.astype(BF16)

    sort_rows(cfg, r.rank, r.tokens, store_rows, base, 512, cfg.rows // 512)
    if cfg.parts == 1:
        r.sorted[0:CHUNK, :] = r.sorted[cfg.rows : cfg.ext, :]
    else:
        sort_rows(cfg, r.rank, r.tokens, store_halo, base + cfg.total - CHUNK, CHUNK, 1)
    raw = r.sorted[:, :DH].astype(F32)
    r.keys[...] = (raw * key_scale(raw)).astype(BF16)
    mask = window_mask()
    lane = lax.broadcasted_iota(jnp.int32, (CHUNK, LANES), 1)

    def attend(c):
        at = pl.multiple_of(c * CHUNK, CHUNK)
        query = r.sorted[pl.ds(at + CHUNK, CHUNK), :DH]
        scores = dot_nt(query, r.keys[pl.ds(at, 2 * CHUNK), :]) / math.sqrt(DH)
        scores = jnp.where(mask, scores, -1000000000.0)
        peak = jnp.max(scores, axis=-1, keepdims=True)
        powers = jnp.exp(scores - peak)
        summed = jnp.sum(powers, axis=-1, keepdims=True)
        weights = (powers / summed).astype(BF16)
        output = dot(weights, r.sorted[pl.ds(at, 2 * CHUNK), DH:])
        high, middle, low = split_three(peak + jnp.log(summed))
        extra = jnp.where(lane == 0, high, 0.0)
        extra = jnp.where(lane == 1, middle, extra)
        extra = jnp.where(lane == 2, low, extra)
        extra = jnp.where(lane == 3, 1.0, extra)
        r.attended[pl.ds(at, CHUNK), :DH] = output.astype(BF16)
        r.attended[pl.ds(at, CHUNK), DH : 2 * DH] = (
            output - output.astype(BF16).astype(F32)
        ).astype(BF16)
        r.attended[pl.ds(at, CHUNK), 2 * DH :] = extra.astype(BF16)

    several(attend, cfg.rows // CHUNK)

    def unsort(spot):
        pick = unsort_pick(cfg, r.rank, spot, base, cfg.rows)
        found = dot(pick, r.attended[:, : 2 * DH])
        r.part[spot] = found[:, :DH] + found[:, DH:]
        extra = jnp.transpose(dot(pick, r.attended[:, 2 * DH :]))
        row = extra[0:1] + extra[1:2] + extra[2:3] + (1.0 - extra[3:4]) * AWAY
        r.lrow[spot] = jnp.broadcast_to(row, (8, band))

    def pass_part(k, spot):
        peer = place.bit_peer(k)
        return [
            remote(mine.at[spot], theirs.at[k, spot], r.psend.at[k, spot, i], r.precv.at[k, spot, i], peer)
            for i, (mine, theirs) in enumerate(((r.part, r.part_in), (r.lrow, r.lrow_in)))
        ]

    def first_half(i, _):
        unsort(place.given(0, i))
        for copy in pass_part(0, place.given(0, i)):
            copy.start()
        return 0

    def second_half(i, _):
        unsort(place.kept(0, i))
        return 0

    lax.fori_loop(0, place.group(0), first_half, 0)
    lax.fori_loop(0, place.group(0), second_half, 0)

    def merge(k, spot):
        for copy in pass_part(k, spot):
            copy.wait_recv()
        mine = rows_to_columns(r.lrow[spot][0:1])
        other = rows_to_columns(r.lrow_in[k, spot][0:1])
        highest = jnp.maximum(mine, other)
        share = jnp.exp(mine - highest)
        share_in = jnp.exp(other - highest)
        both = share + share_in
        merged = (r.part[spot].astype(F32) * share + r.part_in[k, spot].astype(F32) * share_in) / both
        return merged, jnp.transpose(highest + jnp.log(both))[0:8]

    for k in range(cfg.bits - 1):
        for giving in (True, False):
            for i in range(place.group(k + 1)):
                spot = place.given(k + 1, i) if giving else place.kept(k + 1, i)
                merged, joint = merge(k, spot)
                r.part[spot] = merged
                r.lrow[spot] = joint
                if giving:
                    for copy in pass_part(k + 1, spot):
                        copy.start()
    merged, joint = merge(cfg.bits - 1, place.member)
    r.comb[...] = merged
    r.joint[...] = joint
    for head in range(heads):
        r.low_out[head] = merged[head * tok : (head + 1) * tok].astype(BF16)
    back = z_exchange(
        cfg, place, lambda head: r.low_out.at[head], lambda head: r.low_in.at[head], r.csend, r.crecv
    )
    r.low_in[place.head] = r.low_out[place.head]
    loads[2].wait()
    for step in range(1, heads):
        z_arrival(place, r.low_in.at[place.z_source(step)], r.crecv, step).wait_recv()
    low = jnp.concatenate([r.low_in[head] for head in range(heads)], axis=1)

    turned_mix = Turned(place, 3, low, r.turned_mix, r.lhs_mix, r)

    def finish_sends():
        spread.finish()
        for copy in sent + back:
            copy.wait_send()
        for k in range(cfg.bits):
            for i in range(place.group(k)):
                for copy in pass_part(k, place.given(k, i)):
                    copy.wait_send()
        turned_mix.start()

    mixed = (
        r.first[...]
        + y_sum(place, r, 0, dot(low, r.wm[...]), finish_sends)
        + r.mix_bias[one, :]
    )
    r.mixed[...] = mixed
    normed_two = norm_parts(mixed)[0] * r.forward_gain[one, :] + r.forward_shift[one, :]
    normed_two = normed_two.astype(BF16)
    loads[3].wait()
    hidden = dot(normed_two, r.we[...]) + r.expand_bias[one, :]
    r.hidden[...] = hidden
    active = (hidden * (1.0 + lax.erf(hidden * math.sqrt(0.5))) * 0.5).astype(BF16)
    loads[4].wait()

    def turn():
        turned_shrink = Turned(place, 2, active, r.turned_shrink, r.lhs_shrink, r)
        turned_shrink.start()
        turned_expand = Turned(place, 1, normed_two, r.turned_expand, r.lhs_expand, r)
        turned_expand.start()
        for turned in (turned_mix, turned_shrink, turned_expand):
            turned.finish()
        for step in range(1, heads):
            z_arrival(place, column(place.z_source(step)), r.nrecv, step).wait_recv()

    r.renewed[...] = (
        r.second[...] + y_sum(place, r, 1, dot(active, r.ws[...]), turn) + r.shrink_bias[one, :]
    )


def unsort_pick(cfg, rank_ref, spot, base, rows):
    band = cfg.heads * cfg.tok
    ranks = rank_ref[0:1, pl.ds(pl.multiple_of(spot * band, band), band)]
    ranks = rows_to_columns(ranks.astype(F32)).astype(jnp.int32)[:, 0:1]
    places = base + lax.broadcasted_iota(jnp.int32, (band, rows), 1)
    if cfg.parts > 1:
        places = places % cfg.total
    return (ranks == places).astype(BF16)


IN_COUNT = len(Streams._fields) + len(Params._fields)


def forward_call(cfg, layer, streams, params):
    scratch = forward_scratch(cfg)
    whole = pl.BlockSpec(memory_space=pltpu.VMEM)
    apart = pl.BlockSpec(memory_space=pl.ANY)
    specs = Params(*[whole] * len(params))._replace(
        wq_hbm=apart, wv_hbm=apart, wm_hbm=apart, we_hbm=apart, ws_hbm=apart
    )
    outs = pl.pallas_call(
        functools.partial(forward_kernel, cfg, layer, list(scratch)),
        out_shape=[jax.ShapeDtypeStruct(*shape) for shape in saved_shapes(cfg)],
        in_specs=[whole] * len(streams) + list(specs),
        out_specs=[whole] * len(Kept._fields),
        scratch_shapes=list(scratch.values()),
        compiler_params=pltpu.CompilerParams(
            collective_id=layer, has_side_effects=True, vmem_limit_bytes=VMEM_LIMIT
        ),
        name=f"forward_{layer}",
    )(*streams, *params)
    return Kept(*outs)


def lines_of(cfg, extent):
    deep = extent // cfg.seq
    return (cfg.heads, deep, cfg.plane * cfg.tok), BF16 if deep % 16 == 0 else F32


def turned_of(cfg, extent):
    (heads, deep, _), kind = lines_of(cfg, extent)
    return pltpu.VMEM((heads, cfg.plane, deep, cfg.tok), kind)


def saved_shapes(cfg):
    tok, feats, band = cfg.tok, cfg.feats, cfg.heads * cfg.tok
    return Kept(
        second=((tok, feats), F32),
        mixed=((tok, feats), F32),
        sorted=((cfg.ext, 2 * DH), BF16),
        comb=((band, DH), F32),
        joint=((8, band), F32),
        hidden=((tok, cfg.hid), F32),
        rank=((8, cfg.total), jnp.int32),
        lhs_qv=((feats, band), BF16),
        lhs_expand=lines_of(cfg, feats),
        lhs_shrink=lines_of(cfg, cfg.hid),
        lhs_mix=lines_of(cfg, cfg.width),
    )


class Job(NamedTuple):
    name: str
    side: str
    number: int
    rows: int
    columns: int
    fold: int

    def scratch(self, cfg):
        deep, wide = self.rows * self.fold, self.columns // self.fold
        return {
            "rhs" + self.side: pltpu.VMEM((cfg.plane * cfg.tok, self.columns), BF16),
            "prod" + self.name: pltpu.VMEM((cfg.heads, deep, wide), BF16),
            "zin" + self.name: pltpu.VMEM((3, deep, wide), BF16),
        }


def slots_of(cfg):
    return LAYERS if cfg.parts == 1 else 1


def jobs_of(cfg):
    share = cfg.feats // cfg.seq
    mix = cfg.width // cfg.seq
    return (
        Job("s", "s", 0, cfg.hid // cfg.seq, cfg.feats, 1),
        Job("m", "m", 1, mix, cfg.feats, 1 if mix % 16 == 0 else 2),
    ) + tuple(
        Job(f"e{i}", f"e{i}", 2 + i, share, cfg.feats, 1) for i in range(cfg.hid // cfg.feats)
    )


def backward_scratch(cfg):
    tok, heads, plane, bits = cfg.tok, cfg.heads, cfg.plane, cfg.bits
    band = heads * tok
    dma = pltpu.SemaphoreType.DMA
    return dict(
        wq=pltpu.VMEM((cfg.feats, cfg.width), BF16),
        wv=pltpu.VMEM((cfg.feats, cfg.width), BF16),
        wm=pltpu.VMEM((cfg.width, cfg.feats), BF16),
        we=pltpu.VMEM((cfg.feats, cfg.hid), BF16),
        ws=pltpu.VMEM((cfg.hid, cfg.feats), BF16),
        gs=pltpu.VMEM((heads, tok, DH), BF16),
        gtokens=pltpu.VMEM((cfg.total, 2 * DH), BF16),
        arow=pltpu.VMEM((LAYERS, plane, 8, band), F32),
        gsorted=pltpu.VMEM((cfg.rows, DH), BF16),
        stats=pltpu.VMEM((cfg.rows, LANES), F32),
        keys=pltpu.VMEM((cfg.ext, DH), BF16),
        dq=pltpu.VMEM((cfg.ext, DH), F32),
        dk=pltpu.VMEM((cfg.ext, DH), F32),
        dv=pltpu.VMEM((cfg.ext, DH), F32),
        grads=pltpu.VMEM((cfg.ext, 2 * DH), BF16),
        part=pltpu.VMEM((plane, band, 2 * DH), BF16),
        part_in=pltpu.VMEM((plane, band, 2 * DH), BF16),
        home_out=pltpu.VMEM((heads, tok, 2 * DH), BF16),
        home_in=pltpu.VMEM((heads, tok, 2 * DH), BF16),
        ys=pltpu.VMEM((2, tok, cfg.feats), BF16),
        yr=pltpu.VMEM((2, tok, cfg.feats), BF16),
        vectors=pltpu.VMEM((8, cfg.feats), F32),
        **{key: value for job in jobs_of(cfg) for key, value in job.scratch(cfg).items()},
        vbuf=pltpu.VMEM((LAYERS, plane, heads, 8, LANES), F32),
        vin=pltpu.VMEM((LAYERS, plane, heads, 8, LANES), F32),
        vz=pltpu.VMEM((LAYERS, heads, 8, LANES), F32),
        wsem=dma((5,)),
        lsem=dma((LAYERS, len(Kept._fields))),
        zsend=dma((LAYERS, heads)),
        zrecv=dma((LAYERS, heads)),
        gsend=dma((LAYERS, bits, heads, plane)),
        grecv=dma((LAYERS, heads, plane)),
        asend=dma((LAYERS, bits, 1, plane)),
        arecv=dma((LAYERS, 1, plane)),
        psend=dma((LAYERS, bits, plane)),
        precv=dma((LAYERS, bits, plane)),
        csend=dma((LAYERS, heads)),
        crecv=dma((LAYERS, heads)),
        ysend=dma((2,)),
        yrecv=dma((2,)),
        rsend=dma((len(jobs_of(cfg)), bits, 1, plane)),
        rrecv=dma((len(jobs_of(cfg)), 1, plane)),
        usend=dma((len(jobs_of(cfg)), 3)),
        urecv=dma((len(jobs_of(cfg)), 3)),
        qbuf=pltpu.VMEM((plane, heads, cfg.feats // cfg.seq, 2 * DH), BF16),
        qin=pltpu.VMEM((plane, heads, cfg.feats // cfg.seq, 2 * DH), BF16),
        qz=pltpu.VMEM((heads, cfg.feats // cfg.seq, 2 * DH), BF16),
        qsend=dma((bits + heads,)),
        qrecv=dma((bits + heads,)),
        vsend=dma((LAYERS, bits + heads)),
        vrecv=dma((LAYERS, bits + heads)),
    )


class Unit:
    def __init__(self, place, fill, done, buf, arrive, zbuf, send, recv):
        self.place, self.fill, self.done = place, fill, done
        self.buf, self.arrive, self.zbuf, self.send, self.recv = buf, arrive, zbuf, send, recv

    def halved(self, k):
        place, plane = self.place, self.place.cfg.plane
        group = place.group(k)
        start = plane - plane // 2**k
        shape = (group, 2 ** (k + 1)) + self.buf.shape[1:]
        spot = (1 - place.bit(k)) * 2**k + place.member % 2**k
        return remote(
            self.buf.reshape(*shape).at[:, spot],
            self.arrive.at[start : start + group],
            self.send.at[k],
            self.recv.at[k],
            place.bit_peer(k),
        )

    def across(self, step):
        place = self.place
        head, peer = place.z_peer(step)
        at = place.cfg.bits + step
        return remote(
            self.buf.at[place.member, head], self.zbuf.at[step], self.send.at[at], self.recv.at[at], peer
        )

    def start(self):
        self.fill(self.buf)
        self.halved(0).start()

    def fold(self):
        place, cfg = self.place, self.place.cfg
        for k in range(cfg.bits):
            self.halved(k).wait_recv()
            start = cfg.plane - cfg.plane // 2**k
            for i in range(place.group(k)):
                spot = place.kept(k, i)
                both = self.buf[spot].astype(F32) + self.arrive[start + i].astype(F32)
                self.buf[spot] = both.astype(self.buf.dtype)
            if k + 1 < cfg.bits:
                self.halved(k + 1).start()
            if k + 2 == cfg.bits:
                yield
        for step in range(1, cfg.heads):
            self.across(step).start()
        yield
        found = [(place.head, self.buf[place.member, place.head])]
        for step in range(1, cfg.heads):
            self.across(step).wait_recv()
            found.append((place.z_source(step), self.zbuf[step]))
        self.done(found)
        for k in range(cfg.bits):
            self.halved(k).wait_send()
        for step in range(1, cfg.heads):
            self.across(step).wait_send()
        yield


class Gathered:
    def __init__(self, place, job, left, right, done, r):
        self.place, self.job, self.left, self.right, self.done = place, job, left, right, done
        tok = place.cfg.tok
        self.rhs = vars(r)["rhs" + job.side]
        self.prod, self.zin = vars(r)["prod" + job.name], vars(r)["zin" + job.name]
        self.send, self.recv = r.usend.at[job.number], r.urecv.at[job.number]
        self.spread = Doubling(
            place,
            [0],
            lambda key, spot: self.rhs.at[pl.ds(pl.multiple_of(spot * tok, tok), tok), :],
            r.rsend.at[job.number],
            r.rrecv.at[job.number],
        )
        head = place.head
        self.inner = (head * (3 - head)) // 2
        self.near = head + 1 - 2 * (head % 2)
        self.far = 3 - 3 * (head // 2)

    def copy(self, number):
        place, inner = self.place, self.inner
        if number == 0:
            dest, block, slot = self.near, self.near, 0
        elif number == 1:
            dest, block, slot = self.far, self.far, 2 - inner
        else:
            other = 3 - place.head
            dest = self.near * (1 - inner) + other * inner
            block = (3 - self.near) * (1 - inner) + other * inner
            slot = 2 - inner
        return remote(
            self.prod.at[block],
            self.zin.at[slot],
            self.send.at[number],
            self.recv.at[slot],
            (dest * place.cfg.plane + place.member, place.half),
        )

    def arrival(self, slot):
        spot = self.zin.at[slot]
        return remote(spot, spot, self.send.at[slot], self.recv.at[slot], self.place.y_peer())

    def start(self):
        self.spread.block(0, self.place.member)[...] = self.right
        self.spread.offer(0)

    def forward(self):
        for k in reversed(range(1, self.place.cfg.bits)):
            self.spread.receive_bit(k)

    def multiply(self):
        cfg, job = self.place.cfg, self.job
        self.spread.receive_bit(0)
        lines = self.left[...].reshape(cfg.heads * job.rows, cfg.plane * cfg.tok).astype(BF16)
        wide = job.columns // job.fold
        found = [
            dot(lines, self.rhs[:, i * wide : (i + 1) * wide]).reshape(cfg.heads, job.rows, wide)
            for i in range(job.fold)
        ]
        found = found[0] if job.fold == 1 else jnp.concatenate(found, axis=1)
        self.prod[...] = found.astype(BF16)

        @pl.when(self.inner == 0)
        def _():
            self.copy(2).start()

        self.copy(1).start()
        self.copy(0).start()
        self.spread.finish()

    def relay(self):
        @pl.when(self.inner == 1)
        def _():
            self.arrival(2).wait_recv()
            block = 3 - self.place.head
            both = self.prod[block].astype(F32) + self.zin[2].astype(F32)
            self.prod[block] = both.astype(BF16)
            self.copy(2).start()

    def finish(self):
        self.arrival(0).wait_recv()
        self.arrival(1).wait_recv()

        @pl.when(self.inner == 0)
        def _():
            self.arrival(2).wait_recv()

        total = self.prod[self.place.head].astype(F32)
        total = total + self.zin[0].astype(F32) + self.zin[1].astype(F32)
        total = jnp.where(self.inner == 0, total + self.zin[2].astype(F32), total)
        wide, deep = self.job.columns // self.job.fold, self.job.rows
        for i in range(self.job.fold):
            self.done(total[i * deep : (i + 1) * deep], i * wide, wide)
        for number in range(3):
            self.copy(number).wait_send()


def backward_kernel(cfg, names, *refs):
    params, refs = Params(*refs[: len(Params._fields)]), refs[len(Params._fields) :]
    (first_cot, second_cot), refs = refs[:2], refs[2:]
    stored, held = [], []
    for _ in range(LAYERS):
        stored.append(Kept(*refs[: len(Kept._fields)]))
        refs = refs[len(Kept._fields) :]
    out, refs = Grads(*refs[: len(Grads._fields)]), refs[len(Grads._fields) :]
    for _ in range(slots_of(cfg)):
        held.append(Kept(*refs[: len(Kept._fields)]))
        refs = refs[len(Kept._fields) :]
    held = held * (LAYERS // len(held))
    r = gathered(params, out, **dict(zip(names, refs, strict=True)))
    place = Place(cfg)
    tok, heads, plane, width = cfg.tok, cfg.heads, cfg.plane, cfg.width
    band = heads * tok
    share = cfg.feats // cfg.seq
    base = place.part * cfg.rows
    jobs = jobs_of(cfg)

    def weight_load(i, layer):
        source = (r.ws_hbm, r.we_hbm, r.wm_hbm, r.wq_hbm, r.wv_hbm)[i]
        target = (r.ws, r.we, r.wm, r.wq, r.wv)[i]
        return pltpu.make_async_copy(source.at[layer], target, r.wsem.at[i])

    def saved_load(layer, ref):
        i = [ref is other for other in held[layer]].index(True)
        return pltpu.make_async_copy(stored[layer][i], ref, r.lsem.at[layer, i])

    def weight(number, layer, left, right):
        out = (r.out_ws, r.out_wm)[number] if number < 2 else r.out_we
        first = max(number - 2, 0) * cfg.feats

        def done(total, start, wide):
            out[layer, :, first + start : first + start + wide] = total

        return Gathered(place, jobs[number], left, right, done, r)

    def attention_weights(layer, left, right):
        def fill(buf):
            for head in range(heads):
                rows = left[head * plane * share : (head + 1) * plane * share, :]
                buf[:, head] = dot(rows, right).reshape(plane, share, 2 * DH).astype(BF16)

        def done(found):
            for head, both in found:
                at = pl.ds(pl.multiple_of(head * DH, DH), DH)
                r.out_wq[layer, :, at] = both[:, :DH].astype(F32)
                r.out_wv[layer, :, at] = both[:, DH:].astype(F32)

        return Unit(place, fill, done, r.qbuf, r.qin, r.qz, r.qsend, r.qrecv)

    def vector_sums(layer):
        def fill(buf):
            deep = cfg.hid // cfg.seq
            for p in range(cfg.seq):
                at = p * share // LANES * LANES
                tile = r.vectors[:, at : at + LANES]
                at = p * deep // LANES * LANES
                line, at = 6 + at // cfg.feats, at % cfg.feats
                extra = r.vectors[line : line + 1, at : at + LANES]
                buf[p % plane, p // plane, 0:6] = tile[0:6]
                buf[p % plane, p // plane, 6:8] = jnp.broadcast_to(extra, (2, LANES))

        def done(found):
            r.out_small[layer] = sum(both for _, both in found)

        return Unit(
            place, fill, done, r.vbuf.at[layer], r.vin.at[layer], r.vz.at[layer], r.vsend.at[layer], r.vrecv.at[layer]
        )

    order = list(reversed(range(LAYERS)))
    for i in range(5):
        weight_load(i, order[0]).start()

    def fetch(layer):
        k = held[layer]
        for ref in (k.hidden, k.lhs_shrink, k.mixed, k.lhs_expand, k.comb, k.joint, k.sorted):
            saved_load(layer, ref).start()
        for ref in (k.rank, k.lhs_mix, k.second, k.lhs_qv):
            saved_load(layer, ref).start()

    for layer in order[: slots_of(cfg)]:
        fetch(layer)
    place.greet()
    late, small, last = None, None, None

    for layer in order:
        one = slice(layer, layer + 1)
        after = layer - 1

        saved = held[layer]

        def arrived(*fields):
            for field in fields:
                saved_load(layer, field).wait()

        def next_weight(*numbers):
            if after >= 0:
                for i in numbers:
                    weight_load(i, after).start()

        second_grad = second_cot if layer == order[0] else r.second_out
        first_grad = first_cot if layer == order[0] else r.first_out
        branch = second_grad[...].astype(BF16)
        arrived(saved.hidden, saved.lhs_shrink)
        shrink = weight(0, layer, saved.lhs_shrink, branch)
        shrink.start()
        r.vectors[0:1, :] = jnp.sum(branch.astype(F32), axis=0, keepdims=True)
        hidden = saved.hidden[...]
        slope = 0.5 * (1.0 + lax.erf(hidden * math.sqrt(0.5)))
        slope = slope + hidden * jnp.exp(-0.5 * hidden * hidden) * (1.0 / math.sqrt(2.0 * math.pi))
        weight_load(0, layer).wait()
        hidden_grad = (dot_nt(branch, r.ws[...]) * slope).astype(BF16)
        next_weight(0)
        weight_load(1, layer).wait()
        partial = dot_nt(hidden_grad, r.we[...])
        next_weight(1)
        arrived(saved.mixed, saved.lhs_expand)

        def during_two():
            summed = jnp.sum(hidden_grad.astype(F32), axis=0, keepdims=True)
            for i in range(cfg.hid // cfg.feats):
                r.vectors[6 + i : 7 + i, :] = summed[:, i * cfg.feats : (i + 1) * cfg.feats]
            if late is not None:
                for job in late:
                    job.relay()
                next(last)
                next(small)
            shrink.forward()

        expand = [
            weight(2 + i, layer, saved.lhs_expand, hidden_grad[:, i * cfg.feats : (i + 1) * cfg.feats])
            for i in range(cfg.hid // cfg.feats)
        ]
        two_grad = y_sum(place, r, 0, partial, during_two, [expand[0].start])
        xhat, scale = norm_parts(saved.mixed[...])
        mixed_grad = first_grad[...] + norm_back(xhat, scale, r.forward_gain[one, :], two_grad)
        r.first_out[...] = mixed_grad
        mix_low = mixed_grad.astype(BF16)
        weight_load(2, layer).wait()
        combined_grad = dot_nt(mix_low, r.wm[...]).astype(BF16)
        next_weight(2)
        for head in range(heads):
            r.gs[head] = combined_grad[:, head * DH : (head + 1) * DH]

        def rows_of(spot, head):
            return pl.ds(pl.multiple_of((spot * heads + head) * tok, tok), tok)

        def block(head, spot):
            return r.gtokens.at[rows_of(spot, head), :DH]

        sent = z_exchange(
            cfg,
            place,
            lambda head: r.gs.at[head],
            lambda head: block(head, place.member),
            r.zsend.at[layer],
            r.zrecv.at[layer],
        )
        block(place.head, place.member)[...] = r.gs[place.head]
        r.vectors[1:2, :] = jnp.sum(mix_low.astype(F32), axis=0, keepdims=True)
        r.vectors[2:3, :] = jnp.sum(two_grad * xhat, axis=0, keepdims=True)
        r.vectors[3:4, :] = jnp.sum(two_grad, axis=0, keepdims=True)
        arrived(saved.sorted, saved.rank, saved.comb, saved.joint, saved.lhs_mix)
        rank = saved.rank
        rows = saved.sorted
        mixing = weight(1, layer, saved.lhs_mix, mix_low)
        raw = rows[:, :DH].astype(F32)
        r.keys[...] = (raw * key_scale(raw)).astype(BF16)
        if late is not None:
            for job in late:
                job.finish()
            next(last)
        spread = Doubling(
            place,
            [place.z_source(step) for step in range(heads)],
            block,
            r.gsend.at[layer],
            r.grecv.at[layer],
        )
        for step in range(heads):
            if step > 0:
                spot = block(place.z_source(step), place.member)
                z_arrival(place, spot, r.zrecv.at[layer], step).wait_recv()
            spread.offer(place.z_source(step))
        mine = r.gtokens[pl.ds(pl.multiple_of(place.member * band, band), band), :DH].astype(F32)
        inner = jnp.sum(jnp.transpose(mine * saved.comb[...]), axis=0, keepdims=True)
        line = lax.broadcasted_iota(jnp.int32, (8, band), 0)
        r.arow[layer, place.member] = jnp.where(
            line == 0, saved.joint[...], jnp.broadcast_to(inner, (8, band))
        )
        extras = Doubling(
            place,
            [0],
            lambda key, spot: r.arow.at[layer, spot],
            r.asend.at[layer],
            r.arecv.at[layer],
        )
        extras.offer(0)
        shrink.multiply()
        spread.receive()
        extras.receive()
        expand[0].forward()
        expand[1].start()
        mixing.start()
        if late is not None:
            next(small)
        lines = lax.broadcasted_iota(jnp.int32, (LANES, band), 0)
        for spot in range(plane):
            pieces = split_three(r.arow[layer, spot][0:1]) + split_three(r.arow[layer, spot][1:2])
            table = jnp.zeros((LANES, band), F32)
            for i, piece in enumerate(pieces):
                table = jnp.where(lines == i, piece, table)
            r.gtokens[spot * band : (spot + 1) * band, DH:] = jnp.transpose(table).astype(BF16)

        def store_rows(c, found):
            at = pl.ds(pl.multiple_of(c * 512, 512), 512)
            r.gsorted[at, :] = found[:, :DH].astype(BF16)
            r.stats[at, :] = found[:, DH:]

        sort_rows(cfg, rank, r.gtokens, store_rows, base, 512, cfg.rows // 512)
        if late is not None:
            next(small)
        r.dq[0:CHUNK, :] = jnp.zeros((CHUNK, DH), F32)
        r.dk[0:CHUNK, :] = jnp.zeros((CHUNK, DH), F32)
        r.dv[0:CHUNK, :] = jnp.zeros((CHUNK, DH), F32)
        mask = window_mask()

        def attend(c):
            at = pl.multiple_of(c * CHUNK, CHUNK)
            own = pl.ds(at + CHUNK, CHUNK)
            window = pl.ds(at, 2 * CHUNK)
            query = rows[own, :DH]
            near = r.keys[window, :]
            grad = r.gsorted[pl.ds(at, CHUNK), :]
            stats = r.stats[pl.ds(at, CHUNK), :]
            joint = stats[:, 0:1] + stats[:, 1:2] + stats[:, 2:3]
            inner = stats[:, 3:4] + stats[:, 4:5] + stats[:, 5:6]
            scores = dot_nt(query, near) / math.sqrt(DH)
            scores = jnp.where(mask, scores, -1000000000.0)
            probs = jnp.exp(scores - joint)
            prob_grad = dot_nt(grad, rows[window, DH:])
            score_grad = (probs * (prob_grad - inner) / math.sqrt(DH)).astype(BF16)
            r.dq[own, :] = dot(score_grad, near)
            return dot_tn(score_grad, query), dot_tn(probs.astype(BF16), grad)

        def attend_some(i, _):
            parts = [attend(i * UNROLL + u) for u in range(UNROLL)]
            for ref, found in zip((r.dk, r.dv), zip(*parts)):
                for u in range(UNROLL):
                    at = pl.multiple_of((i * UNROLL + u) * CHUNK, CHUNK)
                    if u == 0:
                        before = pl.ds(at, CHUNK)
                        ref[before, :] = ref[before, :] + found[u][:CHUNK]
                    own = found[u][CHUNK:]
                    if u + 1 < UNROLL:
                        own = own + found[u + 1][:CHUNK]
                    ref[pl.ds(at + CHUNK, CHUNK), :] = own
            return 0

        rounds = cfg.rows // CHUNK // UNROLL
        lax.fori_loop(0, rounds // 2, attend_some, 0)
        shrink.relay()
        expand[0].multiply()
        expand[1].forward()
        lax.fori_loop(rounds // 2, rounds, attend_some, 0)
        if cfg.parts == 1:
            last = slice(cfg.rows, cfg.ext)
            r.dk[last, :] = r.dk[last, :] + r.dk[0:CHUNK, :]
            r.dv[last, :] = r.dv[last, :] + r.dv[0:CHUNK, :]
        raw = rows[:, :DH].astype(F32)
        scale = key_scale(raw)
        dk = r.dk[...]
        inner = jnp.mean(raw * dk, axis=-1, keepdims=True)
        r.grads[:, :DH] = (
            r.dq[...] + scale * dk - raw * (scale * scale * scale * inner)
        ).astype(BF16)
        r.grads[:, DH:] = r.dv[...].astype(BF16)
        skip = CHUNK if cfg.parts == 1 else 0

        def unsort(spot):
            start = base if cfg.parts == 1 else base + cfg.total - CHUNK
            pick = unsort_pick(cfg, rank, spot, start, cfg.ext - skip)
            r.part[spot] = dot(pick, r.grads[skip:, :]).astype(BF16)

        def pass_part(k, spot):
            return remote(
                r.part.at[spot],
                r.part_in.at[plane - plane // 2**k + spot // 2 ** (k + 1)],
                r.psend.at[layer, k, spot],
                r.precv.at[layer, k, spot // 2 ** (k + 1)],
                place.bit_peer(k),
            )

        def first_half(i, _):
            unsort(place.given(0, i))
            pass_part(0, place.given(0, i)).start()
            return 0

        def second_half(i, _):
            unsort(place.kept(0, i))
            return 0

        lax.fori_loop(0, place.group(0), first_half, 0)
        lax.fori_loop(0, place.group(0), second_half, 0)

        def merge(k, spot):
            pass_part(k, spot).wait_recv()
            other = r.part_in[plane - plane // 2**k + spot // 2 ** (k + 1)]
            return (r.part[spot].astype(F32) + other.astype(F32)).astype(BF16)

        for k in range(cfg.bits - 1):
            for giving in (True, False):
                for i in range(place.group(k + 1)):
                    spot = place.given(k + 1, i) if giving else place.kept(k + 1, i)
                    r.part[spot] = merge(k, spot)
                    if giving:
                        pass_part(k + 1, spot).start()
        spread.finish()
        extras.finish()
        shrink.finish()
        expand[0].relay()
        mixing.forward()
        merged = merge(cfg.bits - 1, place.member)
        for head in range(heads):
            r.home_out[head] = merged[head * tok : (head + 1) * tok]
        back = z_exchange(
            cfg,
            place,
            lambda head: r.home_out.at[head],
            lambda head: r.home_in.at[head],
            r.csend.at[layer],
            r.crecv.at[layer],
        )
        r.home_in[place.head] = r.home_out[place.head]
        arrived(saved.second, saved.lhs_qv)
        last = attention_weights(layer, saved.lhs_qv, merged)
        last.start()
        last = last.fold()
        weight_load(3, layer).wait()
        weight_load(4, layer).wait()
        expand[0].finish()
        next(last)
        for step in range(1, heads):
            spot = r.home_in.at[place.z_source(step)]
            z_arrival(place, spot, r.crecv.at[layer], step).wait_recv()
        query_grad = jnp.concatenate([r.home_in[head][:, :DH] for head in range(heads)], axis=1)
        value_grad = jnp.concatenate([r.home_in[head][:, DH:] for head in range(heads)], axis=1)
        one_grad = dot_nt(query_grad, r.wq[...]) + dot_nt(value_grad, r.wv[...])
        next_weight(3, 4)

        late = [expand[1], mixing]

        def during_one():
            for copy in sent + back:
                copy.wait_send()
            for k in range(cfg.bits):
                for i in range(place.group(k)):
                    pass_part(k, place.given(k, i)).wait_send()

        one_grad = y_sum(place, r, 1, one_grad, during_one, [job.multiply for job in late])
        xhat, scale = norm_parts(saved.second[...])
        dx = norm_back(xhat, scale, r.attention_gain[one, :], one_grad)
        r.second_out[...] = second_grad[...] + dx
        r.vectors[4:5, :] = jnp.sum(one_grad * xhat, axis=0, keepdims=True)
        r.vectors[5:6, :] = jnp.sum(one_grad, axis=0, keepdims=True)
        small = vector_sums(layer)
        small.start()
        small = small.fold()
        if layer > 0 and slots_of(cfg) == 1:
            fetch(layer - 1)
    for job in late:
        job.relay()
    next(last)
    next(small)
    for job in late:
        job.finish()
    next(last)
    next(small)
    next(small)


def backward_call(cfg, params, cotangents, saved):
    scratch = backward_scratch(cfg)
    tok, feats = cfg.tok, cfg.feats
    share = feats // cfg.seq
    shapes = Grads(
        first_out=(tok, feats),
        second_out=(tok, feats),
        out_wq=(LAYERS, share, cfg.width),
        out_wv=(LAYERS, share, cfg.width),
        out_wm=(LAYERS, cfg.width // cfg.seq, feats),
        out_we=(LAYERS, share, cfg.hid),
        out_ws=(LAYERS, cfg.hid // cfg.seq, feats),
        out_small=(LAYERS, 8, LANES),
    )
    whole = pl.BlockSpec(memory_space=pltpu.VMEM)
    apart = pl.BlockSpec(memory_space=pl.ANY)
    specs = Params(*[apart] * len(params))._replace(attention_gain=whole, forward_gain=whole)
    held = [pltpu.VMEM(*shape) for shape in saved_shapes(cfg)] * slots_of(cfg)
    outs = pl.pallas_call(
        functools.partial(backward_kernel, cfg, list(scratch)),
        out_shape=[jax.ShapeDtypeStruct(shape, F32) for shape in shapes],
        in_specs=list(specs) + [whole] * 2 + [apart] * (LAYERS * len(Kept._fields)),
        out_specs=[whole] * len(shapes),
        scratch_shapes=held + list(scratch.values()),
        compiler_params=pltpu.CompilerParams(
            collective_id=LAYERS, has_side_effects=True, vmem_limit_bytes=VMEM_LIMIT
        ),
        name="backward",
    )(*params, *cotangents, *[array for kept in saved for array in kept])
    return Grads(*outs)


def shards(stream_one, stream_two, cotangent_one, cotangent_two, bucket_numbers, *params):
    cfg = sizes_of(lax.axis_size("seq"), stream_one, params[0], params[4])
    params = Params(*params)
    first, second = stream_one, stream_two
    saved = []
    for layer in range(LAYERS):
        kept = forward_call(cfg, layer, Streams(first, second, bucket_numbers), params)
        saved.append(kept._replace(second=second))
        first, second = kept.mixed, kept.second
    out = backward_call(cfg, params, (cotangent_one, cotangent_two), saved)
    index = lax.axis_index("seq")

    def columns(extent):
        share = extent // cfg.seq
        return lambda line: lax.dynamic_slice_in_dim(
            out.out_small[:, line], index * share % LANES, share, axis=1
        )

    small = columns(cfg.feats)
    return (
        first,
        second,
        out.first_out,
        out.second_out,
        out.out_wq,
        out.out_wv,
        out.out_wm,
        small(1),
        out.out_we,
        columns(cfg.hid)(6),
        out.out_ws,
        small(0),
        small(4),
        small(5),
        small(2),
        small(3),
    )


def solution(mesh):
    in_specs = (
        P("seq", None),
        P("seq", None),
        P("seq", None),
        P("seq", None),
        P(None, None, "mp", None),
        P(None, None, "mp"),
        P(None, None, "mp"),
        P(None, "mp", None),
        P(),
        P(None, None, "mp"),
        P(None, "mp"),
        P(None, "mp", None),
        P(),
        P(),
        P(),
        P(),
        P(),
    )
    out_specs = (
        P("seq", None),
        P("seq", None),
        P("seq", None),
        P("seq", None),
        P(None, "seq", "mp"),
        P(None, "seq", "mp"),
        P(None, ("mp", "seq"), None),
        P(None, "seq"),
        P(None, "seq", "mp"),
        P(None, ("mp", "seq")),
        P(None, ("mp", "seq"), None),
        P(None, "seq"),
        P(None, "seq"),
        P(None, "seq"),
        P(None, "seq"),
        P(None, "seq"),
    )
    return jax.shard_map(shards, mesh=mesh, in_specs=in_specs, out_specs=out_specs, check_vma=False)
```

```python
import functools
import math
from types import SimpleNamespace
from typing import NamedTuple

import jax
import jax.numpy as jnp
from jax import lax
from jax.experimental import pallas as pl
from jax.experimental.pallas import tpu as pltpu
from jax.sharding import PartitionSpec as P

DH = 128
SPAN = 64
ROUNDS = 4
LAYERS = 2
LANES = 128
CHUNK = 128
UNROLL = 8
MESH = pl.DeviceIdType.MESH
F32 = jnp.float32
BF16 = jnp.bfloat16
AWAY = -1e30
VMEM_LIMIT = 62 << 20


class Sizes(NamedTuple):
    seq: int
    tok: int
    heads: int
    plane: int
    bits: int
    parts: int
    total: int
    rows: int
    ext: int
    buckets: int
    feats: int
    width: int
    hid: int


def sizes_of(seq, stream, query_weight, expand_weight):
    tok, feats = stream.shape
    width = query_weight.shape[2]
    heads = width // DH
    plane = seq // heads
    parts = plane // ROUNDS
    total = seq * tok
    rows = total // parts
    return Sizes(
        seq,
        tok,
        heads,
        plane,
        plane.bit_length() - 1,
        parts,
        total,
        rows,
        rows + CHUNK,
        total // SPAN,
        feats,
        width,
        expand_weight.shape[2],
    )


def dot(left, right):
    return lax.dot_general(left, right, (((1,), (0,)), ((), ())), preferred_element_type=F32)


def dot_nt(left, right):
    return lax.dot_general(left, right, (((1,), (1,)), ((), ())), preferred_element_type=F32)


def dot_tn(left, right):
    return lax.dot_general(left, right, (((0,), (0,)), ((), ())), preferred_element_type=F32)


def norm_parts(values):
    center = values - jnp.mean(values, axis=-1, keepdims=True)
    scale = lax.rsqrt(jnp.mean(center * center, axis=-1, keepdims=True) + 1e-05)
    return center * scale, scale


def norm_back(xhat, scale, gain, grad):
    t = grad * gain
    inner = t - jnp.mean(t, axis=-1, keepdims=True) - xhat * jnp.mean(t * xhat, axis=-1, keepdims=True)
    return scale * inner


def key_scale(keys):
    return lax.rsqrt(jnp.mean(keys * keys, axis=-1, keepdims=True) + 1e-06)


def rows_to_columns(rows):
    return jnp.transpose(jnp.broadcast_to(rows, (LANES, rows.shape[1])))


def split_three(values):
    high = values.astype(BF16).astype(F32)
    rest = values - high
    middle = rest.astype(BF16).astype(F32)
    return high, middle, rest - middle


class Place:
    def __init__(self, cfg):
        self.cfg = cfg
        self.index = lax.axis_index("seq")
        self.half = lax.axis_index("mp")
        self.head = self.index // cfg.plane
        self.member = self.index % cfg.plane
        self.round = self.member // cfg.parts
        self.part = self.member % cfg.parts

    def bit(self, k):
        return (self.member // 2**k) % 2

    def z_peer(self, step):
        head = (self.head + step) % self.cfg.heads
        return head, (head * self.cfg.plane + self.member, self.half)

    def z_source(self, step):
        return (self.head + self.cfg.heads - step) % self.cfg.heads

    def bit_peer(self, k):
        return (self.index + (1 - 2 * self.bit(k)) * 2**k, self.half)

    def y_peer(self):
        return (self.index, 1 - self.half)

    def kept(self, k, i):
        return 2 ** (k + 1) * i + self.member % 2 ** (k + 1)

    def given(self, k, i):
        return 2 ** (k + 1) * i + (1 - self.bit(k)) * 2**k + self.member % 2**k

    def landing(self, k, spot):
        return self.cfg.plane - self.cfg.plane // 2**k + spot // 2 ** (k + 1)

    def group(self, k):
        return self.cfg.plane // 2 ** (k + 1)

    def plane_peer(self, step):
        member = (self.member + step) % self.cfg.plane
        return member, (self.head * self.cfg.plane + member, self.half)

    def greet(self):
        barrier = pltpu.get_barrier_semaphore()
        peers = [self.z_peer(step)[1] for step in range(1, self.cfg.heads)]
        peers += [self.plane_peer(step)[1] for step in range(1, self.cfg.plane)]
        peers += [self.y_peer()]
        for peer in peers:
            pl.semaphore_signal(barrier, inc=1, device_id=peer, device_id_type=MESH)
        pl.semaphore_wait(barrier, len(peers))


def remote(src, dst, send, recv, peer):
    return pltpu.make_async_remote_copy(
        src_ref=src, dst_ref=dst, send_sem=send, recv_sem=recv, device_id=peer, device_id_type=MESH
    )


def rank_rows(cfg, bucket_row, rank_ref):
    count = cfg.buckets
    ids = lax.broadcasted_iota(jnp.int32, (count, LANES), 0)
    ahead = (
        lax.broadcasted_iota(jnp.int32, (LANES, LANES), 0)
        < lax.broadcasted_iota(jnp.int32, (LANES, LANES), 1)
    ).astype(BF16)
    lower = (
        lax.broadcasted_iota(jnp.int32, (count, count), 1)
        < lax.broadcasted_iota(jnp.int32, (count, count), 0)
    ).astype(BF16)
    marks = [
        (bucket_row[:, p * LANES : (p + 1) * LANES] == ids).astype(F32) for p in range(cfg.seq)
    ]
    totals = sum(marks)
    totals = jnp.broadcast_to(jnp.sum(totals, axis=1, keepdims=True), (count, LANES))
    carry = dot(lower, totals.astype(BF16))
    for p in range(cfg.seq):
        within = dot(marks[p].astype(BF16), ahead)
        rank = jnp.sum(marks[p] * (within + carry), axis=0, keepdims=True)
        carry = carry + jnp.broadcast_to(jnp.sum(marks[p], axis=1, keepdims=True), (count, LANES))
        spot = (p % cfg.plane) * cfg.heads + p // cfg.plane
        rank_ref[:, spot * LANES : (spot + 1) * LANES] = jnp.broadcast_to(
            rank.astype(jnp.int32), (8, LANES)
        )


def sort_rows(cfg, rank_ref, source_ref, store, start, size, chunks):
    step = min(cfg.total, 2048)

    def body(c, _):
        spots = start + c * size + lax.broadcasted_iota(jnp.int32, (size, step), 0)
        spots = spots % cfg.total if cfg.parts > 1 else spots
        found = None
        for k in range(cfg.total // step):
            ranks = rank_ref[0:1, k * step : (k + 1) * step]
            pick = (spots == ranks).astype(BF16)
            part = dot(pick, source_ref[k * step : (k + 1) * step, :])
            found = part if found is None else found + part
        store(c, found)
        return 0

    lax.fori_loop(0, chunks, body, 0)


def several(step, count):
    def body(c, _):
        for i in range(UNROLL):
            step(c * UNROLL + i)
        return 0

    lax.fori_loop(0, count // UNROLL, body, 0)


def window_mask():
    row = lax.broadcasted_iota(jnp.int32, (CHUNK, 2 * CHUNK), 0)
    column = lax.broadcasted_iota(jnp.int32, (CHUNK, 2 * CHUNK), 1)
    gap = column // SPAN - row // SPAN
    near = jnp.logical_or(gap == 1, gap == 2)
    return jnp.logical_and(near, column != row + CHUNK)


def z_exchange(cfg, place, source, target, send, recv):
    copies = []
    for step in range(1, cfg.heads):
        head, peer = place.z_peer(step)
        copy = remote(source(head), target(place.head), send.at[step], recv.at[step], peer)
        copy.start()
        copies.append(copy)
    return copies


def z_arrival(place, block, recv, step):
    return remote(block, block, recv.at[step], recv.at[step], place.z_peer(step)[1])


class Doubling:
    def __init__(self, place, keys, block, send, recv):
        self.place, self.keys, self.block = place, keys, block
        self.send, self.recv = send, recv

    def give(self, key, spot, k):
        return remote(
            self.block(key, spot),
            self.block(key, spot),
            self.send.at[k, key, spot],
            self.recv.at[key, spot],
            self.place.bit_peer(k),
        )

    def offer(self, key):
        for k in range(self.place.cfg.bits):
            self.give(key, self.place.member, k).start()

    def spots(self):
        for k in reversed(range(self.place.cfg.bits)):
            for key in self.keys:
                for i in range(self.place.group(k)):
                    yield k, key, self.place.given(k, i)

    def receive_bit(self, k):
        for key in self.keys:
            for i in range(self.place.group(k)):
                spot = self.place.given(k, i)
                self.give(key, spot, k).wait_recv()
                for low in range(k):
                    self.give(key, spot, low).start()

    def receive(self):
        for k in reversed(range(self.place.cfg.bits)):
            self.receive_bit(k)

    def finish(self):
        for key in self.keys:
            for k in range(self.place.cfg.bits):
                self.give(key, self.place.member, k).wait_send()
        for k, key, spot in self.spots():
            for low in range(k):
                self.give(key, spot, low).wait_send()


class Params(NamedTuple):
    wq_hbm: jax.Array
    wv_hbm: jax.Array
    wm_hbm: jax.Array
    mix_bias: jax.Array
    we_hbm: jax.Array
    expand_bias: jax.Array
    ws_hbm: jax.Array
    shrink_bias: jax.Array
    attention_gain: jax.Array
    attention_shift: jax.Array
    forward_gain: jax.Array
    forward_shift: jax.Array


class Streams(NamedTuple):
    first: jax.Array
    second: jax.Array
    buckets: jax.Array


class Kept(NamedTuple):
    mixed: jax.Array
    sorted: jax.Array
    comb: jax.Array
    joint: jax.Array
    slope: jax.Array
    rank: jax.Array
    lhs_qv: jax.Array
    lhs_expand: jax.Array
    lhs_shrink: jax.Array
    lhs_mix: jax.Array
    second: jax.Array


class Grads(NamedTuple):
    first_out: jax.Array
    second_out: jax.Array
    out_wq: jax.Array
    out_wv: jax.Array
    out_wm: jax.Array
    out_we: jax.Array
    out_ws: jax.Array
    out_small: jax.Array


def gathered(*groups, **scratch):
    merged = {}
    for group in groups:
        merged.update(group._asdict())
    return SimpleNamespace(**merged, **scratch)


def common_scratch(cfg):
    dma = pltpu.SemaphoreType.DMA
    return dict(
        wq=pltpu.VMEM((cfg.feats, cfg.width), BF16),
        wv=pltpu.VMEM((cfg.feats, cfg.width), BF16),
        wm=pltpu.VMEM((cfg.width, cfg.feats), BF16),
        we=pltpu.VMEM((cfg.feats, cfg.hid), BF16),
        ws=pltpu.VMEM((cfg.hid, cfg.feats), BF16),
        ys=pltpu.VMEM((2, cfg.tok, cfg.feats), BF16),
        yr=pltpu.VMEM((2, cfg.tok, cfg.feats), BF16),
        wsem=dma((5,)),
        ysend=dma((2,)),
        yrecv=dma((2,)),
    )


class Weights:
    def __init__(self, r, layers):
        self.pairs = (
            (r.wq_hbm, r.wq),
            (r.wv_hbm, r.wv),
            (r.wm_hbm, r.wm),
            (r.we_hbm, r.we),
            (r.ws_hbm, r.ws),
        )
        self.sem, self.layers = r.wsem, layers
        self.turn, self.flying = [0] * 5, [False] * 5

    def copy(self, i):
        source, target = self.pairs[i]
        return pltpu.make_async_copy(source.at[self.layers[self.turn[i]]], target, self.sem.at[i])

    def fetch(self, *numbers):
        for i in numbers:
            self.copy(i).start()
            self.flying[i] = True

    def need(self, *numbers):
        for i in numbers:
            if self.flying[i]:
                self.copy(i).wait()
                self.flying[i] = False

    def release(self, *numbers):
        for i in numbers:
            if self.turn[i] + 1 < len(self.layers):
                self.turn[i] += 1
                self.fetch(i)


def forward_scratch(cfg):
    tok, heads, plane, bits = cfg.tok, cfg.heads, cfg.plane, cfg.bits
    band = heads * tok
    return dict(
        zs=pltpu.VMEM((heads, tok, 2 * DH), BF16),
        tokens=pltpu.VMEM((cfg.total, 2 * DH), BF16),
        keys=pltpu.VMEM((cfg.ext, DH), BF16),
        attended=pltpu.VMEM((cfg.rows, 3 * DH), BF16),
        part=pltpu.VMEM((plane, band, DH), F32),
        lrow=pltpu.VMEM((plane, 8, band), F32),
        part_in=pltpu.VMEM((plane, band, DH), F32),
        lrow_in=pltpu.VMEM((plane, 8, band), F32),
        low_out=pltpu.VMEM((heads, tok, DH), BF16),
        low_in=pltpu.VMEM((heads, tok, DH), BF16),
        normed_t=pltpu.VMEM((cfg.feats, tok), BF16),
        turned_expand=turned_of(cfg, cfg.feats),
        turned_shrink=turned_of(cfg, cfg.hid),
        turned_mix=turned_of(cfg, cfg.width),
    )


def forward_sems(cfg, layers):
    heads, plane, bits = cfg.heads, cfg.plane, cfg.bits
    shapes = dict(
        zsend=(heads,),
        zrecv=(heads,),
        gsend=(bits, heads, plane),
        grecv=(heads, plane),
        psend=(bits, plane, 2),
        precv=(bits, plane, 2),
        csend=(heads,),
        crecv=(heads,),
        nsend=(heads,),
        nrecv=(heads,),
        tsend=(4, plane),
        trecv=(4, plane),
    )
    return {name: pltpu.SemaphoreType.DMA((layers,) + shape) for name, shape in shapes.items()}


class Turned:
    def __init__(self, place, number, values, source, target, r):
        self.place, self.source, self.target = place, source, target
        self.send, self.recv = r.tsend.at[number], r.trecv.at[number]
        source[...] = jnp.transpose(values).reshape(source.shape).astype(source.dtype)

    def slot(self, member):
        tok = self.place.cfg.tok
        return self.target.at[:, :, pl.ds(pl.multiple_of(member * tok, tok), tok)]

    def copy(self, step):
        member, peer = self.place.plane_peer(step)
        return remote(
            self.source.at[:, member], self.slot(self.place.member), self.send.at[step], self.recv.at[step], peer
        )

    def start(self):
        for step in range(1, self.place.cfg.plane):
            self.copy(step).start()
        self.slot(self.place.member)[...] = self.source[:, self.place.member]

    def finish(self):
        cfg = self.place.cfg
        for step in range(1, cfg.plane):
            self.copy(step).wait_send()
            arrived = self.slot((self.place.member + cfg.plane - step) % cfg.plane)
            remote(arrived, arrived, self.send.at[step], self.recv.at[step], self.place.y_peer()).wait_recv()


def y_sum(place, r, slot, partial, meanwhile=None, first=()):
    r.ys[slot] = partial.astype(BF16)
    copy = remote(r.ys.at[slot], r.yr.at[slot], r.ysend.at[slot], r.yrecv.at[slot], place.y_peer())
    copy.start()
    for step in first:
        step()
    if meanwhile is not None:
        meanwhile()
    copy.wait()
    return r.ys[slot].astype(F32) + r.yr[slot].astype(F32)


def forward_kernel(cfg, layer, names, sems, *refs):
    inputs, refs = refs[:IN_COUNT], refs[IN_COUNT:]
    streams, params = Streams(*inputs[:3]), Params(*inputs[3:])
    out, refs = Kept(*refs[: len(Kept._fields)]), refs[len(Kept._fields) :]
    r = gathered(out, streams, params, **dict(zip(names, refs)))
    vars(r).update({name: ref.at[0] for name, ref in zip(sems, refs[len(names) :])})
    r.second, r.renewed = streams.second, out.second
    weights = Weights(r, [layer])
    weights.fetch(*range(5))
    forward_layer(cfg, Place(cfg), layer, r, weights, True)


def forward_layer(cfg, place, layer, r, weights, first):
    tok, heads = cfg.tok, cfg.heads
    band = heads * tok
    one = slice(layer, layer + 1)
    normed = norm_parts(r.second[...])[0] * r.attention_gain[one, :] + r.attention_shift[one, :]
    normed = normed.astype(BF16)
    weights.need(0, 1)
    queries = dot(normed, r.wq[...]).astype(BF16)
    values = dot(normed, r.wv[...]).astype(BF16)
    if first:
        weights.release(0, 1)
    for head in range(heads):
        r.zs[head, :, :DH] = queries[:, head * DH : (head + 1) * DH]
        r.zs[head, :, DH:] = values[:, head * DH : (head + 1) * DH]

    def block(head, spot):
        return r.tokens.at[pl.ds(pl.multiple_of((spot * heads + head) * tok, tok), tok), :]

    if first:
        place.greet()
    sent = z_exchange(
        cfg,
        place,
        lambda head: r.zs.at[head],
        lambda head: block(head, place.member),
        r.zsend,
        r.zrecv,
    )
    block(place.head, place.member)[...] = r.zs[place.head]
    r.normed_t[...] = jnp.transpose(normed)

    def column(head):
        return r.lhs_qv.at[:, pl.ds(pl.multiple_of(head * tok, tok), tok)]

    column(place.head)[...] = r.normed_t[...]
    rank_rows(cfg, r.buckets[layer, place.round, pl.ds(place.head, 1), :], r.rank)

    spread = Doubling(
        place, [place.z_source(step) for step in range(heads)], block, r.gsend, r.grecv
    )
    for step in range(heads):
        if step > 0:
            z_arrival(place, block(place.z_source(step), place.member), r.zrecv, step).wait_recv()
        spread.offer(place.z_source(step))
    spread.receive()
    sent += z_exchange(cfg, place, lambda head: r.normed_t, column, r.nsend, r.nrecv)
    base = place.part * cfg.rows

    def store_rows(c, found):
        r.sorted[pl.ds(pl.multiple_of(CHUNK + c * 512, CHUNK), 512), :] = found.astype(BF16)

    def store_halo(c, found):
        r.sorted[0:CHUNK, :] = found.astype(BF16)

    sort_rows(cfg, r.rank, r.tokens, store_rows, base, 512, cfg.rows // 512)
    if cfg.parts == 1:
        r.sorted[0:CHUNK, :] = r.sorted[cfg.rows : cfg.ext, :]
    else:
        sort_rows(cfg, r.rank, r.tokens, store_halo, base + cfg.total - CHUNK, CHUNK, 1)
    raw = r.sorted[:, :DH].astype(F32)
    r.keys[...] = (raw * key_scale(raw)).astype(BF16)
    mask = window_mask()
    lane = lax.broadcasted_iota(jnp.int32, (CHUNK, LANES), 1)

    def attend(c):
        at = pl.multiple_of(c * CHUNK, CHUNK)
        query = r.sorted[pl.ds(at + CHUNK, CHUNK), :DH]
        scores = dot_nt(query, r.keys[pl.ds(at, 2 * CHUNK), :]) / math.sqrt(DH)
        scores = jnp.where(mask, scores, -1000000000.0)
        peak = jnp.max(scores, axis=-1, keepdims=True)
        powers = jnp.exp(scores - peak)
        summed = jnp.sum(powers, axis=-1, keepdims=True)
        weights = (powers / summed).astype(BF16)
        output = dot(weights, r.sorted[pl.ds(at, 2 * CHUNK), DH:])
        high, middle, low = split_three(peak + jnp.log(summed))
        extra = jnp.where(lane == 0, high, 0.0)
        extra = jnp.where(lane == 1, middle, extra)
        extra = jnp.where(lane == 2, low, extra)
        extra = jnp.where(lane == 3, 1.0, extra)
        r.attended[pl.ds(at, CHUNK), :DH] = output.astype(BF16)
        r.attended[pl.ds(at, CHUNK), DH : 2 * DH] = (
            output - output.astype(BF16).astype(F32)
        ).astype(BF16)
        r.attended[pl.ds(at, CHUNK), 2 * DH :] = extra.astype(BF16)

    several(attend, cfg.rows // CHUNK)

    def unsort(spot):
        pick = unsort_pick(cfg, r.rank, spot, base, cfg.rows)
        found = dot(pick, r.attended[:, : 2 * DH])
        r.part[spot] = found[:, :DH] + found[:, DH:]
        extra = jnp.transpose(dot(pick, r.attended[:, 2 * DH :]))
        row = extra[0:1] + extra[1:2] + extra[2:3] + (1.0 - extra[3:4]) * AWAY
        r.lrow[spot] = jnp.broadcast_to(row, (8, band))

    def pass_part(k, spot):
        peer = place.bit_peer(k)
        return [
            remote(
                mine.at[spot],
                theirs.at[place.landing(k, spot)],
                r.psend.at[k, spot, i],
                r.precv.at[k, spot, i],
                peer,
            )
            for i, (mine, theirs) in enumerate(((r.part, r.part_in), (r.lrow, r.lrow_in)))
        ]

    def first_half(i, _):
        unsort(place.given(0, i))
        for copy in pass_part(0, place.given(0, i)):
            copy.start()
        return 0

    def second_half(i, _):
        unsort(place.kept(0, i))
        return 0

    lax.fori_loop(0, place.group(0), first_half, 0)
    lax.fori_loop(0, place.group(0), second_half, 0)

    def merge(k, spot):
        for copy in pass_part(k, spot):
            copy.wait_recv()
        mine = rows_to_columns(r.lrow[spot][0:1])
        landed = place.landing(k, spot)
        other = rows_to_columns(r.lrow_in[landed][0:1])
        highest = jnp.maximum(mine, other)
        share = jnp.exp(mine - highest)
        share_in = jnp.exp(other - highest)
        both = share + share_in
        merged = (r.part[spot].astype(F32) * share + r.part_in[landed].astype(F32) * share_in) / both
        return merged, jnp.transpose(highest + jnp.log(both))[0:8]

    for k in range(cfg.bits - 1):
        for giving in (True, False):
            for i in range(place.group(k + 1)):
                spot = place.given(k + 1, i) if giving else place.kept(k + 1, i)
                merged, joint = merge(k, spot)
                r.part[spot] = merged
                r.lrow[spot] = joint
                if giving:
                    for copy in pass_part(k + 1, spot):
                        copy.start()
    merged, joint = merge(cfg.bits - 1, place.member)
    r.comb[...] = merged
    r.joint[...] = joint
    spread.finish()
    for head in range(heads):
        r.low_out[head] = merged[head * tok : (head + 1) * tok].astype(BF16)
    back = z_exchange(
        cfg, place, lambda head: r.low_out.at[head], lambda head: r.low_in.at[head], r.csend, r.crecv
    )
    r.low_in[place.head] = r.low_out[place.head]
    weights.need(2)
    for step in range(1, heads):
        z_arrival(place, r.low_in.at[place.z_source(step)], r.crecv, step).wait_recv()
    low = jnp.concatenate([r.low_in[head] for head in range(heads)], axis=1)

    turned_mix = Turned(place, 3, low, r.turned_mix, r.lhs_mix, r)

    def finish_sends():
        for copy in sent + back:
            copy.wait_send()
        for k in range(cfg.bits):
            for i in range(place.group(k)):
                for copy in pass_part(k, place.given(k, i)):
                    copy.wait_send()
        turned_mix.start()

    partial = dot(low, r.wm[...])
    if first:
        weights.release(2)
    mixed = r.first[...] + y_sum(place, r, 0, partial, finish_sends) + r.mix_bias[one, :]
    r.mixed[...] = mixed
    normed_two = norm_parts(mixed)[0] * r.forward_gain[one, :] + r.forward_shift[one, :]
    normed_two = normed_two.astype(BF16)
    weights.need(3)
    hidden = dot(normed_two, r.we[...]) + r.expand_bias[one, :]
    curve = 0.5 * (1.0 + lax.erf(hidden * math.sqrt(0.5)))
    active = (hidden * curve).astype(BF16)
    weights.need(4)

    def turn():
        turned_shrink = Turned(place, 2, active, r.turned_shrink, r.lhs_shrink, r)
        turned_shrink.start()
        turned_expand = Turned(place, 1, normed_two, r.turned_expand, r.lhs_expand, r)
        turned_expand.start()
        bell = jnp.exp(-0.5 * hidden * hidden) * (1.0 / math.sqrt(2.0 * math.pi))
        r.slope[...] = curve + hidden * bell
        for turned in (turned_mix, turned_shrink, turned_expand):
            turned.finish()
        for step in range(1, heads):
            z_arrival(place, column(place.z_source(step)), r.nrecv, step).wait_recv()

    partial = dot(active, r.ws[...])
    if first:
        weights.release(3, 4)
    r.renewed[...] = r.second[...] + y_sum(place, r, 1, partial, turn) + r.shrink_bias[one, :]


def unsort_pick(cfg, rank_ref, spot, base, rows):
    band = cfg.heads * cfg.tok
    ranks = rank_ref[0:1, pl.ds(pl.multiple_of(spot * band, band), band)]
    ranks = rows_to_columns(ranks.astype(F32)).astype(jnp.int32)[:, 0:1]
    places = base + lax.broadcasted_iota(jnp.int32, (band, rows), 1)
    if cfg.parts > 1:
        places = places % cfg.total
    return (ranks == places).astype(BF16)


IN_COUNT = len(Streams._fields) + len(Params._fields)


def forward_call(cfg, layer, streams, params):
    scratch = common_scratch(cfg) | forward_scratch(cfg)
    sems = forward_sems(cfg, 1)
    whole = pl.BlockSpec(memory_space=pltpu.VMEM)
    apart = pl.BlockSpec(memory_space=pl.ANY)
    specs = Params(*[whole] * len(params))._replace(
        wq_hbm=apart, wv_hbm=apart, wm_hbm=apart, we_hbm=apart, ws_hbm=apart
    )
    outs = pl.pallas_call(
        functools.partial(forward_kernel, cfg, layer, list(scratch), list(sems)),
        out_shape=[jax.ShapeDtypeStruct(*shape) for shape in saved_shapes(cfg)],
        in_specs=[whole] * len(streams) + list(specs),
        out_specs=[whole] * len(Kept._fields),
        scratch_shapes=list(scratch.values()) + list(sems.values()),
        compiler_params=pltpu.CompilerParams(
            collective_id=layer, has_side_effects=True, vmem_limit_bytes=VMEM_LIMIT
        ),
        name=f"forward_{layer}",
    )(*streams, *params)
    return Kept(*outs)


def lines_of(cfg, extent):
    deep = extent // cfg.seq
    return (cfg.heads, deep, cfg.plane * cfg.tok), BF16 if deep % 16 == 0 else F32


def turned_of(cfg, extent):
    (heads, deep, _), kind = lines_of(cfg, extent)
    return pltpu.VMEM((heads, cfg.plane, deep, cfg.tok), kind)


def saved_shapes(cfg):
    tok, feats, band = cfg.tok, cfg.feats, cfg.heads * cfg.tok
    return Kept(
        second=((tok, feats), F32),
        mixed=((tok, feats), F32),
        sorted=((cfg.ext, 2 * DH), BF16),
        comb=((band, DH), F32),
        joint=((8, band), F32),
        slope=((tok, cfg.hid), F32),
        rank=((8, cfg.total), jnp.int32),
        lhs_qv=((feats, band), BF16),
        lhs_expand=lines_of(cfg, feats),
        lhs_shrink=lines_of(cfg, cfg.hid),
        lhs_mix=lines_of(cfg, cfg.width),
    )


class Job(NamedTuple):
    name: str
    side: str
    number: int
    rows: int
    columns: int
    fold: int

    def scratch(self, cfg):
        deep, wide = self.rows * self.fold, self.columns // self.fold
        return {
            "rhs" + self.side: pltpu.VMEM((cfg.plane * cfg.tok, self.columns), BF16),
            "prod" + self.name: pltpu.VMEM((cfg.heads, deep, wide), BF16),
            "zin" + self.name: pltpu.VMEM((3, deep, wide), BF16),
        }


def slots_of(cfg):
    return LAYERS if cfg.parts == 1 else 1


def jobs_of(cfg):
    share = cfg.feats // cfg.seq
    mix = cfg.width // cfg.seq
    return (
        Job("s", "s", 0, cfg.hid // cfg.seq, cfg.feats, 1),
        Job("m", "m", 1, mix, cfg.feats, 1 if mix % 16 == 0 else 2),
    ) + tuple(
        Job(f"e{i}", f"e{i}", 2 + i, share, cfg.feats, 1) for i in range(cfg.hid // cfg.feats)
    )


def backward_scratch(cfg):
    tok, heads, plane, bits = cfg.tok, cfg.heads, cfg.plane, cfg.bits
    band = heads * tok
    dma = pltpu.SemaphoreType.DMA
    return dict(
        gs=pltpu.VMEM((heads, tok, DH), BF16),
        gtokens=pltpu.VMEM((cfg.total, 2 * DH), BF16),
        arow=pltpu.VMEM((LAYERS, plane, 8, band), F32),
        gsorted=pltpu.VMEM((cfg.rows, DH), BF16),
        stats=pltpu.VMEM((cfg.rows, LANES), F32),
        keys=pltpu.VMEM((cfg.ext, DH), BF16),
        dq=pltpu.VMEM((cfg.ext, DH), F32),
        dk=pltpu.VMEM((cfg.ext, DH), F32),
        dv=pltpu.VMEM((cfg.ext, DH), F32),
        grads=pltpu.VMEM((cfg.ext, 2 * DH), BF16),
        part=pltpu.VMEM((plane, band, 2 * DH), BF16),
        part_in=pltpu.VMEM((plane, band, 2 * DH), BF16),
        home_out=pltpu.VMEM((heads, tok, 2 * DH), BF16),
        home_in=pltpu.VMEM((heads, tok, 2 * DH), BF16),
        vectors=pltpu.VMEM((8, cfg.feats), F32),
        vys=pltpu.VMEM((8, cfg.feats), F32),
        vyr=pltpu.VMEM((8, cfg.feats), F32),
        vysem=dma((2,)),
        **{key: value for job in jobs_of(cfg) for key, value in job.scratch(cfg).items()},
        vbuf=pltpu.VMEM((LAYERS, plane, heads, 8, LANES), F32),
        vin=pltpu.VMEM((LAYERS, plane, heads, 8, LANES), F32),
        vz=pltpu.VMEM((LAYERS, heads, 8, LANES), F32),
        lsem=dma((LAYERS, len(Kept._fields))),
        zsend=dma((LAYERS, heads)),
        zrecv=dma((LAYERS, heads)),
        gsend=dma((LAYERS, bits, heads, plane)),
        grecv=dma((LAYERS, heads, plane)),
        asend=dma((LAYERS, bits, 1, plane)),
        arecv=dma((LAYERS, 1, plane)),
        psend=dma((LAYERS, bits, plane)),
        precv=dma((LAYERS, bits, plane)),
        csend=dma((LAYERS, heads)),
        crecv=dma((LAYERS, heads)),
        rsend=dma((len(jobs_of(cfg)), bits, 1, plane)),
        rrecv=dma((len(jobs_of(cfg)), 1, plane)),
        usend=dma((len(jobs_of(cfg)), 3)),
        urecv=dma((len(jobs_of(cfg)), 3)),
        qbuf=pltpu.VMEM((plane, heads, cfg.feats // cfg.seq, 2 * DH), BF16),
        qin=pltpu.VMEM((plane, heads, cfg.feats // cfg.seq, 2 * DH), BF16),
        qz=pltpu.VMEM((heads, cfg.feats // cfg.seq, 2 * DH), BF16),
        qsend=dma((bits + heads,)),
        qrecv=dma((bits + heads,)),
        vsend=dma((LAYERS, bits + heads)),
        vrecv=dma((LAYERS, bits + heads)),
    )


class Unit:
    def __init__(self, place, fill, done, buf, arrive, zbuf, send, recv):
        self.place, self.fill, self.done = place, fill, done
        self.buf, self.arrive, self.zbuf, self.send, self.recv = buf, arrive, zbuf, send, recv

    def halved(self, k):
        place, plane = self.place, self.place.cfg.plane
        group = place.group(k)
        start = plane - plane // 2**k
        shape = (group, 2 ** (k + 1)) + self.buf.shape[1:]
        spot = (1 - place.bit(k)) * 2**k + place.member % 2**k
        return remote(
            self.buf.reshape(*shape).at[:, spot],
            self.arrive.at[start : start + group],
            self.send.at[k],
            self.recv.at[k],
            place.bit_peer(k),
        )

    def across(self, step):
        place = self.place
        head, peer = place.z_peer(step)
        at = place.cfg.bits + step
        return remote(
            self.buf.at[place.member, head], self.zbuf.at[step], self.send.at[at], self.recv.at[at], peer
        )

    def start(self):
        self.fill(self.buf)
        self.halved(0).start()

    def fold(self):
        place, cfg = self.place, self.place.cfg
        for k in range(cfg.bits):
            self.halved(k).wait_recv()
            start = cfg.plane - cfg.plane // 2**k
            for i in range(place.group(k)):
                spot = place.kept(k, i)
                both = self.buf[spot].astype(F32) + self.arrive[start + i].astype(F32)
                self.buf[spot] = both.astype(self.buf.dtype)
            if k + 1 < cfg.bits:
                self.halved(k + 1).start()
            if k + 2 == cfg.bits:
                yield
        for step in range(1, cfg.heads):
            self.across(step).start()
        yield
        found = [(place.head, self.buf[place.member, place.head])]
        for step in range(1, cfg.heads):
            self.across(step).wait_recv()
            found.append((place.z_source(step), self.zbuf[step]))
        self.done(found)
        for k in range(cfg.bits):
            self.halved(k).wait_send()
        for step in range(1, cfg.heads):
            self.across(step).wait_send()
        yield


class Gathered:
    def __init__(self, place, job, left, right, done, r):
        self.place, self.job, self.left, self.right, self.done = place, job, left, right, done
        tok = place.cfg.tok
        self.rhs = vars(r)["rhs" + job.side]
        self.prod, self.zin = vars(r)["prod" + job.name], vars(r)["zin" + job.name]
        self.send, self.recv = r.usend.at[job.number], r.urecv.at[job.number]
        self.spread = Doubling(
            place,
            [0],
            lambda key, spot: self.rhs.at[pl.ds(pl.multiple_of(spot * tok, tok), tok), :],
            r.rsend.at[job.number],
            r.rrecv.at[job.number],
        )
        head = place.head
        self.inner = (head * (3 - head)) // 2
        self.near = head + 1 - 2 * (head % 2)
        self.far = 3 - 3 * (head // 2)

    def copy(self, number):
        place, inner = self.place, self.inner
        if number == 0:
            dest, block, slot = self.near, self.near, 0
        elif number == 1:
            dest, block, slot = self.far, self.far, 2 - inner
        else:
            other = 3 - place.head
            dest = self.near * (1 - inner) + other * inner
            block = (3 - self.near) * (1 - inner) + other * inner
            slot = 2 - inner
        return remote(
            self.prod.at[block],
            self.zin.at[slot],
            self.send.at[number],
            self.recv.at[slot],
            (dest * place.cfg.plane + place.member, place.half),
        )

    def arrival(self, slot):
        spot = self.zin.at[slot]
        return remote(spot, spot, self.send.at[slot], self.recv.at[slot], self.place.y_peer())

    def start(self):
        self.spread.block(0, self.place.member)[...] = self.right
        self.spread.offer(0)

    def forward(self):
        for k in reversed(range(1, self.place.cfg.bits)):
            self.spread.receive_bit(k)

    def multiply(self):
        cfg, job = self.place.cfg, self.job
        self.spread.receive_bit(0)
        lines = self.left[...].reshape(cfg.heads * job.rows, cfg.plane * cfg.tok).astype(BF16)
        wide = job.columns // job.fold
        found = [
            dot(lines, self.rhs[:, i * wide : (i + 1) * wide]).reshape(cfg.heads, job.rows, wide)
            for i in range(job.fold)
        ]
        found = found[0] if job.fold == 1 else jnp.concatenate(found, axis=1)
        self.prod[...] = found.astype(BF16)

        @pl.when(self.inner == 0)
        def _():
            self.copy(2).start()

        self.copy(1).start()
        self.copy(0).start()
        self.spread.finish()

    def relay(self):
        @pl.when(self.inner == 1)
        def _():
            self.arrival(2).wait_recv()
            block = 3 - self.place.head
            both = self.prod[block].astype(F32) + self.zin[2].astype(F32)
            self.prod[block] = both.astype(BF16)
            self.copy(2).start()

    def finish(self):
        self.arrival(0).wait_recv()
        self.arrival(1).wait_recv()

        @pl.when(self.inner == 0)
        def _():
            self.arrival(2).wait_recv()

        total = self.prod[self.place.head].astype(F32)
        total = total + self.zin[0].astype(F32) + self.zin[1].astype(F32)
        total = jnp.where(self.inner == 0, total + self.zin[2].astype(F32), total)
        wide, deep = self.job.columns // self.job.fold, self.job.rows
        for i in range(self.job.fold):
            self.done(total[i * deep : (i + 1) * deep], i * wide, wide)
        for number in range(3):
            self.copy(number).wait_send()


def backward_kernel(cfg, names, *refs):
    params, refs = Params(*refs[: len(Params._fields)]), refs[len(Params._fields) :]
    (first_cot, second_cot), refs = refs[:2], refs[2:]
    stored, held = [], []
    for _ in range(LAYERS):
        stored.append(Kept(*refs[: len(Kept._fields)]))
        refs = refs[len(Kept._fields) :]
    out, refs = Grads(*refs[: len(Grads._fields)]), refs[len(Grads._fields) :]
    for _ in range(slots_of(cfg)):
        held.append(Kept(*refs[: len(Kept._fields)]))
        refs = refs[len(Kept._fields) :]
    held = held * (LAYERS // len(held))
    r = gathered(params, out, **dict(zip(names, refs, strict=True)))
    weights = Weights(r, list(reversed(range(LAYERS))))
    weights.fetch(4, 3, 2, 0, 1)

    def saved_load(layer, ref):
        i = [ref is other for other in held[layer]].index(True)
        return pltpu.make_async_copy(stored[layer][i], ref, r.lsem.at[layer, i])

    def fetch(layer):
        k = held[layer]
        for ref in (k.slope, k.lhs_shrink, k.mixed, k.lhs_expand, k.comb, k.joint, k.sorted):
            saved_load(layer, ref).start()
        for ref in (k.rank, k.lhs_mix, k.second, k.lhs_qv):
            saved_load(layer, ref).start()

    for layer in list(reversed(range(LAYERS)))[: slots_of(cfg)]:
        fetch(layer)
    place = Place(cfg)
    place.greet()
    after = fetch if slots_of(cfg) == 1 else None
    backward_layers(cfg, place, r, weights, held, saved_load, after, first_cot, second_cot)


def backward_layers(cfg, place, r, weights, held, saved_load, fetch, first_cot, second_cot):
    tok, heads, plane, width = cfg.tok, cfg.heads, cfg.plane, cfg.width
    band = heads * tok
    share = cfg.feats // cfg.seq
    base = place.part * cfg.rows
    jobs = jobs_of(cfg)

    def weight(number, layer, left, right):
        out = (r.out_ws, r.out_wm)[number] if number < 2 else r.out_we
        first = max(number - 2, 0) * cfg.feats

        def done(total, start, wide):
            out[layer, :, first + start : first + start + wide] = total

        return Gathered(place, jobs[number], left, right, done, r)

    def attention_weights(layer, left, right):
        def fill(buf):
            for head in range(heads):
                rows = left[head * plane * share : (head + 1) * plane * share, :]
                buf[:, head] = dot(rows, right).reshape(plane, share, 2 * DH).astype(BF16)

        def done(found):
            for head, both in found:
                at = pl.ds(pl.multiple_of(head * DH, DH), DH)
                r.out_wq[layer, :, at] = both[:, :DH].astype(F32)
                r.out_wv[layer, :, at] = both[:, DH:].astype(F32)

        return Unit(place, fill, done, r.qbuf, r.qin, r.qz, r.qsend, r.qrecv)

    def vector_sums(layer):
        def fill(buf):
            deep = cfg.hid // cfg.seq
            for p in range(cfg.seq):
                at = p * share // LANES * LANES
                tile = r.vectors[:, at : at + LANES]
                at = p * deep // LANES * LANES
                line, at = 6 + at // cfg.feats, at % cfg.feats
                extra = r.vectors[line : line + 1, at : at + LANES]
                buf[p % plane, p // plane, 0:6] = tile[0:6]
                buf[p % plane, p // plane, 6:8] = jnp.broadcast_to(extra, (2, LANES))

        def done(found):
            r.out_small[layer] = sum(both for _, both in found)

        return Unit(
            place, fill, done, r.vbuf.at[layer], r.vin.at[layer], r.vz.at[layer], r.vsend.at[layer], r.vrecv.at[layer]
        )

    order = list(reversed(range(LAYERS)))
    late, small, last = None, None, None

    for layer in order:
        one = slice(layer, layer + 1)
        saved = held[layer]

        def arrived(*fields):
            if saved_load is not None:
                for field in fields:
                    saved_load(layer, field).wait()

        second_grad = second_cot if layer == order[0] else r.second_out
        first_grad = first_cot if layer == order[0] else r.first_out
        branch = second_grad[...].astype(BF16)
        arrived(saved.slope, saved.lhs_shrink)
        shrink = weight(0, layer, saved.lhs_shrink, branch)
        shrink.start()
        weights.need(4)
        hidden_grad = (dot_nt(branch, r.ws[...]) * saved.slope[...]).astype(BF16)
        weights.release(4)
        weights.need(3)
        partial = dot_nt(hidden_grad, r.we[...])
        weights.release(3)
        arrived(saved.mixed, saved.lhs_expand)

        def during_two():
            r.vectors[0:1, :] = jnp.sum(branch.astype(F32), axis=0, keepdims=True)
            summed = jnp.sum(hidden_grad.astype(F32), axis=0, keepdims=True)
            for i in range(cfg.hid // cfg.feats):
                r.vectors[6 + i : 7 + i, :] = summed[:, i * cfg.feats : (i + 1) * cfg.feats]
            if late is not None:
                for job in late:
                    job.relay()
                next(last)
            shrink.forward()

        expand = [
            weight(2 + i, layer, saved.lhs_expand, hidden_grad[:, i * cfg.feats : (i + 1) * cfg.feats])
            for i in range(cfg.hid // cfg.feats)
        ]
        two_grad = y_sum(place, r, 0, partial, during_two, [expand[0].start])
        xhat, scale = norm_parts(saved.mixed[...])
        mixed_grad = first_grad[...] + norm_back(xhat, scale, r.forward_gain[one, :], two_grad)
        r.first_out[...] = mixed_grad
        mix_low = mixed_grad.astype(BF16)
        weights.need(2)
        combined_grad = dot_nt(mix_low, r.wm[...]).astype(BF16)
        weights.release(2)
        for head in range(heads):
            r.gs[head] = combined_grad[:, head * DH : (head + 1) * DH]

        def rows_of(spot, head):
            return pl.ds(pl.multiple_of((spot * heads + head) * tok, tok), tok)

        def block(head, spot):
            return r.gtokens.at[rows_of(spot, head), :DH]

        sent = z_exchange(
            cfg,
            place,
            lambda head: r.gs.at[head],
            lambda head: block(head, place.member),
            r.zsend.at[layer],
            r.zrecv.at[layer],
        )
        block(place.head, place.member)[...] = r.gs[place.head]
        r.vectors[1:2, :] = jnp.sum(mix_low.astype(F32), axis=0, keepdims=True)
        r.vectors[2:3, :] = jnp.sum(two_grad * xhat, axis=0, keepdims=True)
        r.vectors[3:4, :] = jnp.sum(two_grad, axis=0, keepdims=True)
        arrived(saved.sorted, saved.rank, saved.comb, saved.joint, saved.lhs_mix)
        rank = saved.rank
        rows = saved.sorted
        mixing = weight(1, layer, saved.lhs_mix, mix_low)
        raw = rows[:, :DH].astype(F32)
        r.keys[...] = (raw * key_scale(raw)).astype(BF16)
        if late is not None:
            for job in late:
                job.finish()
            next(last)
            next(small)
        spread = Doubling(
            place,
            [place.z_source(step) for step in range(heads)],
            block,
            r.gsend.at[layer],
            r.grecv.at[layer],
        )
        for step in range(heads):
            if step > 0:
                spot = block(place.z_source(step), place.member)
                z_arrival(place, spot, r.zrecv.at[layer], step).wait_recv()
            spread.offer(place.z_source(step))
        mine = r.gtokens[pl.ds(pl.multiple_of(place.member * band, band), band), :DH].astype(F32)
        inner = jnp.sum(jnp.transpose(mine * saved.comb[...]), axis=0, keepdims=True)
        line = lax.broadcasted_iota(jnp.int32, (8, band), 0)
        r.arow[layer, place.member] = jnp.where(
            line == 0, saved.joint[...], jnp.broadcast_to(inner, (8, band))
        )
        extras = Doubling(
            place,
            [0],
            lambda key, spot: r.arow.at[layer, spot],
            r.asend.at[layer],
            r.arecv.at[layer],
        )
        extras.offer(0)
        shrink.multiply()
        spread.receive()
        extras.receive()
        expand[0].forward()
        expand[1].start()
        mixing.start()
        if late is not None:
            next(small)
        lines = lax.broadcasted_iota(jnp.int32, (LANES, band), 0)
        for spot in range(plane):
            pieces = split_three(r.arow[layer, spot][0:1]) + split_three(r.arow[layer, spot][1:2])
            table = jnp.zeros((LANES, band), F32)
            for i, piece in enumerate(pieces):
                table = jnp.where(lines == i, piece, table)
            r.gtokens[spot * band : (spot + 1) * band, DH:] = jnp.transpose(table).astype(BF16)

        def store_rows(c, found):
            at = pl.ds(pl.multiple_of(c * 512, 512), 512)
            r.gsorted[at, :] = found[:, :DH].astype(BF16)
            r.stats[at, :] = found[:, DH:]

        sort_rows(cfg, rank, r.gtokens, store_rows, base, 512, cfg.rows // 512)
        r.dq[0:CHUNK, :] = jnp.zeros((CHUNK, DH), F32)
        r.dk[0:CHUNK, :] = jnp.zeros((CHUNK, DH), F32)
        r.dv[0:CHUNK, :] = jnp.zeros((CHUNK, DH), F32)
        mask = window_mask()

        def attend(c):
            at = pl.multiple_of(c * CHUNK, CHUNK)
            own = pl.ds(at + CHUNK, CHUNK)
            window = pl.ds(at, 2 * CHUNK)
            query = rows[own, :DH]
            near = r.keys[window, :]
            grad = r.gsorted[pl.ds(at, CHUNK), :]
            stats = r.stats[pl.ds(at, CHUNK), :]
            joint = stats[:, 0:1] + stats[:, 1:2] + stats[:, 2:3]
            inner = stats[:, 3:4] + stats[:, 4:5] + stats[:, 5:6]
            scores = dot_nt(query, near) / math.sqrt(DH)
            scores = jnp.where(mask, scores, -1000000000.0)
            probs = jnp.exp(scores - joint)
            prob_grad = dot_nt(grad, rows[window, DH:])
            score_grad = (probs * (prob_grad - inner) / math.sqrt(DH)).astype(BF16)
            r.dq[own, :] = dot(score_grad, near)
            return dot_tn(score_grad, query), dot_tn(probs.astype(BF16), grad)

        def attend_some(i, _):
            parts = [attend(i * UNROLL + u) for u in range(UNROLL)]
            for ref, found in zip((r.dk, r.dv), zip(*parts)):
                for u in range(UNROLL):
                    at = pl.multiple_of((i * UNROLL + u) * CHUNK, CHUNK)
                    if u == 0:
                        before = pl.ds(at, CHUNK)
                        ref[before, :] = ref[before, :] + found[u][:CHUNK]
                    own = found[u][CHUNK:]
                    if u + 1 < UNROLL:
                        own = own + found[u + 1][:CHUNK]
                    ref[pl.ds(at + CHUNK, CHUNK), :] = own
            return 0

        rounds = cfg.rows // CHUNK // UNROLL
        lax.fori_loop(0, rounds // 2, attend_some, 0)
        shrink.relay()
        expand[0].multiply()
        expand[1].forward()
        lax.fori_loop(rounds // 2, rounds, attend_some, 0)
        if cfg.parts == 1:
            last = slice(cfg.rows, cfg.ext)
            r.dk[last, :] = r.dk[last, :] + r.dk[0:CHUNK, :]
            r.dv[last, :] = r.dv[last, :] + r.dv[0:CHUNK, :]
        raw = rows[:, :DH].astype(F32)
        scale = key_scale(raw)
        dk = r.dk[...]
        inner = jnp.mean(raw * dk, axis=-1, keepdims=True)
        r.grads[:, :DH] = (
            r.dq[...] + scale * dk - raw * (scale * scale * scale * inner)
        ).astype(BF16)
        r.grads[:, DH:] = r.dv[...].astype(BF16)
        skip = CHUNK if cfg.parts == 1 else 0

        def unsort(spot):
            start = base if cfg.parts == 1 else base + cfg.total - CHUNK
            pick = unsort_pick(cfg, rank, spot, start, cfg.ext - skip)
            r.part[spot] = dot(pick, r.grads[skip:, :]).astype(BF16)

        def pass_part(k, spot):
            return remote(
                r.part.at[spot],
                r.part_in.at[place.landing(k, spot)],
                r.psend.at[layer, k, spot],
                r.precv.at[layer, k, spot // 2 ** (k + 1)],
                place.bit_peer(k),
            )

        def first_half(i, _):
            unsort(place.given(0, i))
            pass_part(0, place.given(0, i)).start()
            return 0

        def second_half(i, _):
            unsort(place.kept(0, i))
            return 0

        lax.fori_loop(0, place.group(0), first_half, 0)
        lax.fori_loop(0, place.group(0), second_half, 0)

        def merge(k, spot):
            pass_part(k, spot).wait_recv()
            other = r.part_in[place.landing(k, spot)]
            return (r.part[spot].astype(F32) + other.astype(F32)).astype(BF16)

        for k in range(cfg.bits - 1):
            for giving in (True, False):
                for i in range(place.group(k + 1)):
                    spot = place.given(k + 1, i) if giving else place.kept(k + 1, i)
                    r.part[spot] = merge(k, spot)
                    if giving:
                        pass_part(k + 1, spot).start()
        spread.finish()
        extras.finish()
        shrink.finish()
        expand[0].relay()
        mixing.forward()
        merged = merge(cfg.bits - 1, place.member)
        for head in range(heads):
            r.home_out[head] = merged[head * tok : (head + 1) * tok]
        back = z_exchange(
            cfg,
            place,
            lambda head: r.home_out.at[head],
            lambda head: r.home_in.at[head],
            r.csend.at[layer],
            r.crecv.at[layer],
        )
        r.home_in[place.head] = r.home_out[place.head]
        arrived(saved.second, saved.lhs_qv)
        last = attention_weights(layer, saved.lhs_qv, merged)
        last.start()
        last = last.fold()
        weights.need(0, 1)
        xhat, scale = norm_parts(saved.second[...])
        expand[0].finish()
        next(last)
        for step in range(1, heads):
            spot = r.home_in.at[place.z_source(step)]
            z_arrival(place, spot, r.crecv.at[layer], step).wait_recv()
        query_grad = jnp.concatenate([r.home_in[head][:, :DH] for head in range(heads)], axis=1)
        value_grad = jnp.concatenate([r.home_in[head][:, DH:] for head in range(heads)], axis=1)
        one_grad = dot_nt(query_grad, r.wq[...]) + dot_nt(value_grad, r.wv[...])
        weights.release(0, 1)
        r.vys[0:1, :] = jnp.sum(one_grad * xhat, axis=0, keepdims=True)
        r.vys[1:2, :] = jnp.sum(one_grad, axis=0, keepdims=True)
        edge = remote(r.vys, r.vyr, r.vysem.at[0], r.vysem.at[1], place.y_peer())
        edge.start()
        small = vector_sums(layer)

        late = [expand[1], mixing]

        def during_one():
            for copy in sent + back:
                copy.wait_send()
            for k in range(cfg.bits):
                for i in range(place.group(k)):
                    pass_part(k, place.given(k, i)).wait_send()
            edge.wait()
            r.vectors[4:6, :] = r.vys[0:2, :] + r.vyr[0:2, :]
            small.start()

        one_grad = y_sum(place, r, 1, one_grad, during_one, [job.multiply for job in late])
        dx = norm_back(xhat, scale, r.attention_gain[one, :], one_grad)
        r.second_out[...] = second_grad[...] + dx
        small = small.fold()
        next(small)
        if layer > 0 and fetch is not None:
            fetch(layer - 1)
    for job in late:
        job.relay()
    next(last)
    next(small)
    for job in late:
        job.finish()
    next(last)
    next(small)


def grad_shapes(cfg):
    tok, feats = cfg.tok, cfg.feats
    share = feats // cfg.seq
    return Grads(
        first_out=(tok, feats),
        second_out=(tok, feats),
        out_wq=(LAYERS, share, cfg.width),
        out_wv=(LAYERS, share, cfg.width),
        out_wm=(LAYERS, cfg.width // cfg.seq, feats),
        out_we=(LAYERS, share, cfg.hid),
        out_ws=(LAYERS, cfg.hid // cfg.seq, feats),
        out_small=(LAYERS, 8, LANES),
    )


def backward_call(cfg, params, cotangents, saved):
    scratch = common_scratch(cfg) | backward_scratch(cfg)
    shapes = grad_shapes(cfg)
    whole = pl.BlockSpec(memory_space=pltpu.VMEM)
    apart = pl.BlockSpec(memory_space=pl.ANY)
    specs = Params(*[apart] * len(params))._replace(attention_gain=whole, forward_gain=whole)
    held = [pltpu.VMEM(*shape) for shape in saved_shapes(cfg)] * slots_of(cfg)
    outs = pl.pallas_call(
        functools.partial(backward_kernel, cfg, list(scratch)),
        out_shape=[jax.ShapeDtypeStruct(shape, F32) for shape in shapes],
        in_specs=list(specs) + [whole] * 2 + [apart] * (LAYERS * len(Kept._fields)),
        out_specs=[whole] * len(shapes),
        scratch_shapes=held + list(scratch.values()),
        compiler_params=pltpu.CompilerParams(
            collective_id=LAYERS, has_side_effects=True, vmem_limit_bytes=VMEM_LIMIT
        ),
        name="backward",
    )(*params, *cotangents, *[array for kept in saved for array in kept])
    return Grads(*outs)


def whole_kernel(cfg, common, forth, sems, back, *refs):
    inputs, refs = refs[:IN_COUNT], refs[IN_COUNT:]
    streams, params = Streams(*inputs[:3]), Params(*inputs[3:])
    (first_cot, second_cot, result_one, result_two), refs = refs[:4], refs[4:]
    out, refs = Grads(*refs[: len(Grads._fields)]), refs[len(Grads._fields) :]
    held = []
    for _ in range(LAYERS):
        held.append(Kept(*refs[: len(Kept._fields)]))
        refs = refs[len(Kept._fields) :]
    shared, refs = dict(zip(common, refs)), refs[len(common) :]
    ahead, refs = dict(zip(forth, refs)), refs[len(forth) :]
    signals, refs = dict(zip(sems, refs)), refs[len(sems) :]
    place = Place(cfg)
    weights = None
    first, second = streams.first, streams.second
    for layer in range(LAYERS):
        done = layer == LAYERS - 1
        if layer == 0:
            held[0] = held[0]._replace(second=second)
        if done:
            held[layer] = held[layer]._replace(mixed=result_one)
        r = gathered(held[layer], params, **shared, **ahead)
        vars(r).update({name: ref.at[layer] for name, ref in signals.items()})
        r.first, r.buckets = first, streams.buckets
        r.renewed = result_two if done else held[layer + 1].second
        if weights is None:
            weights = Weights(r, [0, 1, 0])
            weights.fetch(*range(5))
        forward_layer(cfg, place, layer, r, weights, layer == 0)
        first, second = r.mixed, r.renewed
    r = gathered(params, out, **shared, **dict(zip(back, refs, strict=True)))
    backward_layers(cfg, place, r, weights, held, None, None, first_cot, second_cot)


def whole_call(cfg, streams, cotangents, params):
    common, forth, back = common_scratch(cfg), forward_scratch(cfg), backward_scratch(cfg)
    sems = forward_sems(cfg, LAYERS)
    whole = pl.BlockSpec(memory_space=pltpu.VMEM)
    apart = pl.BlockSpec(memory_space=pl.ANY)
    specs = Params(*[whole] * len(params))._replace(
        wq_hbm=apart, wv_hbm=apart, wm_hbm=apart, we_hbm=apart, ws_hbm=apart
    )
    unused, shapes = ((8, LANES), F32), saved_shapes(cfg)
    held = [shapes._replace(second=unused)] + [shapes] * (LAYERS - 1)
    held[-1] = held[-1]._replace(mixed=unused)
    held = [pltpu.VMEM(*shape) for kept in held for shape in kept]
    scratch = [value for part in (common, forth, sems, back) for value in part.values()]
    shapes = [(cfg.tok, cfg.feats)] * 2 + list(grad_shapes(cfg))
    outs = pl.pallas_call(
        functools.partial(whole_kernel, cfg, list(common), list(forth), list(sems), list(back)),
        out_shape=[jax.ShapeDtypeStruct(shape, F32) for shape in shapes],
        in_specs=[whole] * len(streams) + list(specs) + [whole] * 2,
        out_specs=[whole] * len(shapes),
        scratch_shapes=held + scratch,
        compiler_params=pltpu.CompilerParams(
            collective_id=0, has_side_effects=True, vmem_limit_bytes=VMEM_LIMIT
        ),
        name="whole",
    )(*streams, *params, *cotangents)
    return outs[0], outs[1], Grads(*outs[2:])


def finish_kernel(cfg, count, *refs):
    small, sources, refs = refs[0], refs[1 : 1 + count], refs[1 + count :]
    targets, pieces, sem = refs[:count], refs[count:-1], refs[-1]
    copies = [
        pltpu.make_async_copy(source, target, sem.at[i])
        for i, (source, target) in enumerate(zip(sources, targets))
    ]
    for copy in copies:
        copy.start()
    index = lax.axis_index("seq")
    for line, piece in enumerate(pieces):
        share = piece.shape[1]
        tile = small[:, line, :]
        found = jnp.zeros(piece.shape, F32)
        for k in range(LANES // share):
            here = index % (LANES // share) == k
            found = jnp.where(here, tile[:, k * share : (k + 1) * share], found)
        piece[...] = found
    for copy in copies:
        copy.wait()


def finish_call(cfg, small, arrays):
    whole = pl.BlockSpec(memory_space=pltpu.VMEM)
    apart = pl.BlockSpec(memory_space=pl.ANY)
    count = len(arrays)
    shapes = [array.shape for array in arrays]
    shapes += [(LAYERS, cfg.feats // cfg.seq)] * 6 + [(LAYERS, cfg.hid // cfg.seq)]
    outs = pl.pallas_call(
        functools.partial(finish_kernel, cfg, count),
        out_shape=[jax.ShapeDtypeStruct(shape, F32) for shape in shapes],
        in_specs=[whole] * (1 + count),
        out_specs=[apart] * count + [whole] * 7,
        scratch_shapes=[pltpu.SemaphoreType.DMA((count,))],
        compiler_params=pltpu.CompilerParams(vmem_limit_bytes=VMEM_LIMIT),
        name="finish",
    )(small, *arrays)
    return outs[:count], outs[count:]


def shards(stream_one, stream_two, cotangent_one, cotangent_two, bucket_numbers, *params):
    cfg = sizes_of(lax.axis_size("seq"), stream_one, params[0], params[4])
    params = Params(*params)
    first, second = stream_one, stream_two
    if cfg.parts == 1:
        streams = Streams(first, second, bucket_numbers)
        first, second, out = whole_call(cfg, streams, (cotangent_one, cotangent_two), params)
    else:
        saved = []
        for layer in range(LAYERS):
            kept = forward_call(cfg, layer, Streams(first, second, bucket_numbers), params)
            saved.append(kept._replace(second=second))
            first, second = kept.mixed, kept.second
        out = backward_call(cfg, params, (cotangent_one, cotangent_two), saved)
    arrays = (first, second) + tuple(out)[:-1]
    (first, second, one, two, wq, wv, wm, we, ws), small = finish_call(cfg, out.out_small, arrays)
    return (
        first,
        second,
        one,
        two,
        wq,
        wv,
        wm,
        small[1],
        we,
        small[6],
        ws,
        small[0],
        small[4],
        small[5],
        small[2],
        small[3],
    )


def solution(mesh):
    in_specs = (
        P("seq", None),
        P("seq", None),
        P("seq", None),
        P("seq", None),
        P(None, None, "mp", None),
        P(None, None, "mp"),
        P(None, None, "mp"),
        P(None, "mp", None),
        P(),
        P(None, None, "mp"),
        P(None, "mp"),
        P(None, "mp", None),
        P(),
        P(),
        P(),
        P(),
        P(),
    )
    out_specs = (
        P("seq", None),
        P("seq", None),
        P("seq", None),
        P("seq", None),
        P(None, "seq", "mp"),
        P(None, "seq", "mp"),
        P(None, ("mp", "seq"), None),
        P(None, "seq"),
        P(None, "seq", "mp"),
        P(None, ("mp", "seq")),
        P(None, ("mp", "seq"), None),
        P(None, "seq"),
        P(None, "seq"),
        P(None, "seq"),
        P(None, "seq"),
        P(None, "seq"),
    )
    return jax.shard_map(shards, mesh=mesh, in_specs=in_specs, out_specs=out_specs, check_vma=False)
```

```python
import functools
import math
from types import SimpleNamespace
from typing import NamedTuple

import jax
import jax.numpy as jnp
from jax import lax
from jax.experimental import pallas as pl
from jax.experimental.pallas import tpu as pltpu
from jax.sharding import PartitionSpec as P

DH = 128
SPAN = 64
ROUNDS = 4
LAYERS = 2
LANES = 128
CHUNK = 128
UNROLL = 8
MESH = pl.DeviceIdType.MESH
F32 = jnp.float32
BF16 = jnp.bfloat16
AWAY = -1e30
VMEM_LIMIT = 62 << 20


class Sizes(NamedTuple):
    seq: int
    tok: int
    heads: int
    plane: int
    bits: int
    parts: int
    total: int
    rows: int
    ext: int
    buckets: int
    feats: int
    width: int
    hid: int


def sizes_of(seq, stream, query_weight, expand_weight):
    tok, feats = stream.shape
    width = query_weight.shape[2]
    heads = width // DH
    plane = seq // heads
    parts = plane // ROUNDS
    total = seq * tok
    rows = total // parts
    return Sizes(
        seq,
        tok,
        heads,
        plane,
        plane.bit_length() - 1,
        parts,
        total,
        rows,
        rows + CHUNK,
        total // SPAN,
        feats,
        width,
        expand_weight.shape[2],
    )


def dot(left, right):
    return lax.dot_general(left, right, (((1,), (0,)), ((), ())), preferred_element_type=F32)


def dot_nt(left, right):
    return lax.dot_general(left, right, (((1,), (1,)), ((), ())), preferred_element_type=F32)


def dot_tn(left, right):
    return lax.dot_general(left, right, (((0,), (0,)), ((), ())), preferred_element_type=F32)


def norm_parts(values):
    center = values - jnp.mean(values, axis=-1, keepdims=True)
    scale = lax.rsqrt(jnp.mean(center * center, axis=-1, keepdims=True) + 1e-05)
    return center * scale, scale


def norm_back(xhat, scale, gain, grad):
    t = grad * gain
    inner = t - jnp.mean(t, axis=-1, keepdims=True) - xhat * jnp.mean(t * xhat, axis=-1, keepdims=True)
    return scale * inner


def key_scale(keys):
    return lax.rsqrt(jnp.mean(keys * keys, axis=-1, keepdims=True) + 1e-06)


def rows_to_columns(rows):
    return jnp.transpose(jnp.broadcast_to(rows, (LANES, rows.shape[1])))


def split_three(values):
    high = values.astype(BF16).astype(F32)
    rest = values - high
    middle = rest.astype(BF16).astype(F32)
    return high, middle, rest - middle


class Place:
    def __init__(self, cfg):
        self.cfg = cfg
        self.index = lax.axis_index("seq")
        self.half = lax.axis_index("mp")
        self.head = self.index // cfg.plane
        self.member = self.index % cfg.plane
        self.round = self.member // cfg.parts
        self.part = self.member % cfg.parts

    def bit(self, k):
        return (self.member // 2**k) % 2

    def z_peer(self, step):
        head = (self.head + step) % self.cfg.heads
        return head, (head * self.cfg.plane + self.member, self.half)

    def z_source(self, step):
        return (self.head + self.cfg.heads - step) % self.cfg.heads

    def bit_peer(self, k):
        return (self.index + (1 - 2 * self.bit(k)) * 2**k, self.half)

    def y_peer(self):
        return (self.index, 1 - self.half)

    def kept(self, k, i):
        return 2 ** (k + 1) * i + self.member % 2 ** (k + 1)

    def given(self, k, i):
        return 2 ** (k + 1) * i + (1 - self.bit(k)) * 2**k + self.member % 2**k

    def landing(self, k, spot):
        return self.cfg.plane - self.cfg.plane // 2**k + spot // 2 ** (k + 1)

    def group(self, k):
        return self.cfg.plane // 2 ** (k + 1)

    def plane_peer(self, step):
        member = (self.member + step) % self.cfg.plane
        return member, (self.head * self.cfg.plane + member, self.half)

    def greet(self):
        barrier = pltpu.get_barrier_semaphore()
        peers = [self.z_peer(step)[1] for step in range(1, self.cfg.heads)]
        peers += [self.plane_peer(step)[1] for step in range(1, self.cfg.plane)]
        peers += [self.y_peer()]
        for peer in peers:
            pl.semaphore_signal(barrier, inc=1, device_id=peer, device_id_type=MESH)
        pl.semaphore_wait(barrier, len(peers))


def remote(src, dst, send, recv, peer):
    return pltpu.make_async_remote_copy(
        src_ref=src, dst_ref=dst, send_sem=send, recv_sem=recv, device_id=peer, device_id_type=MESH
    )


def rank_rows(cfg, bucket_row, rank_ref):
    count = cfg.buckets
    ids = lax.broadcasted_iota(jnp.int32, (count, LANES), 0)
    ahead = (
        lax.broadcasted_iota(jnp.int32, (LANES, LANES), 0)
        < lax.broadcasted_iota(jnp.int32, (LANES, LANES), 1)
    ).astype(BF16)
    lower = (
        lax.broadcasted_iota(jnp.int32, (count, count), 1)
        < lax.broadcasted_iota(jnp.int32, (count, count), 0)
    ).astype(BF16)
    marks = [
        (bucket_row[:, p * LANES : (p + 1) * LANES] == ids).astype(F32) for p in range(cfg.seq)
    ]
    totals = sum(marks)
    totals = jnp.broadcast_to(jnp.sum(totals, axis=1, keepdims=True), (count, LANES))
    carry = dot(lower, totals.astype(BF16))
    for p in range(cfg.seq):
        within = dot(marks[p].astype(BF16), ahead)
        rank = jnp.sum(marks[p] * (within + carry), axis=0, keepdims=True)
        carry = carry + jnp.broadcast_to(jnp.sum(marks[p], axis=1, keepdims=True), (count, LANES))
        spot = (p % cfg.plane) * cfg.heads + p // cfg.plane
        rank_ref[:, spot * LANES : (spot + 1) * LANES] = jnp.broadcast_to(
            rank.astype(jnp.int32), (8, LANES)
        )


def sort_rows(cfg, rank_ref, source_ref, store, start, size, chunks):
    step = min(cfg.total, 2048)

    def body(c, _):
        spots = start + c * size + lax.broadcasted_iota(jnp.int32, (size, step), 0)
        spots = spots % cfg.total if cfg.parts > 1 else spots
        found = None
        for k in range(cfg.total // step):
            ranks = rank_ref[0:1, k * step : (k + 1) * step]
            pick = (spots == ranks).astype(BF16)
            part = dot(pick, source_ref[k * step : (k + 1) * step, :])
            found = part if found is None else found + part
        store(c, found)
        return 0

    lax.fori_loop(0, chunks, body, 0)


def several(step, count):
    def body(c, _):
        for i in range(UNROLL):
            step(c * UNROLL + i)
        return 0

    lax.fori_loop(0, count // UNROLL, body, 0)


def window_mask():
    row = lax.broadcasted_iota(jnp.int32, (CHUNK, 2 * CHUNK), 0)
    column = lax.broadcasted_iota(jnp.int32, (CHUNK, 2 * CHUNK), 1)
    gap = column // SPAN - row // SPAN
    near = jnp.logical_or(gap == 1, gap == 2)
    return jnp.logical_and(near, column != row + CHUNK)


def z_exchange(cfg, place, source, target, send, recv):
    copies = []
    for step in range(1, cfg.heads):
        head, peer = place.z_peer(step)
        copy = remote(source(head), target(place.head), send.at[step], recv.at[step], peer)
        copy.start()
        copies.append(copy)
    return copies


def z_arrival(place, block, recv, step):
    return remote(block, block, recv.at[step], recv.at[step], place.z_peer(step)[1])


class Doubling:
    def __init__(self, place, keys, block, send, recv):
        self.place, self.keys, self.block = place, keys, block
        self.send, self.recv = send, recv

    def give(self, key, spot, k):
        return remote(
            self.block(key, spot),
            self.block(key, spot),
            self.send.at[k, key, spot],
            self.recv.at[key, spot],
            self.place.bit_peer(k),
        )

    def offer(self, key):
        for k in range(self.place.cfg.bits):
            self.give(key, self.place.member, k).start()

    def spots(self):
        for k in reversed(range(self.place.cfg.bits)):
            for key in self.keys:
                for i in range(self.place.group(k)):
                    yield k, key, self.place.given(k, i)

    def receive_bit(self, k):
        for key in self.keys:
            for i in range(self.place.group(k)):
                spot = self.place.given(k, i)
                self.give(key, spot, k).wait_recv()
                for low in range(k):
                    self.give(key, spot, low).start()

    def receive(self):
        for k in reversed(range(self.place.cfg.bits)):
            self.receive_bit(k)

    def finish(self):
        for key in self.keys:
            for k in range(self.place.cfg.bits):
                self.give(key, self.place.member, k).wait_send()
        for k, key, spot in self.spots():
            for low in range(k):
                self.give(key, spot, low).wait_send()


class Params(NamedTuple):
    wq_hbm: jax.Array
    wv_hbm: jax.Array
    wm_hbm: jax.Array
    mix_bias: jax.Array
    we_hbm: jax.Array
    expand_bias: jax.Array
    ws_hbm: jax.Array
    shrink_bias: jax.Array
    attention_gain: jax.Array
    attention_shift: jax.Array
    forward_gain: jax.Array
    forward_shift: jax.Array


class Streams(NamedTuple):
    first: jax.Array
    second: jax.Array
    buckets: jax.Array


class Kept(NamedTuple):
    mixed: jax.Array
    sorted: jax.Array
    comb: jax.Array
    joint: jax.Array
    slope: jax.Array
    rank: jax.Array
    lhs_qv: jax.Array
    lhs_expand: jax.Array
    lhs_shrink: jax.Array
    lhs_mix: jax.Array
    second: jax.Array


class Grads(NamedTuple):
    first_out: jax.Array
    second_out: jax.Array
    out_wq: jax.Array
    out_wv: jax.Array
    out_wm: jax.Array
    out_we: jax.Array
    out_ws: jax.Array
    out_small: jax.Array


def gathered(*groups, **scratch):
    merged = {}
    for group in groups:
        merged.update(group._asdict())
    return SimpleNamespace(**merged, **scratch)


def common_scratch(cfg):
    dma = pltpu.SemaphoreType.DMA
    return dict(
        wq=pltpu.VMEM((cfg.feats, cfg.width), BF16),
        wv=pltpu.VMEM((cfg.feats, cfg.width), BF16),
        wm=pltpu.VMEM((cfg.width, cfg.feats), BF16),
        we=pltpu.VMEM((cfg.feats, cfg.hid), BF16),
        ws=pltpu.VMEM((cfg.hid, cfg.feats), BF16),
        ys=pltpu.VMEM((2, cfg.tok, cfg.feats), BF16),
        yr=pltpu.VMEM((2, cfg.tok, cfg.feats), BF16),
        wsem=dma((5,)),
        ysend=dma((2, 2)),
        yrecv=dma((2, 2)),
        wm_other=pltpu.VMEM((cfg.width, cfg.feats), BF16),
        low_own=pltpu.VMEM((cfg.tok, cfg.width), BF16),
        low_other=pltpu.VMEM((cfg.tok, cfg.width), BF16),
        msend=dma((2,)),
        mrecv=dma((2,)),
    )


class Weights:
    def __init__(self, r, layers):
        self.pairs = (
            (r.wq_hbm, r.wq),
            (r.wv_hbm, r.wv),
            (r.wm_hbm, r.wm),
            (r.we_hbm, r.we),
            (r.ws_hbm, r.ws),
        )
        self.sem, self.layers = r.wsem, layers
        self.turn, self.flying = [0] * 5, [False] * 5

    def copy(self, i):
        source, target = self.pairs[i]
        return pltpu.make_async_copy(source.at[self.layers[self.turn[i]]], target, self.sem.at[i])

    def fetch(self, *numbers):
        for i in numbers:
            self.copy(i).start()
            self.flying[i] = True

    def need(self, *numbers):
        for i in numbers:
            if self.flying[i]:
                self.copy(i).wait()
                self.flying[i] = False

    def release(self, *numbers):
        for i in numbers:
            if self.turn[i] + 1 < len(self.layers):
                self.turn[i] += 1
                self.fetch(i)


def forward_scratch(cfg):
    tok, heads, plane, bits = cfg.tok, cfg.heads, cfg.plane, cfg.bits
    band = heads * tok
    return dict(
        zs=pltpu.VMEM((heads, tok, 2 * DH), BF16),
        tokens=pltpu.VMEM((cfg.total, 2 * DH), BF16),
        keys=pltpu.VMEM((cfg.ext, DH), BF16),
        attended=pltpu.VMEM((cfg.rows, 3 * DH), BF16),
        part=pltpu.VMEM((plane, band, DH), F32),
        lrow=pltpu.VMEM((plane, 8, band), F32),
        part_in=pltpu.VMEM((plane, band, DH), F32),
        lrow_in=pltpu.VMEM((plane, 8, band), F32),
        low_out=pltpu.VMEM((heads, tok, DH), BF16),
        low_in=pltpu.VMEM((heads, tok, DH), BF16),
        normed_t=pltpu.VMEM((cfg.feats, tok), BF16),
        turned_expand=turned_of(cfg, cfg.feats),
        turned_shrink=turned_of(cfg, cfg.hid),
        turned_mix=turned_of(cfg, cfg.width),
    )


def forward_sems(cfg, layers):
    heads, plane, bits = cfg.heads, cfg.plane, cfg.bits
    shapes = dict(
        zsend=(heads,),
        zrecv=(heads,),
        gsend=(bits, heads, plane),
        grecv=(heads, plane),
        psend=(bits, plane, 2),
        precv=(bits, plane, 2),
        csend=(heads,),
        crecv=(heads,),
        nsend=(heads,),
        nrecv=(heads,),
        tsend=(4, plane),
        trecv=(4, plane),
    )
    return {name: pltpu.SemaphoreType.DMA((layers,) + shape) for name, shape in shapes.items()}


class Turned:
    def __init__(self, place, number, values, source, target, r):
        self.place, self.source, self.target = place, source, target
        self.send, self.recv = r.tsend.at[number], r.trecv.at[number]
        source[...] = jnp.transpose(values).reshape(source.shape).astype(source.dtype)

    def slot(self, member):
        tok = self.place.cfg.tok
        return self.target.at[:, :, pl.ds(pl.multiple_of(member * tok, tok), tok)]

    def copy(self, step):
        member, peer = self.place.plane_peer(step)
        return remote(
            self.source.at[:, member], self.slot(self.place.member), self.send.at[step], self.recv.at[step], peer
        )

    def start(self):
        for step in range(1, self.place.cfg.plane):
            self.copy(step).start()
        self.slot(self.place.member)[...] = self.source[:, self.place.member]

    def finish(self):
        cfg = self.place.cfg
        for step in range(1, cfg.plane):
            self.copy(step).wait_send()
            arrived = self.slot((self.place.member + cfg.plane - step) % cfg.plane)
            remote(arrived, arrived, self.send.at[step], self.recv.at[step], self.place.y_peer()).wait_recv()


def y_sum(place, r, slot, partial, meanwhile=None, first=()):
    wide = r.ys.shape[2] // 2
    copies = []
    for c in range(2):
        at = slice(c * wide, (c + 1) * wide)
        r.ys[slot, :, at] = partial(at).astype(BF16)
        mine, theirs = r.ys.at[slot, :, at], r.yr.at[slot, :, at]
        copies.append(remote(mine, theirs, r.ysend.at[slot, c], r.yrecv.at[slot, c], place.y_peer()))
        copies[-1].start()
    for step in first:
        step()
    if meanwhile is not None:
        meanwhile()
    for copy in copies:
        copy.wait()
    return r.ys[slot].astype(F32) + r.yr[slot].astype(F32)


def forward_kernel(cfg, layer, names, sems, *refs):
    inputs, refs = refs[:IN_COUNT], refs[IN_COUNT:]
    streams, params = Streams(*inputs[:3]), Params(*inputs[3:])
    out, refs = Kept(*refs[: len(Kept._fields)]), refs[len(Kept._fields) :]
    r = gathered(out, streams, params, **dict(zip(names, refs)))
    vars(r).update({name: ref.at[0] for name, ref in zip(sems, refs[len(names) :])})
    r.second, r.renewed = streams.second, out.second
    weights = Weights(r, [layer])
    weights.fetch(*range(5))
    forward_layer(cfg, Place(cfg), layer, r, weights, True)()


def forward_layer(cfg, place, layer, r, weights, first, before=None):
    tok, heads = cfg.tok, cfg.heads
    band = heads * tok
    one = slice(layer, layer + 1)
    normed = norm_parts(r.second[...])[0] * r.attention_gain[one, :] + r.attention_shift[one, :]
    normed = normed.astype(BF16)
    weights.need(0, 1)
    queries = dot(normed, r.wq[...]).astype(BF16)
    values = dot(normed, r.wv[...]).astype(BF16)
    if first:
        weights.release(0, 1)
    for head in range(heads):
        r.zs[head, :, :DH] = queries[:, head * DH : (head + 1) * DH]
        r.zs[head, :, DH:] = values[:, head * DH : (head + 1) * DH]

    def block(head, spot):
        return r.tokens.at[pl.ds(pl.multiple_of((spot * heads + head) * tok, tok), tok), :]

    if first:
        place.greet()
    sent = z_exchange(
        cfg,
        place,
        lambda head: r.zs.at[head],
        lambda head: block(head, place.member),
        r.zsend,
        r.zrecv,
    )
    block(place.head, place.member)[...] = r.zs[place.head]
    weights.need(2)
    swapped = remote(r.wm, r.wm_other, r.msend.at[0], r.mrecv.at[0], place.y_peer())
    swapped.start()
    r.normed_t[...] = jnp.transpose(normed)

    def column(head):
        return r.lhs_qv.at[:, pl.ds(pl.multiple_of(head * tok, tok), tok)]

    column(place.head)[...] = r.normed_t[...]
    rank_rows(cfg, r.buckets[layer, place.round, pl.ds(place.head, 1), :], r.rank)

    spread = Doubling(
        place, [place.z_source(step) for step in range(heads)], block, r.gsend, r.grecv
    )
    for step in range(heads):
        if step > 0:
            z_arrival(place, block(place.z_source(step), place.member), r.zrecv, step).wait_recv()
        spread.offer(place.z_source(step))
    spread.receive()
    if before is not None:
        before()
    sent += z_exchange(cfg, place, lambda head: r.normed_t, column, r.nsend, r.nrecv)
    base = place.part * cfg.rows

    def store_rows(c, found):
        r.sorted[pl.ds(pl.multiple_of(CHUNK + c * 512, CHUNK), 512), :] = found.astype(BF16)

    def store_halo(c, found):
        r.sorted[0:CHUNK, :] = found.astype(BF16)

    sort_rows(cfg, r.rank, r.tokens, store_rows, base, 512, cfg.rows // 512)
    if cfg.parts == 1:
        r.sorted[0:CHUNK, :] = r.sorted[cfg.rows : cfg.ext, :]
    else:
        sort_rows(cfg, r.rank, r.tokens, store_halo, base + cfg.total - CHUNK, CHUNK, 1)
    raw = r.sorted[:, :DH].astype(F32)
    r.keys[...] = (raw * key_scale(raw)).astype(BF16)
    mask = window_mask()
    lane = lax.broadcasted_iota(jnp.int32, (CHUNK, LANES), 1)

    def attend(c):
        at = pl.multiple_of(c * CHUNK, CHUNK)
        query = r.sorted[pl.ds(at + CHUNK, CHUNK), :DH]
        scores = dot_nt(query, r.keys[pl.ds(at, 2 * CHUNK), :]) / math.sqrt(DH)
        scores = jnp.where(mask, scores, -1000000000.0)
        peak = jnp.max(scores, axis=-1, keepdims=True)
        powers = jnp.exp(scores - peak)
        summed = jnp.sum(powers, axis=-1, keepdims=True)
        weights = (powers / summed).astype(BF16)
        output = dot(weights, r.sorted[pl.ds(at, 2 * CHUNK), DH:])
        high, middle, low = split_three(peak + jnp.log(summed))
        extra = jnp.where(lane == 0, high, 0.0)
        extra = jnp.where(lane == 1, middle, extra)
        extra = jnp.where(lane == 2, low, extra)
        extra = jnp.where(lane == 3, 1.0, extra)
        r.attended[pl.ds(at, CHUNK), :DH] = output.astype(BF16)
        r.attended[pl.ds(at, CHUNK), DH : 2 * DH] = (
            output - output.astype(BF16).astype(F32)
        ).astype(BF16)
        r.attended[pl.ds(at, CHUNK), 2 * DH :] = extra.astype(BF16)

    several(attend, cfg.rows // CHUNK)
    spread.finish()

    def unsort(spot):
        pick = unsort_pick(cfg, r.rank, spot, base, cfg.rows)
        found = dot(pick, r.attended[:, : 2 * DH])
        r.part[spot] = found[:, :DH] + found[:, DH:]
        extra = jnp.transpose(dot(pick, r.attended[:, 2 * DH :]))
        row = extra[0:1] + extra[1:2] + extra[2:3] + (1.0 - extra[3:4]) * AWAY
        r.lrow[spot] = jnp.broadcast_to(row, (8, band))

    def pass_part(k, spot):
        peer = place.bit_peer(k)
        return [
            remote(
                mine.at[spot],
                theirs.at[place.landing(k, spot)],
                r.psend.at[k, spot, i],
                r.precv.at[k, spot, i],
                peer,
            )
            for i, (mine, theirs) in enumerate(((r.part, r.part_in), (r.lrow, r.lrow_in)))
        ]

    def first_half(i, _):
        unsort(place.given(0, i))
        for copy in pass_part(0, place.given(0, i)):
            copy.start()
        return 0

    def second_half(i, _):
        unsort(place.kept(0, i))
        return 0

    lax.fori_loop(0, place.group(0), first_half, 0)
    lax.fori_loop(0, place.group(0), second_half, 0)

    def merge(k, spot):
        for copy in pass_part(k, spot):
            copy.wait_recv()
        mine = rows_to_columns(r.lrow[spot][0:1])
        landed = place.landing(k, spot)
        other = rows_to_columns(r.lrow_in[landed][0:1])
        highest = jnp.maximum(mine, other)
        share = jnp.exp(mine - highest)
        share_in = jnp.exp(other - highest)
        both = share + share_in
        merged = (r.part[spot].astype(F32) * share + r.part_in[landed].astype(F32) * share_in) / both
        return merged, jnp.transpose(highest + jnp.log(both))[0:8]

    for k in range(cfg.bits - 1):
        for giving in (True, False):
            for i in range(place.group(k + 1)):
                spot = place.given(k + 1, i) if giving else place.kept(k + 1, i)
                merged, joint = merge(k, spot)
                r.part[spot] = merged
                r.lrow[spot] = joint
                if giving:
                    for copy in pass_part(k + 1, spot):
                        copy.start()
    merged, joint = merge(cfg.bits - 1, place.member)
    r.comb[...] = merged
    r.joint[...] = joint
    for head in range(heads):
        r.low_out[head] = merged[head * tok : (head + 1) * tok].astype(BF16)
    back = z_exchange(
        cfg, place, lambda head: r.low_out.at[head], lambda head: r.low_in.at[head], r.csend, r.crecv
    )
    r.low_in[place.head] = r.low_out[place.head]
    weights.need(2)
    for step in range(1, heads):
        z_arrival(place, r.low_in.at[place.z_source(step)], r.crecv, step).wait_recv()
    low = jnp.concatenate([r.low_in[head] for head in range(heads)], axis=1)

    turned_mix = Turned(place, 3, low, r.turned_mix, r.lhs_mix, r)

    def finish_sends():
        for copy in sent + back:
            copy.wait_send()
        for k in range(cfg.bits):
            for i in range(place.group(k)):
                for copy in pass_part(k, place.given(k, i)):
                    copy.wait_send()
        turned_mix.start()

    r.low_own[...] = low
    passed = remote(r.low_own, r.low_other, r.msend.at[1], r.mrecv.at[1], place.y_peer())
    passed.start()
    own = dot(low, r.wm[...])
    finish_sends()
    swapped.wait()
    if first:
        weights.release(2)
    passed.wait()
    mixed = r.first[...] + (own + dot(r.low_other[...], r.wm_other[...])) + r.mix_bias[one, :]
    r.mixed[...] = mixed
    normed_two = norm_parts(mixed)[0] * r.forward_gain[one, :] + r.forward_shift[one, :]
    normed_two = normed_two.astype(BF16)
    weights.need(3)
    hidden = dot(normed_two, r.we[...]) + r.expand_bias[one, :]
    curve = 0.5 * (1.0 + lax.erf(hidden * math.sqrt(0.5)))
    active = (hidden * curve).astype(BF16)
    weights.need(4)

    def turn():
        turned_shrink = Turned(place, 2, active, r.turned_shrink, r.lhs_shrink, r)
        turned_shrink.start()
        turned_expand = Turned(place, 1, normed_two, r.turned_expand, r.lhs_expand, r)
        turned_expand.start()
        bell = jnp.exp(-0.5 * hidden * hidden) * (1.0 / math.sqrt(2.0 * math.pi))
        r.slope[...] = curve + hidden * bell
        pending.extend([turned_shrink, turned_expand])

    pending = [turned_mix]
    moved = [lambda: weights.release(3, 4)] if first else []
    branch = y_sum(place, r, 1, lambda at: dot(active, r.ws[:, at]), turn, moved)
    r.renewed[...] = r.second[...] + branch + r.shrink_bias[one, :]

    def finish_turned():
        for turned in pending:
            turned.finish()
        for step in range(1, heads):
            z_arrival(place, column(place.z_source(step)), r.nrecv, step).wait_recv()

    return finish_turned


def unsort_pick(cfg, rank_ref, spot, base, rows):
    band = cfg.heads * cfg.tok
    ranks = rank_ref[0:1, pl.ds(pl.multiple_of(spot * band, band), band)]
    ranks = rows_to_columns(ranks.astype(F32)).astype(jnp.int32)[:, 0:1]
    places = base + lax.broadcasted_iota(jnp.int32, (band, rows), 1)
    if cfg.parts > 1:
        places = places % cfg.total
    return (ranks == places).astype(BF16)


IN_COUNT = len(Streams._fields) + len(Params._fields)


def forward_call(cfg, layer, streams, params):
    scratch = common_scratch(cfg) | forward_scratch(cfg)
    sems = forward_sems(cfg, 1)
    whole = pl.BlockSpec(memory_space=pltpu.VMEM)
    apart = pl.BlockSpec(memory_space=pl.ANY)
    specs = Params(*[whole] * len(params))._replace(
        wq_hbm=apart, wv_hbm=apart, wm_hbm=apart, we_hbm=apart, ws_hbm=apart
    )
    outs = pl.pallas_call(
        functools.partial(forward_kernel, cfg, layer, list(scratch), list(sems)),
        out_shape=[jax.ShapeDtypeStruct(*shape) for shape in saved_shapes(cfg)],
        in_specs=[whole] * len(streams) + list(specs),
        out_specs=[whole] * len(Kept._fields),
        scratch_shapes=list(scratch.values()) + list(sems.values()),
        compiler_params=pltpu.CompilerParams(
            collective_id=layer, has_side_effects=True, vmem_limit_bytes=VMEM_LIMIT
        ),
        name=f"forward_{layer}",
    )(*streams, *params)
    return Kept(*outs)


def lines_of(cfg, extent):
    deep = extent // cfg.seq
    return (cfg.heads, deep, cfg.plane * cfg.tok), BF16 if deep % 16 == 0 else F32


def turned_of(cfg, extent):
    (heads, deep, _), kind = lines_of(cfg, extent)
    return pltpu.VMEM((heads, cfg.plane, deep, cfg.tok), kind)


def saved_shapes(cfg):
    tok, feats, band = cfg.tok, cfg.feats, cfg.heads * cfg.tok
    return Kept(
        second=((tok, feats), F32),
        mixed=((tok, feats), F32),
        sorted=((cfg.ext, 2 * DH), BF16),
        comb=((band, DH), F32),
        joint=((8, band), F32),
        slope=((tok, cfg.hid), F32),
        rank=((8, cfg.total), jnp.int32),
        lhs_qv=((feats, band), BF16),
        lhs_expand=lines_of(cfg, feats),
        lhs_shrink=lines_of(cfg, cfg.hid),
        lhs_mix=lines_of(cfg, cfg.width),
    )


class Job(NamedTuple):
    name: str
    side: str
    number: int
    rows: int
    columns: int
    fold: int

    def scratch(self, cfg):
        deep, wide = self.rows * self.fold, self.columns // self.fold
        return {
            "rhs" + self.side: pltpu.VMEM((cfg.plane * cfg.tok, self.columns), BF16),
            "prod" + self.name: pltpu.VMEM((cfg.heads, deep, wide), BF16),
            "zin" + self.name: pltpu.VMEM((3, deep, wide), BF16),
        }


def slots_of(cfg):
    return LAYERS if cfg.parts == 1 else 1


def jobs_of(cfg):
    share = cfg.feats // cfg.seq
    mix = cfg.width // cfg.seq
    return (
        Job("s", "s", 0, cfg.hid // cfg.seq, cfg.feats, 1),
        Job("m", "m", 1, mix, cfg.feats, 1 if mix % 16 == 0 else 2),
    ) + tuple(
        Job(f"e{i}", f"e{i}", 2 + i, share, cfg.feats, 1) for i in range(cfg.hid // cfg.feats)
    )


def backward_scratch(cfg):
    tok, heads, plane, bits = cfg.tok, cfg.heads, cfg.plane, cfg.bits
    band = heads * tok
    dma = pltpu.SemaphoreType.DMA
    return dict(
        gs=pltpu.VMEM((heads, tok, DH), BF16),
        gtokens=pltpu.VMEM((cfg.total, 2 * DH), BF16),
        arow=pltpu.VMEM((LAYERS, plane, 8, band), F32),
        gsorted=pltpu.VMEM((cfg.rows, DH), BF16),
        stats=pltpu.VMEM((cfg.rows, LANES), F32),
        keys=pltpu.VMEM((cfg.ext, DH), BF16),
        dq=pltpu.VMEM((cfg.ext, DH), F32),
        dk=pltpu.VMEM((cfg.ext, DH), F32),
        dv=pltpu.VMEM((cfg.ext, DH), F32),
        grads=pltpu.VMEM((cfg.ext, 2 * DH), BF16),
        part=pltpu.VMEM((plane, band, 2 * DH), BF16),
        part_in=pltpu.VMEM((plane, band, 2 * DH), BF16),
        home_out=pltpu.VMEM((heads, tok, 2 * DH), BF16),
        home_in=pltpu.VMEM((heads, tok, 2 * DH), BF16),
        vectors=pltpu.VMEM((8, cfg.feats), F32),
        vys=pltpu.VMEM((8, cfg.feats), F32),
        vyr=pltpu.VMEM((8, cfg.feats), F32),
        vysem=dma((2,)),
        **{key: value for job in jobs_of(cfg) for key, value in job.scratch(cfg).items()},
        vbuf=pltpu.VMEM((LAYERS, plane, heads, 8, LANES), F32),
        vin=pltpu.VMEM((LAYERS, plane, heads, 8, LANES), F32),
        vz=pltpu.VMEM((LAYERS, heads, 8, LANES), F32),
        lsem=dma((LAYERS, len(Kept._fields))),
        zsend=dma((LAYERS, heads)),
        zrecv=dma((LAYERS, heads)),
        gsend=dma((LAYERS, bits, heads, plane)),
        grecv=dma((LAYERS, heads, plane)),
        asend=dma((LAYERS, bits, 1, plane)),
        arecv=dma((LAYERS, 1, plane)),
        psend=dma((LAYERS, bits, plane)),
        precv=dma((LAYERS, bits, plane)),
        csend=dma((LAYERS, heads)),
        crecv=dma((LAYERS, heads)),
        rsend=dma((len(jobs_of(cfg)), bits, 1, plane)),
        rrecv=dma((len(jobs_of(cfg)), 1, plane)),
        usend=dma((len(jobs_of(cfg)), 3)),
        urecv=dma((len(jobs_of(cfg)), 3)),
        qbuf=pltpu.VMEM((plane, heads, cfg.feats // cfg.seq, 2 * DH), BF16),
        qin=pltpu.VMEM((plane, heads, cfg.feats // cfg.seq, 2 * DH), BF16),
        qz=pltpu.VMEM((heads, cfg.feats // cfg.seq, 2 * DH), BF16),
        qsend=dma((bits + heads,)),
        qrecv=dma((bits + heads,)),
        vsend=dma((LAYERS, bits + heads)),
        vrecv=dma((LAYERS, bits + heads)),
    )


class Unit:
    def __init__(self, place, fill, done, buf, arrive, zbuf, send, recv):
        self.place, self.fill, self.done = place, fill, done
        self.buf, self.arrive, self.zbuf, self.send, self.recv = buf, arrive, zbuf, send, recv

    def halved(self, k):
        place, plane = self.place, self.place.cfg.plane
        group = place.group(k)
        start = plane - plane // 2**k
        shape = (group, 2 ** (k + 1)) + self.buf.shape[1:]
        spot = (1 - place.bit(k)) * 2**k + place.member % 2**k
        return remote(
            self.buf.reshape(*shape).at[:, spot],
            self.arrive.at[start : start + group],
            self.send.at[k],
            self.recv.at[k],
            place.bit_peer(k),
        )

    def across(self, step):
        place = self.place
        head, peer = place.z_peer(step)
        at = place.cfg.bits + step
        return remote(
            self.buf.at[place.member, head], self.zbuf.at[step], self.send.at[at], self.recv.at[at], peer
        )

    def start(self):
        self.fill(self.buf)
        self.halved(0).start()

    def fold(self):
        place, cfg = self.place, self.place.cfg
        for k in range(cfg.bits):
            self.halved(k).wait_recv()
            start = cfg.plane - cfg.plane // 2**k
            for i in range(place.group(k)):
                spot = place.kept(k, i)
                both = self.buf[spot].astype(F32) + self.arrive[start + i].astype(F32)
                self.buf[spot] = both.astype(self.buf.dtype)
            if k + 1 < cfg.bits:
                self.halved(k + 1).start()
            if k + 2 == cfg.bits:
                yield
        for step in range(1, cfg.heads):
            self.across(step).start()
        yield
        found = [(place.head, self.buf[place.member, place.head])]
        for step in range(1, cfg.heads):
            self.across(step).wait_recv()
            found.append((place.z_source(step), self.zbuf[step]))
        self.done(found)
        for k in range(cfg.bits):
            self.halved(k).wait_send()
        for step in range(1, cfg.heads):
            self.across(step).wait_send()
        yield


class Gathered:
    def __init__(self, place, job, left, right, done, r):
        self.place, self.job, self.left, self.right, self.done = place, job, left, right, done
        tok = place.cfg.tok
        self.rhs = vars(r)["rhs" + job.side]
        self.prod, self.zin = vars(r)["prod" + job.name], vars(r)["zin" + job.name]
        self.send, self.recv = r.usend.at[job.number], r.urecv.at[job.number]
        self.spread = Doubling(
            place,
            [0],
            lambda key, spot: self.rhs.at[pl.ds(pl.multiple_of(spot * tok, tok), tok), :],
            r.rsend.at[job.number],
            r.rrecv.at[job.number],
        )
        head = place.head
        self.inner = (head * (3 - head)) // 2
        self.near = head + 1 - 2 * (head % 2)
        self.far = 3 - 3 * (head // 2)

    def copy(self, number):
        place, inner = self.place, self.inner
        if number == 0:
            dest, block, slot = self.near, self.near, 0
        elif number == 1:
            dest, block, slot = self.far, self.far, 2 - inner
        else:
            other = 3 - place.head
            dest = self.near * (1 - inner) + other * inner
            block = (3 - self.near) * (1 - inner) + other * inner
            slot = 2 - inner
        return remote(
            self.prod.at[block],
            self.zin.at[slot],
            self.send.at[number],
            self.recv.at[slot],
            (dest * place.cfg.plane + place.member, place.half),
        )

    def arrival(self, slot):
        spot = self.zin.at[slot]
        return remote(spot, spot, self.send.at[slot], self.recv.at[slot], self.place.y_peer())

    def start(self):
        self.spread.block(0, self.place.member)[...] = self.right
        self.spread.offer(0)

    def forward(self):
        for k in reversed(range(1, self.place.cfg.bits)):
            self.spread.receive_bit(k)

    def multiply(self):
        cfg, job = self.place.cfg, self.job
        self.spread.receive_bit(0)
        lines = self.left[...].reshape(cfg.heads * job.rows, cfg.plane * cfg.tok).astype(BF16)
        wide = job.columns // job.fold
        found = [
            dot(lines, self.rhs[:, i * wide : (i + 1) * wide]).reshape(cfg.heads, job.rows, wide)
            for i in range(job.fold)
        ]
        found = found[0] if job.fold == 1 else jnp.concatenate(found, axis=1)
        self.prod[...] = found.astype(BF16)

        @pl.when(self.inner == 0)
        def _():
            self.copy(2).start()

        self.copy(1).start()
        self.copy(0).start()
        self.spread.finish()

    def relay(self):
        @pl.when(self.inner == 1)
        def _():
            self.arrival(2).wait_recv()
            block = 3 - self.place.head
            both = self.prod[block].astype(F32) + self.zin[2].astype(F32)
            self.prod[block] = both.astype(BF16)
            self.copy(2).start()

    def finish(self):
        self.arrival(0).wait_recv()
        self.arrival(1).wait_recv()

        @pl.when(self.inner == 0)
        def _():
            self.arrival(2).wait_recv()

        total = self.prod[self.place.head].astype(F32)
        total = total + self.zin[0].astype(F32) + self.zin[1].astype(F32)
        total = jnp.where(self.inner == 0, total + self.zin[2].astype(F32), total)
        wide, deep = self.job.columns // self.job.fold, self.job.rows
        for i in range(self.job.fold):
            self.done(total[i * deep : (i + 1) * deep], i * wide, wide)
        for number in range(3):
            self.copy(number).wait_send()


def backward_kernel(cfg, names, *refs):
    params, refs = Params(*refs[: len(Params._fields)]), refs[len(Params._fields) :]
    (first_cot, second_cot), refs = refs[:2], refs[2:]
    stored, held = [], []
    for _ in range(LAYERS):
        stored.append(Kept(*refs[: len(Kept._fields)]))
        refs = refs[len(Kept._fields) :]
    out, refs = Grads(*refs[: len(Grads._fields)]), refs[len(Grads._fields) :]
    for _ in range(slots_of(cfg)):
        held.append(Kept(*refs[: len(Kept._fields)]))
        refs = refs[len(Kept._fields) :]
    held = held * (LAYERS // len(held))
    r = gathered(params, out, **dict(zip(names, refs, strict=True)))
    weights = Weights(r, list(reversed(range(LAYERS))))
    weights.fetch(4, 3, 2, 0, 1)

    def saved_load(layer, ref):
        i = [ref is other for other in held[layer]].index(True)
        return pltpu.make_async_copy(stored[layer][i], ref, r.lsem.at[layer, i])

    def fetch(layer):
        k = held[layer]
        for ref in (k.slope, k.lhs_shrink, k.mixed, k.lhs_expand, k.comb, k.joint, k.sorted):
            saved_load(layer, ref).start()
        for ref in (k.rank, k.lhs_mix, k.second, k.lhs_qv):
            saved_load(layer, ref).start()

    for layer in list(reversed(range(LAYERS)))[: slots_of(cfg)]:
        fetch(layer)
    place = Place(cfg)
    place.greet()
    after = fetch if slots_of(cfg) == 1 else None
    backward_layers(cfg, place, r, weights, held, saved_load, after, first_cot, second_cot)


def backward_layers(cfg, place, r, weights, held, saved_load, fetch, first_cot, second_cot, before=None):
    tok, heads, plane, width = cfg.tok, cfg.heads, cfg.plane, cfg.width
    band = heads * tok
    share = cfg.feats // cfg.seq
    base = place.part * cfg.rows
    jobs = jobs_of(cfg)

    def weight(number, layer, left, right):
        out = (r.out_ws, r.out_wm)[number] if number < 2 else r.out_we
        first = max(number - 2, 0) * cfg.feats

        def done(total, start, wide):
            out[layer, :, first + start : first + start + wide] = total

        return Gathered(place, jobs[number], left, right, done, r)

    def attention_weights(layer, left, right):
        def fill(buf):
            for head in range(heads):
                rows = left[head * plane * share : (head + 1) * plane * share, :]
                buf[:, head] = dot(rows, right).reshape(plane, share, 2 * DH).astype(BF16)

        def done(found):
            for head, both in found:
                at = pl.ds(pl.multiple_of(head * DH, DH), DH)
                r.out_wq[layer, :, at] = both[:, :DH].astype(F32)
                r.out_wv[layer, :, at] = both[:, DH:].astype(F32)

        return Unit(place, fill, done, r.qbuf, r.qin, r.qz, r.qsend, r.qrecv)

    def vector_sums(layer):
        def fill(buf):
            deep = cfg.hid // cfg.seq
            for p in range(cfg.seq):
                at = p * share // LANES * LANES
                tile = r.vectors[:, at : at + LANES]
                at = p * deep // LANES * LANES
                line, at = 6 + at // cfg.feats, at % cfg.feats
                extra = r.vectors[line : line + 1, at : at + LANES]
                buf[p % plane, p // plane, 0:6] = tile[0:6]
                buf[p % plane, p // plane, 6:8] = jnp.broadcast_to(extra, (2, LANES))

        def done(found):
            r.out_small[layer] = sum(both for _, both in found)

        return Unit(
            place, fill, done, r.vbuf.at[layer], r.vin.at[layer], r.vz.at[layer], r.vsend.at[layer], r.vrecv.at[layer]
        )

    order = list(reversed(range(LAYERS)))
    late, small, last = None, None, None

    for layer in order:
        one = slice(layer, layer + 1)
        saved = held[layer]

        def arrived(*fields):
            if saved_load is not None:
                for field in fields:
                    saved_load(layer, field).wait()

        second_grad = second_cot if layer == order[0] else r.second_out
        first_grad = first_cot if layer == order[0] else r.first_out
        branch = second_grad[...].astype(BF16)
        arrived(saved.slope, saved.lhs_shrink)
        shrink = weight(0, layer, saved.lhs_shrink, branch)
        shrink.start()
        weights.need(4)
        hidden_grad = (dot_nt(branch, r.ws[...]) * saved.slope[...]).astype(BF16)
        weights.release(4)
        weights.need(3)
        arrived(saved.mixed, saved.lhs_expand)

        def during_two():
            r.vectors[0:1, :] = jnp.sum(branch.astype(F32), axis=0, keepdims=True)
            summed = jnp.sum(hidden_grad.astype(F32), axis=0, keepdims=True)
            for i in range(cfg.hid // cfg.feats):
                r.vectors[6 + i : 7 + i, :] = summed[:, i * cfg.feats : (i + 1) * cfg.feats]
            if late is not None:
                for job in late:
                    job.relay()
                next(last)
            shrink.forward()
            if before is not None and layer == order[0]:
                before()

        expand = [
            weight(2 + i, layer, saved.lhs_expand, hidden_grad[:, i * cfg.feats : (i + 1) * cfg.feats])
            for i in range(cfg.hid // cfg.feats)
        ]
        two_grad = y_sum(
            place,
            r,
            0,
            lambda at: dot_nt(hidden_grad, r.we[at, :]),
            during_two,
            [lambda: weights.release(3), expand[0].start],
        )
        xhat, scale = norm_parts(saved.mixed[...])
        mixed_grad = first_grad[...] + norm_back(xhat, scale, r.forward_gain[one, :], two_grad)
        r.first_out[...] = mixed_grad
        mix_low = mixed_grad.astype(BF16)
        weights.need(2)
        combined_grad = dot_nt(mix_low, r.wm[...]).astype(BF16)
        weights.release(2)
        for head in range(heads):
            r.gs[head] = combined_grad[:, head * DH : (head + 1) * DH]

        def rows_of(spot, head):
            return pl.ds(pl.multiple_of((spot * heads + head) * tok, tok), tok)

        def block(head, spot):
            return r.gtokens.at[rows_of(spot, head), :DH]

        sent = z_exchange(
            cfg,
            place,
            lambda head: r.gs.at[head],
            lambda head: block(head, place.member),
            r.zsend.at[layer],
            r.zrecv.at[layer],
        )
        block(place.head, place.member)[...] = r.gs[place.head]
        r.vectors[1:2, :] = jnp.sum(mix_low.astype(F32), axis=0, keepdims=True)
        r.vectors[2:3, :] = jnp.sum(two_grad * xhat, axis=0, keepdims=True)
        r.vectors[3:4, :] = jnp.sum(two_grad, axis=0, keepdims=True)
        arrived(saved.sorted, saved.rank, saved.comb, saved.joint, saved.lhs_mix)
        rank = saved.rank
        rows = saved.sorted
        mixing = weight(1, layer, saved.lhs_mix, mix_low)
        raw = rows[:, :DH].astype(F32)
        r.keys[...] = (raw * key_scale(raw)).astype(BF16)
        if late is not None:
            for job in late:
                job.finish()
            next(last)
            next(small)
        spread = Doubling(
            place,
            [place.z_source(step) for step in range(heads)],
            block,
            r.gsend.at[layer],
            r.grecv.at[layer],
        )
        for step in range(heads):
            if step > 0:
                spot = block(place.z_source(step), place.member)
                z_arrival(place, spot, r.zrecv.at[layer], step).wait_recv()
            spread.offer(place.z_source(step))
        mine = r.gtokens[pl.ds(pl.multiple_of(place.member * band, band), band), :DH].astype(F32)
        inner = jnp.sum(jnp.transpose(mine * saved.comb[...]), axis=0, keepdims=True)
        line = lax.broadcasted_iota(jnp.int32, (8, band), 0)
        r.arow[layer, place.member] = jnp.where(
            line == 0, saved.joint[...], jnp.broadcast_to(inner, (8, band))
        )
        extras = Doubling(
            place,
            [0],
            lambda key, spot: r.arow.at[layer, spot],
            r.asend.at[layer],
            r.arecv.at[layer],
        )
        extras.offer(0)
        shrink.multiply()
        spread.receive()
        extras.receive()
        expand[0].forward()
        expand[1].start()
        mixing.start()
        if late is not None:
            next(small)
        lines = lax.broadcasted_iota(jnp.int32, (LANES, band), 0)
        for spot in range(plane):
            pieces = split_three(r.arow[layer, spot][0:1]) + split_three(r.arow[layer, spot][1:2])
            table = jnp.zeros((LANES, band), F32)
            for i, piece in enumerate(pieces):
                table = jnp.where(lines == i, piece, table)
            r.gtokens[spot * band : (spot + 1) * band, DH:] = jnp.transpose(table).astype(BF16)

        def store_rows(c, found):
            at = pl.ds(pl.multiple_of(c * 512, 512), 512)
            r.gsorted[at, :] = found[:, :DH].astype(BF16)
            r.stats[at, :] = found[:, DH:]

        sort_rows(cfg, rank, r.gtokens, store_rows, base, 512, cfg.rows // 512)
        r.dq[0:CHUNK, :] = jnp.zeros((CHUNK, DH), F32)
        r.dk[0:CHUNK, :] = jnp.zeros((CHUNK, DH), F32)
        r.dv[0:CHUNK, :] = jnp.zeros((CHUNK, DH), F32)
        mask = window_mask()

        def attend(c):
            at = pl.multiple_of(c * CHUNK, CHUNK)
            own = pl.ds(at + CHUNK, CHUNK)
            window = pl.ds(at, 2 * CHUNK)
            query = rows[own, :DH]
            near = r.keys[window, :]
            grad = r.gsorted[pl.ds(at, CHUNK), :]
            stats = r.stats[pl.ds(at, CHUNK), :]
            joint = stats[:, 0:1] + stats[:, 1:2] + stats[:, 2:3]
            inner = stats[:, 3:4] + stats[:, 4:5] + stats[:, 5:6]
            scores = dot_nt(query, near) / math.sqrt(DH)
            scores = jnp.where(mask, scores, -1000000000.0)
            probs = jnp.exp(scores - joint)
            prob_grad = dot_nt(grad, rows[window, DH:])
            score_grad = (probs * (prob_grad - inner) / math.sqrt(DH)).astype(BF16)
            r.dq[own, :] = dot(score_grad, near)
            return dot_tn(score_grad, query), dot_tn(probs.astype(BF16), grad)

        def attend_some(i, _):
            parts = [attend(i * UNROLL + u) for u in range(UNROLL)]
            for ref, found in zip((r.dk, r.dv), zip(*parts)):
                for u in range(UNROLL):
                    at = pl.multiple_of((i * UNROLL + u) * CHUNK, CHUNK)
                    if u == 0:
                        before = pl.ds(at, CHUNK)
                        ref[before, :] = ref[before, :] + found[u][:CHUNK]
                    own = found[u][CHUNK:]
                    if u + 1 < UNROLL:
                        own = own + found[u + 1][:CHUNK]
                    ref[pl.ds(at + CHUNK, CHUNK), :] = own
            return 0

        rounds = cfg.rows // CHUNK // UNROLL
        lax.fori_loop(0, rounds // 2, attend_some, 0)
        shrink.relay()
        expand[0].multiply()
        expand[1].forward()
        lax.fori_loop(rounds // 2, rounds, attend_some, 0)
        if cfg.parts == 1:
            last = slice(cfg.rows, cfg.ext)
            r.dk[last, :] = r.dk[last, :] + r.dk[0:CHUNK, :]
            r.dv[last, :] = r.dv[last, :] + r.dv[0:CHUNK, :]
        raw = rows[:, :DH].astype(F32)
        scale = key_scale(raw)
        dk = r.dk[...]
        inner = jnp.mean(raw * dk, axis=-1, keepdims=True)
        r.grads[:, :DH] = (
            r.dq[...] + scale * dk - raw * (scale * scale * scale * inner)
        ).astype(BF16)
        r.grads[:, DH:] = r.dv[...].astype(BF16)
        skip = CHUNK if cfg.parts == 1 else 0

        def unsort(spot):
            start = base if cfg.parts == 1 else base + cfg.total - CHUNK
            pick = unsort_pick(cfg, rank, spot, start, cfg.ext - skip)
            r.part[spot] = dot(pick, r.grads[skip:, :]).astype(BF16)

        def pass_part(k, spot):
            return remote(
                r.part.at[spot],
                r.part_in.at[place.landing(k, spot)],
                r.psend.at[layer, k, spot],
                r.precv.at[layer, k, spot // 2 ** (k + 1)],
                place.bit_peer(k),
            )

        def first_half(i, _):
            unsort(place.given(0, i))
            pass_part(0, place.given(0, i)).start()
            return 0

        def second_half(i, _):
            unsort(place.kept(0, i))
            return 0

        lax.fori_loop(0, place.group(0), first_half, 0)
        lax.fori_loop(0, place.group(0), second_half, 0)

        def merge(k, spot):
            pass_part(k, spot).wait_recv()
            other = r.part_in[place.landing(k, spot)]
            return (r.part[spot].astype(F32) + other.astype(F32)).astype(BF16)

        for k in range(cfg.bits - 1):
            for giving in (True, False):
                for i in range(place.group(k + 1)):
                    spot = place.given(k + 1, i) if giving else place.kept(k + 1, i)
                    r.part[spot] = merge(k, spot)
                    if giving:
                        pass_part(k + 1, spot).start()
        spread.finish()
        extras.finish()
        shrink.finish()
        expand[0].relay()
        mixing.forward()
        merged = merge(cfg.bits - 1, place.member)
        for head in range(heads):
            r.home_out[head] = merged[head * tok : (head + 1) * tok]
        back = z_exchange(
            cfg,
            place,
            lambda head: r.home_out.at[head],
            lambda head: r.home_in.at[head],
            r.csend.at[layer],
            r.crecv.at[layer],
        )
        r.home_in[place.head] = r.home_out[place.head]
        arrived(saved.second, saved.lhs_qv)
        last = attention_weights(layer, saved.lhs_qv, merged)
        last.start()
        last = last.fold()
        weights.need(0, 1)
        xhat, scale = norm_parts(saved.second[...])
        expand[0].finish()
        next(last)
        for step in range(1, heads):
            spot = r.home_in.at[place.z_source(step)]
            z_arrival(place, spot, r.crecv.at[layer], step).wait_recv()
        query_grad = jnp.concatenate([r.home_in[head][:, :DH] for head in range(heads)], axis=1)
        value_grad = jnp.concatenate([r.home_in[head][:, DH:] for head in range(heads)], axis=1)
        one_grad = dot_nt(query_grad, r.wq[...]) + dot_nt(value_grad, r.wv[...])
        weights.release(0, 1)
        r.vys[0:1, :] = jnp.sum(one_grad * xhat, axis=0, keepdims=True)
        r.vys[1:2, :] = jnp.sum(one_grad, axis=0, keepdims=True)
        edge = remote(r.vys, r.vyr, r.vysem.at[0], r.vysem.at[1], place.y_peer())
        edge.start()
        small = vector_sums(layer)

        late = [expand[1], mixing]

        def during_one():
            for copy in sent + back:
                copy.wait_send()
            for k in range(cfg.bits):
                for i in range(place.group(k)):
                    pass_part(k, place.given(k, i)).wait_send()
            edge.wait()
            r.vectors[4:6, :] = r.vys[0:2, :] + r.vyr[0:2, :]
            small.start()

        partial = one_grad
        one_grad = y_sum(
            place, r, 1, lambda at: partial[:, at], during_one, [job.multiply for job in late]
        )
        dx = norm_back(xhat, scale, r.attention_gain[one, :], one_grad)
        r.second_out[...] = second_grad[...] + dx
        small = small.fold()
        next(small)
        if layer > 0 and fetch is not None:
            fetch(layer - 1)
    for job in late:
        job.relay()
    next(last)
    next(small)
    for job in late:
        job.finish()
    next(last)
    next(small)


def grad_shapes(cfg):
    tok, feats = cfg.tok, cfg.feats
    share = feats // cfg.seq
    return Grads(
        first_out=(tok, feats),
        second_out=(tok, feats),
        out_wq=(LAYERS, share, cfg.width),
        out_wv=(LAYERS, share, cfg.width),
        out_wm=(LAYERS, cfg.width // cfg.seq, feats),
        out_we=(LAYERS, share, cfg.hid),
        out_ws=(LAYERS, cfg.hid // cfg.seq, feats),
        out_small=(LAYERS, 8, LANES),
    )


def backward_call(cfg, params, cotangents, saved):
    scratch = common_scratch(cfg) | backward_scratch(cfg)
    shapes = grad_shapes(cfg)
    whole = pl.BlockSpec(memory_space=pltpu.VMEM)
    apart = pl.BlockSpec(memory_space=pl.ANY)
    specs = Params(*[apart] * len(params))._replace(attention_gain=whole, forward_gain=whole)
    held = [pltpu.VMEM(*shape) for shape in saved_shapes(cfg)] * slots_of(cfg)
    outs = pl.pallas_call(
        functools.partial(backward_kernel, cfg, list(scratch)),
        out_shape=[jax.ShapeDtypeStruct(shape, F32) for shape in shapes],
        in_specs=list(specs) + [whole] * 2 + [apart] * (LAYERS * len(Kept._fields)),
        out_specs=[whole] * len(shapes),
        scratch_shapes=held + list(scratch.values()),
        compiler_params=pltpu.CompilerParams(
            collective_id=LAYERS, has_side_effects=True, vmem_limit_bytes=VMEM_LIMIT
        ),
        name="backward",
    )(*params, *cotangents, *[array for kept in saved for array in kept])
    return Grads(*outs)


def whole_kernel(cfg, common, forth, sems, back, *refs):
    sources, refs = refs[: IN_COUNT + 2], refs[IN_COUNT + 2 :]
    targets, refs = refs[: 2 + len(Grads._fields)], refs[2 + len(Grads._fields) :]
    inputs, refs = list(refs[: IN_COUNT + 2]), refs[IN_COUNT + 2 :]
    result_two, out = refs[0], Grads(*refs[1 : 1 + len(Grads._fields)])
    refs = refs[1 + len(Grads._fields) :]
    in_sem, out_sem, refs = refs[0], refs[1], refs[2:]
    held = []
    for _ in range(LAYERS):
        held.append(Kept(*refs[: len(Kept._fields)]))
        refs = refs[len(Kept._fields) :]
    shared, refs = dict(zip(common, refs)), refs[len(common) :]
    ahead, refs = dict(zip(forth, refs)), refs[len(forth) :]
    signals, refs = dict(zip(sems, refs)), refs[len(sems) :]
    loads = []
    for i, source in enumerate(sources):
        if i in apart_inputs():
            inputs[i] = source
        else:
            loads.append(pltpu.make_async_copy(source, inputs[i], in_sem.at[i]))
    for load in loads:
        load.start()
    streams, params = Streams(*inputs[:3]), Params(*inputs[3:IN_COUNT])
    place = Place(cfg)
    weights, before = None, None
    first, second = streams.first, streams.second
    held[0] = held[0]._replace(second=second)
    for layer in range(LAYERS):
        r = gathered(held[layer], params, **shared, **ahead)
        vars(r).update({name: ref.at[layer] for name, ref in signals.items()})
        r.first, r.buckets = first, streams.buckets
        r.renewed = result_two if layer == LAYERS - 1 else held[layer + 1].second
        if weights is None:
            weights = Weights(r, [0, 1, 0])
            weights.fetch(*range(5))
            for load in loads:
                load.wait()
        before = forward_layer(cfg, place, layer, r, weights, layer == 0, before)
        first, second = r.mixed, r.renewed
    stores = [
        pltpu.make_async_copy(source, target, out_sem.at[i])
        for i, (source, target) in enumerate(zip((first, second) + tuple(out), targets))
    ]
    for store in stores[:2]:
        store.start()
    r = gathered(params, out, **shared, **dict(zip(back, refs, strict=True)))
    backward_layers(cfg, place, r, weights, held, None, None, *inputs[IN_COUNT:], before)
    for store in stores[2:]:
        store.start()
    for store in stores:
        store.wait()


def apart_inputs():
    names = Streams._fields + Params._fields
    return [i for i, name in enumerate(names) if name.endswith("_hbm")]


def whole_call(cfg, streams, cotangents, params):
    common, forth, back = common_scratch(cfg), forward_scratch(cfg), backward_scratch(cfg)
    sems = forward_sems(cfg, LAYERS)
    apart = pl.BlockSpec(memory_space=pl.ANY)
    unused, shapes = ((8, LANES), F32), saved_shapes(cfg)
    held = [shapes._replace(second=unused)] + [shapes] * (LAYERS - 1)
    held = [pltpu.VMEM(*shape) for kept in held for shape in kept]
    operands = (*streams, *params, *cotangents)
    inputs = [
        pltpu.VMEM(*(unused if i in apart_inputs() else (array.shape, array.dtype)))
        for i, array in enumerate(operands)
    ]
    results = [(cfg.tok, cfg.feats)] * 2 + list(grad_shapes(cfg))
    dma = pltpu.SemaphoreType.DMA
    scratch = inputs + [pltpu.VMEM(shape, F32) for shape in results[1:]]
    scratch += [dma((len(inputs),)), dma((len(results),))] + held
    scratch += [value for part in (common, forth, sems, back) for value in part.values()]
    outs = pl.pallas_call(
        functools.partial(whole_kernel, cfg, list(common), list(forth), list(sems), list(back)),
        out_shape=[jax.ShapeDtypeStruct(shape, F32) for shape in results],
        in_specs=[apart] * len(operands),
        out_specs=[apart] * len(results),
        scratch_shapes=scratch,
        compiler_params=pltpu.CompilerParams(
            collective_id=0, has_side_effects=True, vmem_limit_bytes=VMEM_LIMIT
        ),
        name="whole",
    )(*operands)
    return outs[0], outs[1], Grads(*outs[2:])


def finish_kernel(cfg, count, *refs):
    sources, refs = refs[: count + 1], refs[count + 1 :]
    targets, refs = refs[: count + 7], refs[count + 7 :]
    halfway, refs = refs[: count + 1], refs[count + 1 :]
    pieces, sem = refs[:7], refs[7]

    def leg(number, i):
        ends = (sources[i], halfway[i]) if number == 0 else (halfway[i], targets[i])
        return pltpu.make_async_copy(*ends, sem.at[number, i])

    def small_leg(line):
        return pltpu.make_async_copy(pieces[line], targets[count + line], sem.at[1, count + line])

    for i in reversed(range(count + 1)):
        leg(0, i).start()
    leg(0, count).wait()
    index = lax.axis_index("seq")
    for line, piece in enumerate(pieces):
        share = piece.shape[1]
        tile = halfway[count][:, line, :]
        found = jnp.zeros(piece.shape, F32)
        for k in range(LANES // share):
            here = index % (LANES // share) == k
            found = jnp.where(here, tile[:, k * share : (k + 1) * share], found)
        piece[...] = found
        small_leg(line).start()
    for i in reversed(range(count)):
        leg(0, i).wait()
        leg(1, i).start()
    for line in range(7):
        small_leg(line).wait()
    for i in range(count):
        leg(1, i).wait()


def finish_call(cfg, small, arrays):
    apart = pl.BlockSpec(memory_space=pl.ANY)
    count = len(arrays)
    shapes = [(LAYERS, cfg.feats // cfg.seq)] * 6 + [(LAYERS, cfg.hid // cfg.seq)]
    halfway = [array.shape for array in arrays] + [small.shape]
    outs = pl.pallas_call(
        functools.partial(finish_kernel, cfg, count),
        out_shape=[jax.ShapeDtypeStruct(shape, F32) for shape in halfway[:-1] + shapes],
        in_specs=[apart] * (count + 1),
        out_specs=[apart] * (count + 7),
        scratch_shapes=[pltpu.VMEM(shape, F32) for shape in halfway + shapes]
        + [pltpu.SemaphoreType.DMA((2, count + 7))],
        compiler_params=pltpu.CompilerParams(vmem_limit_bytes=VMEM_LIMIT),
        name="finish",
    )(*arrays, small)
    return outs[:count], outs[count:]


def shards(stream_one, stream_two, cotangent_one, cotangent_two, bucket_numbers, *params):
    cfg = sizes_of(lax.axis_size("seq"), stream_one, params[0], params[4])
    params = Params(*params)
    first, second = stream_one, stream_two
    if cfg.parts == 1:
        streams = Streams(first, second, bucket_numbers)
        first, second, out = whole_call(cfg, streams, (cotangent_one, cotangent_two), params)
    else:
        saved = []
        for layer in range(LAYERS):
            kept = forward_call(cfg, layer, Streams(first, second, bucket_numbers), params)
            saved.append(kept._replace(second=second))
            first, second = kept.mixed, kept.second
        out = backward_call(cfg, params, (cotangent_one, cotangent_two), saved)
    arrays = (first, second) + tuple(out)[:-1]
    (first, second, one, two, wq, wv, wm, we, ws), small = finish_call(cfg, out.out_small, arrays)
    return (
        first,
        second,
        one,
        two,
        wq,
        wv,
        wm,
        small[1],
        we,
        small[6],
        ws,
        small[0],
        small[4],
        small[5],
        small[2],
        small[3],
    )


def solution(mesh):
    in_specs = (
        P("seq", None),
        P("seq", None),
        P("seq", None),
        P("seq", None),
        P(None, None, "mp", None),
        P(None, None, "mp"),
        P(None, None, "mp"),
        P(None, "mp", None),
        P(),
        P(None, None, "mp"),
        P(None, "mp"),
        P(None, "mp", None),
        P(),
        P(),
        P(),
        P(),
        P(),
    )
    out_specs = (
        P("seq", None),
        P("seq", None),
        P("seq", None),
        P("seq", None),
        P(None, "seq", "mp"),
        P(None, "seq", "mp"),
        P(None, ("mp", "seq"), None),
        P(None, "seq"),
        P(None, "seq", "mp"),
        P(None, ("mp", "seq")),
        P(None, ("mp", "seq"), None),
        P(None, "seq"),
        P(None, "seq"),
        P(None, "seq"),
        P(None, "seq"),
        P(None, "seq"),
    )
    return jax.shard_map(shards, mesh=mesh, in_specs=in_specs, out_specs=out_specs, check_vma=False)
```

```python
import functools
import math
from types import SimpleNamespace
from typing import NamedTuple

import jax
import jax.numpy as jnp
from jax import lax
from jax.experimental import pallas as pl
from jax.experimental.pallas import tpu as pltpu
from jax.sharding import PartitionSpec as P

DH = 128
SPAN = 64
ROUNDS = 4
LAYERS = 2
LANES = 128
CHUNK = 128
UNROLL = 8
MESH = pl.DeviceIdType.MESH
F32 = jnp.float32
BF16 = jnp.bfloat16
AWAY = -1e30
VMEM_LIMIT = 62 << 20


class Sizes(NamedTuple):
    seq: int
    tok: int
    heads: int
    plane: int
    bits: int
    parts: int
    total: int
    rows: int
    ext: int
    buckets: int
    feats: int
    width: int
    hid: int


def sizes_of(seq, stream, query_weight, expand_weight):
    tok, feats = stream.shape
    width = query_weight.shape[2]
    heads = width // DH
    plane = seq // heads
    parts = plane // ROUNDS
    total = seq * tok
    rows = total // parts
    return Sizes(
        seq,
        tok,
        heads,
        plane,
        plane.bit_length() - 1,
        parts,
        total,
        rows,
        rows + CHUNK,
        total // SPAN,
        feats,
        width,
        expand_weight.shape[2],
    )


def dot(left, right):
    return lax.dot_general(left, right, (((1,), (0,)), ((), ())), preferred_element_type=F32)


def dot_nt(left, right):
    return lax.dot_general(left, right, (((1,), (1,)), ((), ())), preferred_element_type=F32)


def dot_tn(left, right):
    return lax.dot_general(left, right, (((0,), (0,)), ((), ())), preferred_element_type=F32)


def norm_parts(values):
    center = values - jnp.mean(values, axis=-1, keepdims=True)
    scale = lax.rsqrt(jnp.mean(center * center, axis=-1, keepdims=True) + 1e-05)
    return center * scale, scale


def norm_back(xhat, scale, gain, grad):
    t = grad * gain
    inner = t - jnp.mean(t, axis=-1, keepdims=True) - xhat * jnp.mean(t * xhat, axis=-1, keepdims=True)
    return scale * inner


def key_scale(keys):
    return lax.rsqrt(jnp.mean(keys * keys, axis=-1, keepdims=True) + 1e-06)


def rows_to_columns(rows):
    return jnp.transpose(jnp.broadcast_to(rows, (LANES, rows.shape[1])))


def split_three(values):
    high = values.astype(BF16).astype(F32)
    rest = values - high
    middle = rest.astype(BF16).astype(F32)
    return high, middle, rest - middle


class Place:
    def __init__(self, cfg):
        self.cfg = cfg
        self.index = lax.axis_index("seq")
        self.half = lax.axis_index("mp")
        self.head = self.index // cfg.plane
        self.member = self.index % cfg.plane
        self.round = self.member // cfg.parts
        self.part = self.member % cfg.parts

    def bit(self, k):
        return (self.member // 2**k) % 2

    def z_peer(self, step):
        head = (self.head + step) % self.cfg.heads
        return head, (head * self.cfg.plane + self.member, self.half)

    def z_source(self, step):
        return (self.head + self.cfg.heads - step) % self.cfg.heads

    def bit_peer(self, k):
        return (self.index + (1 - 2 * self.bit(k)) * 2**k, self.half)

    def y_peer(self):
        return (self.index, 1 - self.half)

    def kept(self, k, i):
        return 2 ** (k + 1) * i + self.member % 2 ** (k + 1)

    def given(self, k, i):
        return 2 ** (k + 1) * i + (1 - self.bit(k)) * 2**k + self.member % 2**k

    def landing(self, k, spot):
        return self.cfg.plane - self.cfg.plane // 2**k + spot // 2 ** (k + 1)

    def group(self, k):
        return self.cfg.plane // 2 ** (k + 1)

    def plane_peer(self, step):
        member = (self.member + step) % self.cfg.plane
        return member, (self.head * self.cfg.plane + member, self.half)

    def greet(self):
        barrier = pltpu.get_barrier_semaphore()
        peers = [self.z_peer(step)[1] for step in range(1, self.cfg.heads)]
        peers += [self.plane_peer(step)[1] for step in range(1, self.cfg.plane)]
        peers += [self.y_peer()]
        for peer in peers:
            pl.semaphore_signal(barrier, inc=1, device_id=peer, device_id_type=MESH)
        pl.semaphore_wait(barrier, len(peers))


def remote(src, dst, send, recv, peer):
    return pltpu.make_async_remote_copy(
        src_ref=src, dst_ref=dst, send_sem=send, recv_sem=recv, device_id=peer, device_id_type=MESH
    )


def rank_rows(cfg, bucket_row, rank_ref):
    count = cfg.buckets
    ids = lax.broadcasted_iota(jnp.int32, (count, LANES), 0)
    ahead = (
        lax.broadcasted_iota(jnp.int32, (LANES, LANES), 0)
        < lax.broadcasted_iota(jnp.int32, (LANES, LANES), 1)
    ).astype(BF16)
    lower = (
        lax.broadcasted_iota(jnp.int32, (count, count), 1)
        < lax.broadcasted_iota(jnp.int32, (count, count), 0)
    ).astype(BF16)
    marks = [
        (bucket_row[:, p * LANES : (p + 1) * LANES] == ids).astype(F32) for p in range(cfg.seq)
    ]
    totals = sum(marks)
    totals = jnp.broadcast_to(jnp.sum(totals, axis=1, keepdims=True), (count, LANES))
    carry = dot(lower, totals.astype(BF16))
    for p in range(cfg.seq):
        within = dot(marks[p].astype(BF16), ahead)
        rank = jnp.sum(marks[p] * (within + carry), axis=0, keepdims=True)
        carry = carry + jnp.broadcast_to(jnp.sum(marks[p], axis=1, keepdims=True), (count, LANES))
        spot = (p % cfg.plane) * cfg.heads + p // cfg.plane
        rank_ref[:, spot * LANES : (spot + 1) * LANES] = jnp.broadcast_to(
            rank.astype(jnp.int32), (8, LANES)
        )


def sort_rows(cfg, rank_ref, source_ref, store, start, size, chunks):
    step = min(cfg.total, 2048)

    def body(c, _):
        spots = start + c * size + lax.broadcasted_iota(jnp.int32, (size, step), 0)
        spots = spots % cfg.total if cfg.parts > 1 else spots
        found = None
        for k in range(cfg.total // step):
            ranks = rank_ref[0:1, k * step : (k + 1) * step]
            pick = (spots == ranks).astype(BF16)
            part = dot(pick, source_ref[k * step : (k + 1) * step, :])
            found = part if found is None else found + part
        store(c, found)
        return 0

    lax.fori_loop(0, chunks, body, 0)


def several(step, count):
    unroll = 2 * UNROLL

    def body(c, _):
        for i in range(unroll):
            step(c * unroll + i)
        return 0

    lax.fori_loop(0, count // unroll, body, 0)


def window_mask():
    row = lax.broadcasted_iota(jnp.int32, (CHUNK, 2 * CHUNK), 0)
    column = lax.broadcasted_iota(jnp.int32, (CHUNK, 2 * CHUNK), 1)
    gap = column // SPAN - row // SPAN
    near = jnp.logical_or(gap == 1, gap == 2)
    return jnp.logical_and(near, column != row + CHUNK)


def z_exchange(cfg, place, source, target, send, recv):
    copies = []
    for step in range(1, cfg.heads):
        head, peer = place.z_peer(step)
        copy = remote(source(head), target(place.head), send.at[step], recv.at[step], peer)
        copy.start()
        copies.append(copy)
    return copies


def z_arrival(place, block, recv, step):
    return remote(block, block, recv.at[step], recv.at[step], place.z_peer(step)[1])


class Doubling:
    def __init__(self, place, keys, block, send, recv):
        self.place, self.keys, self.block = place, keys, block
        self.send, self.recv = send, recv

    def give(self, key, spot, k):
        return remote(
            self.block(key, spot),
            self.block(key, spot),
            self.send.at[k, key, spot],
            self.recv.at[key, spot],
            self.place.bit_peer(k),
        )

    def offer(self, key):
        for k in range(self.place.cfg.bits):
            self.give(key, self.place.member, k).start()

    def spots(self):
        for k in reversed(range(self.place.cfg.bits)):
            for key in self.keys:
                for i in range(self.place.group(k)):
                    yield k, key, self.place.given(k, i)

    def receive_bit(self, k):
        for key in self.keys:
            for i in range(self.place.group(k)):
                spot = self.place.given(k, i)
                self.give(key, spot, k).wait_recv()
                for low in range(k):
                    self.give(key, spot, low).start()

    def receive(self):
        for k in reversed(range(self.place.cfg.bits)):
            self.receive_bit(k)

    def finish(self):
        for key in self.keys:
            for k in range(self.place.cfg.bits):
                self.give(key, self.place.member, k).wait_send()
        for k, key, spot in self.spots():
            for low in range(k):
                self.give(key, spot, low).wait_send()


class Params(NamedTuple):
    wq_hbm: jax.Array
    wv_hbm: jax.Array
    wm_hbm: jax.Array
    mix_bias: jax.Array
    we_hbm: jax.Array
    expand_bias: jax.Array
    ws_hbm: jax.Array
    shrink_bias: jax.Array
    attention_gain: jax.Array
    attention_shift: jax.Array
    forward_gain: jax.Array
    forward_shift: jax.Array


class Streams(NamedTuple):
    first: jax.Array
    second: jax.Array
    buckets: jax.Array


class Kept(NamedTuple):
    mixed: jax.Array
    sorted: jax.Array
    comb: jax.Array
    joint: jax.Array
    slope: jax.Array
    rank: jax.Array
    lhs_qv: jax.Array
    lhs_expand: jax.Array
    lhs_shrink: jax.Array
    lhs_mix: jax.Array
    second: jax.Array


class Grads(NamedTuple):
    first_out: jax.Array
    second_out: jax.Array
    out_wq: jax.Array
    out_wv: jax.Array
    out_wm: jax.Array
    out_we: jax.Array
    out_ws: jax.Array
    out_small: jax.Array


def gathered(*groups, **scratch):
    merged = {}
    for group in groups:
        merged.update(group._asdict())
    return SimpleNamespace(**merged, **scratch)


def common_scratch(cfg):
    dma = pltpu.SemaphoreType.DMA
    return dict(
        wq=pltpu.VMEM((cfg.feats, cfg.width), BF16),
        wv=pltpu.VMEM((cfg.feats, cfg.width), BF16),
        wm=pltpu.VMEM((cfg.width, cfg.feats), BF16),
        we=pltpu.VMEM((cfg.feats, cfg.hid), BF16),
        ws=pltpu.VMEM((cfg.hid, cfg.feats), BF16),
        ys=pltpu.VMEM((2, cfg.tok, cfg.feats), BF16),
        yr=pltpu.VMEM((2, cfg.tok, cfg.feats), BF16),
        wsem=dma((5,)),
        ysend=dma((2, 2)),
        yrecv=dma((2, 2)),
        wm_other=pltpu.VMEM((cfg.width, cfg.feats), BF16),
        low_own=pltpu.VMEM((cfg.tok, cfg.width), BF16),
        low_other=pltpu.VMEM((cfg.tok, cfg.width), BF16),
        msend=dma((2,)),
        mrecv=dma((2,)),
    )


class Weights:
    def __init__(self, r, layers):
        self.pairs = (
            (r.wq_hbm, r.wq),
            (r.wv_hbm, r.wv),
            (r.wm_hbm, r.wm),
            (r.we_hbm, r.we),
            (r.ws_hbm, r.ws),
        )
        self.sem, self.layers = r.wsem, layers
        self.turn, self.flying = [0] * 5, [False] * 5
        self.rest = (lambda: None, lambda: None)

    def copy(self, i):
        source, target = self.pairs[i]
        return pltpu.make_async_copy(source.at[self.layers[self.turn[i]]], target, self.sem.at[i])

    def fetch(self, *numbers):
        for i in numbers:
            self.copy(i).start()
            self.flying[i] = True

    def need(self, *numbers):
        for i in numbers:
            if self.flying[i]:
                self.copy(i).wait()
                self.flying[i] = False

    def release(self, *numbers):
        for i in numbers:
            if self.turn[i] + 1 < len(self.layers):
                self.turn[i] += 1
                self.fetch(i)


def forward_scratch(cfg):
    tok, heads, plane, bits = cfg.tok, cfg.heads, cfg.plane, cfg.bits
    band = heads * tok
    return dict(
        zs=pltpu.VMEM((heads, tok, 2 * DH), BF16),
        tokens=pltpu.VMEM((cfg.total, 2 * DH), BF16),
        keys=pltpu.VMEM((cfg.ext, DH), BF16),
        attended=pltpu.VMEM((cfg.rows, 3 * DH), BF16),
        part=pltpu.VMEM((plane, band, DH), F32),
        lrow=pltpu.VMEM((plane, 8, band), F32),
        part_in=pltpu.VMEM((plane, band, DH), F32),
        lrow_in=pltpu.VMEM((plane, 8, band), F32),
        low_out=pltpu.VMEM((heads, tok, DH), BF16),
        low_in=pltpu.VMEM((heads, tok, DH), BF16),
        normed_t=pltpu.VMEM((cfg.feats, tok), BF16),
        turned_expand=turned_of(cfg, cfg.feats),
        turned_shrink=turned_of(cfg, cfg.hid),
        turned_mix=turned_of(cfg, cfg.width),
    )


def forward_sems(cfg, layers):
    heads, plane, bits = cfg.heads, cfg.plane, cfg.bits
    shapes = dict(
        zsend=(heads,),
        zrecv=(heads,),
        gsend=(bits, heads, plane),
        grecv=(heads, plane),
        psend=(bits, plane, 2),
        precv=(bits, plane, 2),
        csend=(heads,),
        crecv=(heads,),
        nsend=(2, heads),
        nrecv=(2, heads),
        tsend=(4, plane),
        trecv=(4, plane),
    )
    return {name: pltpu.SemaphoreType.DMA((layers,) + shape) for name, shape in shapes.items()}


class Turned:
    def __init__(self, place, number, values, source, target, r):
        self.place, self.source, self.target = place, source, target
        self.send, self.recv = r.tsend.at[number], r.trecv.at[number]
        source[...] = jnp.transpose(values).reshape(source.shape).astype(source.dtype)

    def slot(self, member):
        tok = self.place.cfg.tok
        return self.target.at[:, :, pl.ds(pl.multiple_of(member * tok, tok), tok)]

    def copy(self, step):
        member, peer = self.place.plane_peer(step)
        return remote(
            self.source.at[:, member], self.slot(self.place.member), self.send.at[step], self.recv.at[step], peer
        )

    def start(self):
        for step in range(1, self.place.cfg.plane):
            self.copy(step).start()
        self.slot(self.place.member)[...] = self.source[:, self.place.member]

    def finish(self):
        cfg = self.place.cfg
        for step in range(1, cfg.plane):
            self.copy(step).wait_send()
            arrived = self.slot((self.place.member + cfg.plane - step) % cfg.plane)
            remote(arrived, arrived, self.send.at[step], self.recv.at[step], self.place.y_peer()).wait_recv()


def y_sum(place, r, slot, partial, meanwhile=None, first=()):
    wide = r.ys.shape[2] // 2
    copies = []
    for c in range(2):
        at = slice(c * wide, (c + 1) * wide)
        r.ys[slot, :, at] = partial(at).astype(BF16)
        mine, theirs = r.ys.at[slot, :, at], r.yr.at[slot, :, at]
        copies.append(remote(mine, theirs, r.ysend.at[slot, c], r.yrecv.at[slot, c], place.y_peer()))
        copies[-1].start()
    for step in first:
        step()
    if meanwhile is not None:
        meanwhile()
    for copy in copies:
        copy.wait()
    return r.ys[slot].astype(F32) + r.yr[slot].astype(F32)


def forward_kernel(cfg, layer, names, sems, *refs):
    inputs, refs = refs[:IN_COUNT], refs[IN_COUNT:]
    streams, params = Streams(*inputs[:3]), Params(*inputs[3:])
    out, refs = Kept(*refs[: len(Kept._fields)]), refs[len(Kept._fields) :]
    r = gathered(out, streams, params, **dict(zip(names, refs)))
    vars(r).update({name: ref.at[0] for name, ref in zip(sems, refs[len(names) :])})
    r.second, r.renewed = streams.second, out.second
    weights = Weights(r, [layer])
    weights.fetch(0, 1)
    for step in forward_layer(cfg, Place(cfg), layer, r, weights, True):
        step()


def forward_layer(cfg, place, layer, r, weights, first, before=None):
    tok, heads = cfg.tok, cfg.heads
    band = heads * tok
    one = slice(layer, layer + 1)
    normed = norm_parts(r.second[...])[0] * r.attention_gain[one, :] + r.attention_shift[one, :]
    normed = normed.astype(BF16)
    weights.need(0, 1)
    queries = dot(normed, r.wq[...]).astype(BF16)
    values = dot(normed, r.wv[...]).astype(BF16)
    if first:
        weights.release(0, 1)
        weights.fetch(2)
    for head in range(heads):
        r.zs[head, :, :DH] = queries[:, head * DH : (head + 1) * DH]
        r.zs[head, :, DH:] = values[:, head * DH : (head + 1) * DH]

    def block(head, spot):
        return r.tokens.at[pl.ds(pl.multiple_of((spot * heads + head) * tok, tok), tok), :]

    if first:
        place.greet()
    sent = z_exchange(
        cfg,
        place,
        lambda head: r.zs.at[head],
        lambda head: block(head, place.member),
        r.zsend,
        r.zrecv,
    )
    block(place.head, place.member)[...] = r.zs[place.head]
    if first:
        weights.rest[0]()
        weights.fetch(3, 4)
    weights.need(2)
    swapped = remote(r.wm, r.wm_other, r.msend.at[0], r.mrecv.at[0], place.y_peer())
    swapped.start()
    if before is not None:
        before[0]()
    r.normed_t[...] = jnp.transpose(normed)

    def column(head, half=None):
        deep = cfg.feats // 2
        rows = slice(None) if half is None else slice(half * deep, (half + 1) * deep)
        return r.lhs_qv.at[rows, pl.ds(pl.multiple_of(head * tok, tok), tok)]

    def pass_normed(half):
        deep = cfg.feats // 2
        return z_exchange(
            cfg,
            place,
            lambda head: r.normed_t.at[half * deep : (half + 1) * deep],
            lambda head: column(head, half),
            r.nsend.at[half],
            r.nrecv.at[half],
        )

    column(place.head)[...] = r.normed_t[...]
    if first:
        weights.rest[1]()
    rank_rows(cfg, r.buckets[layer, place.round, pl.ds(place.head, 1), :], r.rank)

    spread = Doubling(
        place, [place.z_source(step) for step in range(heads)], block, r.gsend, r.grecv
    )
    for step in range(heads):
        if step > 0:
            z_arrival(place, block(place.z_source(step), place.member), r.zrecv, step).wait_recv()
        spread.offer(place.z_source(step))
    spread.receive()
    if before is not None:
        before[1]()
    sent += pass_normed(0)
    base = place.part * cfg.rows

    def store_rows(c, found):
        r.sorted[pl.ds(pl.multiple_of(CHUNK + c * 512, CHUNK), 512), :] = found.astype(BF16)

    def store_halo(c, found):
        r.sorted[0:CHUNK, :] = found.astype(BF16)

    sort_rows(cfg, r.rank, r.tokens, store_rows, base, 512, cfg.rows // 512)
    if cfg.parts == 1:
        r.sorted[0:CHUNK, :] = r.sorted[cfg.rows : cfg.ext, :]
    else:
        sort_rows(cfg, r.rank, r.tokens, store_halo, base + cfg.total - CHUNK, CHUNK, 1)
    raw = r.sorted[:, :DH].astype(F32)
    r.keys[...] = (raw * key_scale(raw)).astype(BF16)
    mask = window_mask()
    lane = lax.broadcasted_iota(jnp.int32, (CHUNK, LANES), 1)

    def attend(c):
        at = pl.multiple_of(c * CHUNK, CHUNK)
        query = r.sorted[pl.ds(at + CHUNK, CHUNK), :DH]
        scores = dot_nt(query, r.keys[pl.ds(at, 2 * CHUNK), :]) / math.sqrt(DH)
        scores = jnp.where(mask, scores, -1000000000.0)
        peak = jnp.max(scores, axis=-1, keepdims=True)
        powers = jnp.exp(scores - peak)
        summed = jnp.sum(powers, axis=-1, keepdims=True)
        weights = (powers / summed).astype(BF16)
        output = dot(weights, r.sorted[pl.ds(at, 2 * CHUNK), DH:])
        high, middle, low = split_three(peak + jnp.log(summed))
        extra = jnp.where(lane == 0, high, 0.0)
        extra = jnp.where(lane == 1, middle, extra)
        extra = jnp.where(lane == 2, low, extra)
        extra = jnp.where(lane == 3, 1.0, extra)
        r.attended[pl.ds(at, CHUNK), :DH] = output.astype(BF16)
        r.attended[pl.ds(at, CHUNK), DH : 2 * DH] = (
            output - output.astype(BF16).astype(F32)
        ).astype(BF16)
        r.attended[pl.ds(at, CHUNK), 2 * DH :] = extra.astype(BF16)

    several(attend, cfg.rows // CHUNK)
    spread.finish()

    def unsort(spot):
        pick = unsort_pick(cfg, r.rank, spot, base, cfg.rows)
        found = dot(pick, r.attended[:, : 2 * DH])
        r.part[spot] = found[:, :DH] + found[:, DH:]
        extra = jnp.transpose(dot(pick, r.attended[:, 2 * DH :]))
        row = extra[0:1] + extra[1:2] + extra[2:3] + (1.0 - extra[3:4]) * AWAY
        r.lrow[spot] = jnp.broadcast_to(row, (8, band))

    def pass_part(k, spot):
        peer = place.bit_peer(k)
        return [
            remote(
                mine.at[spot],
                theirs.at[place.landing(k, spot)],
                r.psend.at[k, spot, i],
                r.precv.at[k, spot, i],
                peer,
            )
            for i, (mine, theirs) in enumerate(((r.part, r.part_in), (r.lrow, r.lrow_in)))
        ]

    def first_half(i, _):
        unsort(place.given(0, i))
        for copy in pass_part(0, place.given(0, i)):
            copy.start()
        return 0

    def second_half(i, _):
        unsort(place.kept(0, i))
        return 0

    lax.fori_loop(0, place.group(0), first_half, 0)
    lax.fori_loop(0, place.group(0), second_half, 0)

    def merge(k, spot):
        for copy in pass_part(k, spot):
            copy.wait_recv()
        mine = rows_to_columns(r.lrow[spot][0:1])
        landed = place.landing(k, spot)
        other = rows_to_columns(r.lrow_in[landed][0:1])
        highest = jnp.maximum(mine, other)
        share = jnp.exp(mine - highest)
        share_in = jnp.exp(other - highest)
        both = share + share_in
        merged = (r.part[spot].astype(F32) * share + r.part_in[landed].astype(F32) * share_in) / both
        return merged, jnp.transpose(highest + jnp.log(both))[0:8]

    for k in range(cfg.bits - 1):
        for giving in (True, False):
            for i in range(place.group(k + 1)):
                spot = place.given(k + 1, i) if giving else place.kept(k + 1, i)
                merged, joint = merge(k, spot)
                r.part[spot] = merged
                r.lrow[spot] = joint
                if giving:
                    for copy in pass_part(k + 1, spot):
                        copy.start()
    merged, joint = merge(cfg.bits - 1, place.member)
    r.comb[...] = merged
    r.joint[...] = joint
    for head in range(heads):
        r.low_out[head] = merged[head * tok : (head + 1) * tok].astype(BF16)
    back = z_exchange(
        cfg, place, lambda head: r.low_out.at[head], lambda head: r.low_in.at[head], r.csend, r.crecv
    )
    r.low_in[place.head] = r.low_out[place.head]
    weights.need(2)
    for step in range(1, heads):
        z_arrival(place, r.low_in.at[place.z_source(step)], r.crecv, step).wait_recv()
    low = jnp.concatenate([r.low_in[head] for head in range(heads)], axis=1)

    turned_mix = Turned(place, 3, low, r.turned_mix, r.lhs_mix, r)

    def finish_sends():
        for copy in sent + back:
            copy.wait_send()
        for k in range(cfg.bits):
            for i in range(place.group(k)):
                for copy in pass_part(k, place.given(k, i)):
                    copy.wait_send()
        turned_mix.start()
        normed_sent.extend(pass_normed(1))

    normed_sent = []
    r.low_own[...] = low
    passed = remote(r.low_own, r.low_other, r.msend.at[1], r.mrecv.at[1], place.y_peer())
    passed.start()
    own = dot(low, r.wm[...])
    finish_sends()
    swapped.wait()
    if first:
        weights.release(2)
    passed.wait()
    mixed = r.first[...] + (own + dot(r.low_other[...], r.wm_other[...])) + r.mix_bias[one, :]
    r.mixed[...] = mixed
    normed_two = norm_parts(mixed)[0] * r.forward_gain[one, :] + r.forward_shift[one, :]
    normed_two = normed_two.astype(BF16)
    weights.need(3)
    hidden = dot(normed_two, r.we[...]) + r.expand_bias[one, :]
    curve = 0.5 * (1.0 + lax.erf(hidden * math.sqrt(0.5)))
    active = (hidden * curve).astype(BF16)
    weights.need(4)

    def turn():
        turned_shrink = Turned(place, 2, active, r.turned_shrink, r.lhs_shrink, r)
        turned_shrink.start()
        turned_expand = Turned(place, 1, normed_two, r.turned_expand, r.lhs_expand, r)
        turned_expand.start()
        bell = jnp.exp(-0.5 * hidden * hidden) * (1.0 / math.sqrt(2.0 * math.pi))
        r.slope[...] = curve + hidden * bell
        pending.extend([turned_shrink, turned_expand])

    pending = [turned_mix]
    moved = [lambda: weights.release(3, 4)] if first else []
    branch = y_sum(place, r, 1, lambda at: dot(active, r.ws[:, at]), turn, moved)
    r.renewed[...] = r.second[...] + branch + r.shrink_bias[one, :]

    def finish_turned():
        for turned in pending:
            turned.finish()
        for half in range(2):
            for step in range(1, heads):
                spot = column(place.z_source(step), half)
                z_arrival(place, spot, r.nrecv.at[half], step).wait_recv()

    def finish_normed():
        for copy in normed_sent:
            copy.wait_send()

    return finish_normed, finish_turned


def unsort_pick(cfg, rank_ref, spot, base, rows):
    band = cfg.heads * cfg.tok
    ranks = rank_ref[0:1, pl.ds(pl.multiple_of(spot * band, band), band)]
    ranks = rows_to_columns(ranks.astype(F32)).astype(jnp.int32)[:, 0:1]
    places = base + lax.broadcasted_iota(jnp.int32, (band, rows), 1)
    if cfg.parts > 1:
        places = places % cfg.total
    return (ranks == places).astype(BF16)


IN_COUNT = len(Streams._fields) + len(Params._fields)


def forward_call(cfg, layer, streams, params):
    scratch = common_scratch(cfg) | forward_scratch(cfg)
    sems = forward_sems(cfg, 1)
    whole = pl.BlockSpec(memory_space=pltpu.VMEM)
    apart = pl.BlockSpec(memory_space=pl.ANY)
    specs = Params(*[whole] * len(params))._replace(
        wq_hbm=apart, wv_hbm=apart, wm_hbm=apart, we_hbm=apart, ws_hbm=apart
    )
    outs = pl.pallas_call(
        functools.partial(forward_kernel, cfg, layer, list(scratch), list(sems)),
        out_shape=[jax.ShapeDtypeStruct(*shape) for shape in saved_shapes(cfg)],
        in_specs=[whole] * len(streams) + list(specs),
        out_specs=[whole] * len(Kept._fields),
        scratch_shapes=list(scratch.values()) + list(sems.values()),
        compiler_params=pltpu.CompilerParams(
            collective_id=layer, has_side_effects=True, vmem_limit_bytes=VMEM_LIMIT
        ),
        name=f"forward_{layer}",
    )(*streams, *params)
    return Kept(*outs)


def lines_of(cfg, extent):
    deep = extent // cfg.seq
    return (cfg.heads, deep, cfg.plane * cfg.tok), BF16 if deep % 16 == 0 else F32


def turned_of(cfg, extent):
    (heads, deep, _), kind = lines_of(cfg, extent)
    return pltpu.VMEM((heads, cfg.plane, deep, cfg.tok), kind)


def saved_shapes(cfg):
    tok, feats, band = cfg.tok, cfg.feats, cfg.heads * cfg.tok
    return Kept(
        second=((tok, feats), F32),
        mixed=((tok, feats), F32),
        sorted=((cfg.ext, 2 * DH), BF16),
        comb=((band, DH), F32),
        joint=((8, band), F32),
        slope=((tok, cfg.hid), F32),
        rank=((8, cfg.total), jnp.int32),
        lhs_qv=((feats, band), BF16),
        lhs_expand=lines_of(cfg, feats),
        lhs_shrink=lines_of(cfg, cfg.hid),
        lhs_mix=lines_of(cfg, cfg.width),
    )


class Job(NamedTuple):
    name: str
    side: str
    number: int
    rows: int
    columns: int
    fold: int

    def scratch(self, cfg):
        deep, wide = self.rows * self.fold, self.columns // self.fold
        return {
            "rhs" + self.side: pltpu.VMEM((cfg.plane * cfg.tok, self.columns), BF16),
            "prod" + self.name: pltpu.VMEM((cfg.heads, deep, wide), BF16),
            "zin" + self.name: pltpu.VMEM((3, deep, wide), BF16),
        }


def slots_of(cfg):
    return LAYERS if cfg.parts == 1 else 1


def jobs_of(cfg):
    share = cfg.feats // cfg.seq
    mix = cfg.width // cfg.seq
    return (
        Job("s", "s", 0, cfg.hid // cfg.seq, cfg.feats, 1),
        Job("m", "m", 1, mix, cfg.feats, 1 if mix % 16 == 0 else 2),
    ) + tuple(
        Job(f"e{i}", f"e{i}", 2 + i, share, cfg.feats, 1) for i in range(cfg.hid // cfg.feats)
    )


def backward_scratch(cfg):
    tok, heads, plane, bits = cfg.tok, cfg.heads, cfg.plane, cfg.bits
    band = heads * tok
    dma = pltpu.SemaphoreType.DMA
    return dict(
        gs=pltpu.VMEM((heads, tok, DH), BF16),
        gtokens=pltpu.VMEM((cfg.total, 2 * DH), BF16),
        arow=pltpu.VMEM((LAYERS, plane, 8, band), F32),
        gsorted=pltpu.VMEM((cfg.rows, DH), BF16),
        stats=pltpu.VMEM((cfg.rows, LANES), F32),
        keys=pltpu.VMEM((cfg.ext, DH), BF16),
        dq=pltpu.VMEM((cfg.ext, DH), F32),
        dk=pltpu.VMEM((cfg.ext, DH), F32),
        dv=pltpu.VMEM((cfg.ext, DH), F32),
        grads=pltpu.VMEM((cfg.ext, 2 * DH), BF16),
        part=pltpu.VMEM((plane, band, 2 * DH), BF16),
        part_in=pltpu.VMEM((plane, band, 2 * DH), BF16),
        home_out=pltpu.VMEM((heads, tok, 2 * DH), BF16),
        home_in=pltpu.VMEM((heads, tok, 2 * DH), BF16),
        vectors=pltpu.VMEM((8, cfg.feats), F32),
        vys=pltpu.VMEM((8, cfg.feats), F32),
        vyr=pltpu.VMEM((8, cfg.feats), F32),
        vysem=dma((2,)),
        **{key: value for job in jobs_of(cfg) for key, value in job.scratch(cfg).items()},
        vbuf=pltpu.VMEM((LAYERS, plane, heads, 8, LANES), F32),
        vin=pltpu.VMEM((LAYERS, plane, heads, 8, LANES), F32),
        vz=pltpu.VMEM((LAYERS, heads, 8, LANES), F32),
        lsem=dma((LAYERS, len(Kept._fields))),
        zsend=dma((LAYERS, heads)),
        zrecv=dma((LAYERS, heads)),
        gsend=dma((LAYERS, bits, heads, plane)),
        grecv=dma((LAYERS, heads, plane)),
        asend=dma((LAYERS, bits, 1, plane)),
        arecv=dma((LAYERS, 1, plane)),
        psend=dma((LAYERS, bits, plane)),
        precv=dma((LAYERS, bits, plane)),
        csend=dma((LAYERS, heads)),
        crecv=dma((LAYERS, heads)),
        rsend=dma((len(jobs_of(cfg)), bits, 1, plane)),
        rrecv=dma((len(jobs_of(cfg)), 1, plane)),
        usend=dma((len(jobs_of(cfg)), 3)),
        urecv=dma((len(jobs_of(cfg)), 3)),
        qbuf=pltpu.VMEM((plane, heads, cfg.feats // cfg.seq, 2 * DH), BF16),
        qin=pltpu.VMEM((plane, heads, cfg.feats // cfg.seq, 2 * DH), BF16),
        qz=pltpu.VMEM((heads, cfg.feats // cfg.seq, 2 * DH), BF16),
        qsend=dma((bits + heads,)),
        qrecv=dma((bits + heads,)),
        vsend=dma((LAYERS, bits + heads)),
        vrecv=dma((LAYERS, bits + heads)),
    )


class Unit:
    def __init__(self, place, fill, done, buf, arrive, zbuf, send, recv):
        self.place, self.fill, self.done = place, fill, done
        self.buf, self.arrive, self.zbuf, self.send, self.recv = buf, arrive, zbuf, send, recv

    def halved(self, k):
        place, plane = self.place, self.place.cfg.plane
        group = place.group(k)
        start = plane - plane // 2**k
        shape = (group, 2 ** (k + 1)) + self.buf.shape[1:]
        spot = (1 - place.bit(k)) * 2**k + place.member % 2**k
        return remote(
            self.buf.reshape(*shape).at[:, spot],
            self.arrive.at[start : start + group],
            self.send.at[k],
            self.recv.at[k],
            place.bit_peer(k),
        )

    def across(self, step):
        place = self.place
        head, peer = place.z_peer(step)
        at = place.cfg.bits + step
        return remote(
            self.buf.at[place.member, head], self.zbuf.at[step], self.send.at[at], self.recv.at[at], peer
        )

    def start(self):
        self.fill(self.buf)
        self.halved(0).start()

    def fold(self):
        place, cfg = self.place, self.place.cfg
        for k in range(cfg.bits):
            self.halved(k).wait_recv()
            start = cfg.plane - cfg.plane // 2**k
            for i in range(place.group(k)):
                spot = place.kept(k, i)
                both = self.buf[spot].astype(F32) + self.arrive[start + i].astype(F32)
                self.buf[spot] = both.astype(self.buf.dtype)
            if k + 1 < cfg.bits:
                self.halved(k + 1).start()
            if k + 2 == cfg.bits:
                yield
        for step in range(1, cfg.heads):
            self.across(step).start()
        yield
        found = [(place.head, self.buf[place.member, place.head])]
        for step in range(1, cfg.heads):
            self.across(step).wait_recv()
            found.append((place.z_source(step), self.zbuf[step]))
        self.done(found)
        for k in range(cfg.bits):
            self.halved(k).wait_send()
        for step in range(1, cfg.heads):
            self.across(step).wait_send()
        yield


class Gathered:
    def __init__(self, place, job, left, right, done, r):
        self.place, self.job, self.left, self.right, self.done = place, job, left, right, done
        tok = place.cfg.tok
        self.rhs = vars(r)["rhs" + job.side]
        self.prod, self.zin = vars(r)["prod" + job.name], vars(r)["zin" + job.name]
        self.send, self.recv = r.usend.at[job.number], r.urecv.at[job.number]
        self.spread = Doubling(
            place,
            [0],
            lambda key, spot: self.rhs.at[pl.ds(pl.multiple_of(spot * tok, tok), tok), :],
            r.rsend.at[job.number],
            r.rrecv.at[job.number],
        )
        head = place.head
        self.inner = (head * (3 - head)) // 2
        self.near = head + 1 - 2 * (head % 2)
        self.far = 3 - 3 * (head // 2)

    def copy(self, number):
        place, inner = self.place, self.inner
        if number == 0:
            dest, block, slot = self.near, self.near, 0
        elif number == 1:
            dest, block, slot = self.far, self.far, 2 - inner
        else:
            other = 3 - place.head
            dest = self.near * (1 - inner) + other * inner
            block = (3 - self.near) * (1 - inner) + other * inner
            slot = 2 - inner
        return remote(
            self.prod.at[block],
            self.zin.at[slot],
            self.send.at[number],
            self.recv.at[slot],
            (dest * place.cfg.plane + place.member, place.half),
        )

    def arrival(self, slot):
        spot = self.zin.at[slot]
        return remote(spot, spot, self.send.at[slot], self.recv.at[slot], self.place.y_peer())

    def start(self):
        self.spread.block(0, self.place.member)[...] = self.right
        self.spread.offer(0)

    def forward(self):
        for k in reversed(range(1, self.place.cfg.bits)):
            self.spread.receive_bit(k)

    def multiply(self):
        cfg, job = self.place.cfg, self.job
        self.spread.receive_bit(0)
        lines = self.left[...].reshape(cfg.heads * job.rows, cfg.plane * cfg.tok).astype(BF16)
        wide = job.columns // job.fold
        found = [
            dot(lines, self.rhs[:, i * wide : (i + 1) * wide]).reshape(cfg.heads, job.rows, wide)
            for i in range(job.fold)
        ]
        found = found[0] if job.fold == 1 else jnp.concatenate(found, axis=1)
        self.prod[...] = found.astype(BF16)

        @pl.when(self.inner == 0)
        def _():
            self.copy(2).start()

        self.copy(1).start()
        self.copy(0).start()
        self.spread.finish()

    def relay(self):
        @pl.when(self.inner == 1)
        def _():
            self.arrival(2).wait_recv()
            block = 3 - self.place.head
            both = self.prod[block].astype(F32) + self.zin[2].astype(F32)
            self.prod[block] = both.astype(BF16)
            self.copy(2).start()

    def finish(self):
        self.arrival(0).wait_recv()
        self.arrival(1).wait_recv()

        @pl.when(self.inner == 0)
        def _():
            self.arrival(2).wait_recv()

        total = self.prod[self.place.head].astype(F32)
        total = total + self.zin[0].astype(F32) + self.zin[1].astype(F32)
        total = jnp.where(self.inner == 0, total + self.zin[2].astype(F32), total)
        wide, deep = self.job.columns // self.job.fold, self.job.rows
        for i in range(self.job.fold):
            self.done(total[i * deep : (i + 1) * deep], i * wide, wide)
        for number in range(3):
            self.copy(number).wait_send()


def backward_kernel(cfg, names, *refs):
    params, refs = Params(*refs[: len(Params._fields)]), refs[len(Params._fields) :]
    (first_cot, second_cot), refs = refs[:2], refs[2:]
    stored, held = [], []
    for _ in range(LAYERS):
        stored.append(Kept(*refs[: len(Kept._fields)]))
        refs = refs[len(Kept._fields) :]
    out, refs = Grads(*refs[: len(Grads._fields)]), refs[len(Grads._fields) :]
    for _ in range(slots_of(cfg)):
        held.append(Kept(*refs[: len(Kept._fields)]))
        refs = refs[len(Kept._fields) :]
    held = held * (LAYERS // len(held))
    r = gathered(params, out, **dict(zip(names, refs, strict=True)))
    weights = Weights(r, list(reversed(range(LAYERS))))
    weights.fetch(4, 3, 2, 0, 1)

    def saved_load(layer, ref):
        i = [ref is other for other in held[layer]].index(True)
        return pltpu.make_async_copy(stored[layer][i], ref, r.lsem.at[layer, i])

    def fetch(layer):
        k = held[layer]
        for ref in (k.slope, k.lhs_shrink, k.mixed, k.lhs_expand, k.comb, k.joint, k.sorted):
            saved_load(layer, ref).start()
        for ref in (k.rank, k.lhs_mix, k.second, k.lhs_qv):
            saved_load(layer, ref).start()

    for layer in list(reversed(range(LAYERS)))[: slots_of(cfg)]:
        fetch(layer)
    place = Place(cfg)
    place.greet()
    after = fetch if slots_of(cfg) == 1 else None
    backward_layers(cfg, place, r, weights, held, saved_load, after, first_cot, second_cot)


def backward_layers(cfg, place, r, weights, held, saved_load, fetch, first_cot, second_cot, before=None):
    tok, heads, plane, width = cfg.tok, cfg.heads, cfg.plane, cfg.width
    band = heads * tok
    share = cfg.feats // cfg.seq
    base = place.part * cfg.rows
    jobs = jobs_of(cfg)

    def weight(number, layer, left, right):
        out = (r.out_ws, r.out_wm)[number] if number < 2 else r.out_we
        first = max(number - 2, 0) * cfg.feats

        def done(total, start, wide):
            out[layer, :, first + start : first + start + wide] = total

        return Gathered(place, jobs[number], left, right, done, r)

    def attention_weights(layer, left, right):
        def fill(buf):
            for head in range(heads):
                rows = left[head * plane * share : (head + 1) * plane * share, :]
                buf[:, head] = dot(rows, right).reshape(plane, share, 2 * DH).astype(BF16)

        def done(found):
            for head, both in found:
                at = pl.ds(pl.multiple_of(head * DH, DH), DH)
                r.out_wq[layer, :, at] = both[:, :DH].astype(F32)
                r.out_wv[layer, :, at] = both[:, DH:].astype(F32)

        return Unit(place, fill, done, r.qbuf, r.qin, r.qz, r.qsend, r.qrecv)

    def vector_sums(layer):
        def fill(buf):
            deep = cfg.hid // cfg.seq
            for p in range(cfg.seq):
                at = p * share // LANES * LANES
                tile = r.vectors[:, at : at + LANES]
                at = p * deep // LANES * LANES
                line, at = 6 + at // cfg.feats, at % cfg.feats
                extra = r.vectors[line : line + 1, at : at + LANES]
                buf[p % plane, p // plane, 0:6] = tile[0:6]
                buf[p % plane, p // plane, 6:8] = jnp.broadcast_to(extra, (2, LANES))

        def done(found):
            r.out_small[layer] = sum(both for _, both in found)

        return Unit(
            place, fill, done, r.vbuf.at[layer], r.vin.at[layer], r.vz.at[layer], r.vsend.at[layer], r.vrecv.at[layer]
        )

    order = list(reversed(range(LAYERS)))
    late, small, last = None, None, None

    for layer in order:
        one = slice(layer, layer + 1)
        saved = held[layer]

        def arrived(*fields):
            if saved_load is not None:
                for field in fields:
                    saved_load(layer, field).wait()

        second_grad = second_cot if layer == order[0] else r.second_out
        first_grad = first_cot if layer == order[0] else r.first_out
        branch = second_grad[...].astype(BF16)
        arrived(saved.slope, saved.lhs_shrink)
        shrink = weight(0, layer, saved.lhs_shrink, branch)
        shrink.start()
        weights.need(4)
        hidden_grad = (dot_nt(branch, r.ws[...]) * saved.slope[...]).astype(BF16)
        weights.release(4)
        weights.need(3)
        arrived(saved.mixed, saved.lhs_expand)

        def during_two():
            r.vectors[0:1, :] = jnp.sum(branch.astype(F32), axis=0, keepdims=True)
            summed = jnp.sum(hidden_grad.astype(F32), axis=0, keepdims=True)
            for i in range(cfg.hid // cfg.feats):
                r.vectors[6 + i : 7 + i, :] = summed[:, i * cfg.feats : (i + 1) * cfg.feats]
            if late is not None:
                for job in late:
                    job.relay()
                next(last)
            shrink.forward()
            if before is not None and layer == order[0]:
                for step in before:
                    step()

        expand = [
            weight(2 + i, layer, saved.lhs_expand, hidden_grad[:, i * cfg.feats : (i + 1) * cfg.feats])
            for i in range(cfg.hid // cfg.feats)
        ]
        two_grad = y_sum(
            place,
            r,
            0,
            lambda at: dot_nt(hidden_grad, r.we[at, :]),
            during_two,
            [lambda: weights.release(3), expand[0].start],
        )
        xhat, scale = norm_parts(saved.mixed[...])
        mixed_grad = first_grad[...] + norm_back(xhat, scale, r.forward_gain[one, :], two_grad)
        r.first_out[...] = mixed_grad
        mix_low = mixed_grad.astype(BF16)
        weights.need(2)
        combined_grad = dot_nt(mix_low, r.wm[...]).astype(BF16)
        weights.release(2)
        for head in range(heads):
            r.gs[head] = combined_grad[:, head * DH : (head + 1) * DH]

        def rows_of(spot, head):
            return pl.ds(pl.multiple_of((spot * heads + head) * tok, tok), tok)

        def block(head, spot):
            return r.gtokens.at[rows_of(spot, head), :DH]

        sent = z_exchange(
            cfg,
            place,
            lambda head: r.gs.at[head],
            lambda head: block(head, place.member),
            r.zsend.at[layer],
            r.zrecv.at[layer],
        )
        block(place.head, place.member)[...] = r.gs[place.head]
        r.vectors[1:2, :] = jnp.sum(mix_low.astype(F32), axis=0, keepdims=True)
        r.vectors[2:3, :] = jnp.sum(two_grad * xhat, axis=0, keepdims=True)
        r.vectors[3:4, :] = jnp.sum(two_grad, axis=0, keepdims=True)
        arrived(saved.sorted, saved.rank, saved.comb, saved.joint, saved.lhs_mix)
        rank = saved.rank
        rows = saved.sorted
        mixing = weight(1, layer, saved.lhs_mix, mix_low)
        raw = rows[:, :DH].astype(F32)
        r.keys[...] = (raw * key_scale(raw)).astype(BF16)
        if late is not None:
            for job in late:
                job.finish()
            next(last)
            next(small)
        spread = Doubling(
            place,
            [place.z_source(step) for step in range(heads)],
            block,
            r.gsend.at[layer],
            r.grecv.at[layer],
        )
        for step in range(heads):
            if step > 0:
                spot = block(place.z_source(step), place.member)
                z_arrival(place, spot, r.zrecv.at[layer], step).wait_recv()
            spread.offer(place.z_source(step))
        mine = r.gtokens[pl.ds(pl.multiple_of(place.member * band, band), band), :DH].astype(F32)
        inner = jnp.sum(jnp.transpose(mine * saved.comb[...]), axis=0, keepdims=True)
        line = lax.broadcasted_iota(jnp.int32, (8, band), 0)
        r.arow[layer, place.member] = jnp.where(
            line == 0, saved.joint[...], jnp.broadcast_to(inner, (8, band))
        )
        extras = Doubling(
            place,
            [0],
            lambda key, spot: r.arow.at[layer, spot],
            r.asend.at[layer],
            r.arecv.at[layer],
        )
        extras.offer(0)
        shrink.multiply()
        spread.receive()
        extras.receive()
        expand[0].forward()
        expand[1].start()
        mixing.start()
        if late is not None:
            next(small)
        lines = lax.broadcasted_iota(jnp.int32, (LANES, band), 0)
        for spot in range(plane):
            pieces = split_three(r.arow[layer, spot][0:1]) + split_three(r.arow[layer, spot][1:2])
            table = jnp.zeros((LANES, band), F32)
            for i, piece in enumerate(pieces):
                table = jnp.where(lines == i, piece, table)
            r.gtokens[spot * band : (spot + 1) * band, DH:] = jnp.transpose(table).astype(BF16)

        def store_rows(c, found):
            at = pl.ds(pl.multiple_of(c * 512, 512), 512)
            r.gsorted[at, :] = found[:, :DH].astype(BF16)
            r.stats[at, :] = found[:, DH:]

        sort_rows(cfg, rank, r.gtokens, store_rows, base, 512, cfg.rows // 512)
        r.dq[0:CHUNK, :] = jnp.zeros((CHUNK, DH), F32)
        r.dk[0:CHUNK, :] = jnp.zeros((CHUNK, DH), F32)
        r.dv[0:CHUNK, :] = jnp.zeros((CHUNK, DH), F32)
        mask = window_mask()

        def attend(c):
            at = pl.multiple_of(c * CHUNK, CHUNK)
            own = pl.ds(at + CHUNK, CHUNK)
            window = pl.ds(at, 2 * CHUNK)
            query = rows[own, :DH]
            near = r.keys[window, :]
            grad = r.gsorted[pl.ds(at, CHUNK), :]
            stats = r.stats[pl.ds(at, CHUNK), :]
            joint = stats[:, 0:1] + stats[:, 1:2] + stats[:, 2:3]
            inner = stats[:, 3:4] + stats[:, 4:5] + stats[:, 5:6]
            scores = dot_nt(query, near) / math.sqrt(DH)
            scores = jnp.where(mask, scores, -1000000000.0)
            probs = jnp.exp(scores - joint)
            prob_grad = dot_nt(grad, rows[window, DH:])
            score_grad = (probs * (prob_grad - inner) / math.sqrt(DH)).astype(BF16)
            r.dq[own, :] = dot(score_grad, near)
            return dot_tn(score_grad, query), dot_tn(probs.astype(BF16), grad)

        def attend_some(i, _):
            parts = [attend(i * UNROLL + u) for u in range(UNROLL)]
            for ref, found in zip((r.dk, r.dv), zip(*parts)):
                for u in range(UNROLL):
                    at = pl.multiple_of((i * UNROLL + u) * CHUNK, CHUNK)
                    if u == 0:
                        before = pl.ds(at, CHUNK)
                        ref[before, :] = ref[before, :] + found[u][:CHUNK]
                    own = found[u][CHUNK:]
                    if u + 1 < UNROLL:
                        own = own + found[u + 1][:CHUNK]
                    ref[pl.ds(at + CHUNK, CHUNK), :] = own
            return 0

        rounds = cfg.rows // CHUNK // UNROLL
        lax.fori_loop(0, rounds // 2, attend_some, 0)
        shrink.relay()
        expand[0].multiply()
        expand[1].forward()
        lax.fori_loop(rounds // 2, rounds, attend_some, 0)
        if cfg.parts == 1:
            last = slice(cfg.rows, cfg.ext)
            r.dk[last, :] = r.dk[last, :] + r.dk[0:CHUNK, :]
            r.dv[last, :] = r.dv[last, :] + r.dv[0:CHUNK, :]
        raw = rows[:, :DH].astype(F32)
        scale = key_scale(raw)
        dk = r.dk[...]
        inner = jnp.mean(raw * dk, axis=-1, keepdims=True)
        r.grads[:, :DH] = (
            r.dq[...] + scale * dk - raw * (scale * scale * scale * inner)
        ).astype(BF16)
        r.grads[:, DH:] = r.dv[...].astype(BF16)
        skip = CHUNK if cfg.parts == 1 else 0

        def unsort(spot):
            start = base if cfg.parts == 1 else base + cfg.total - CHUNK
            pick = unsort_pick(cfg, rank, spot, start, cfg.ext - skip)
            r.part[spot] = dot(pick, r.grads[skip:, :]).astype(BF16)

        def pass_part(k, spot):
            return remote(
                r.part.at[spot],
                r.part_in.at[place.landing(k, spot)],
                r.psend.at[layer, k, spot],
                r.precv.at[layer, k, spot // 2 ** (k + 1)],
                place.bit_peer(k),
            )

        def first_half(i, _):
            unsort(place.given(0, i))
            pass_part(0, place.given(0, i)).start()
            return 0

        def second_half(i, _):
            unsort(place.kept(0, i))
            return 0

        lax.fori_loop(0, place.group(0), first_half, 0)
        lax.fori_loop(0, place.group(0), second_half, 0)
        mixing.forward()

        def merge(k, spot):
            pass_part(k, spot).wait_recv()
            other = r.part_in[place.landing(k, spot)]
            return (r.part[spot].astype(F32) + other.astype(F32)).astype(BF16)

        for k in range(cfg.bits - 1):
            for giving in (True, False):
                for i in range(place.group(k + 1)):
                    spot = place.given(k + 1, i) if giving else place.kept(k + 1, i)
                    r.part[spot] = merge(k, spot)
                    if giving:
                        pass_part(k + 1, spot).start()
        spread.finish()
        extras.finish()
        shrink.finish()
        expand[0].relay()
        merged = merge(cfg.bits - 1, place.member)
        for head in range(heads):
            r.home_out[head] = merged[head * tok : (head + 1) * tok]
        back = z_exchange(
            cfg,
            place,
            lambda head: r.home_out.at[head],
            lambda head: r.home_in.at[head],
            r.csend.at[layer],
            r.crecv.at[layer],
        )
        r.home_in[place.head] = r.home_out[place.head]
        arrived(saved.second, saved.lhs_qv)
        last = attention_weights(layer, saved.lhs_qv, merged)
        last.start()
        last = last.fold()
        weights.need(0, 1)
        xhat, scale = norm_parts(saved.second[...])
        expand[0].finish()
        next(last)
        for step in range(1, heads):
            spot = r.home_in.at[place.z_source(step)]
            z_arrival(place, spot, r.crecv.at[layer], step).wait_recv()
        query_grad = jnp.concatenate([r.home_in[head][:, :DH] for head in range(heads)], axis=1)
        value_grad = jnp.concatenate([r.home_in[head][:, DH:] for head in range(heads)], axis=1)
        one_grad = dot_nt(query_grad, r.wq[...]) + dot_nt(value_grad, r.wv[...])
        weights.release(0, 1)
        r.vys[0:1, :] = jnp.sum(one_grad * xhat, axis=0, keepdims=True)
        r.vys[1:2, :] = jnp.sum(one_grad, axis=0, keepdims=True)
        edge = remote(r.vys, r.vyr, r.vysem.at[0], r.vysem.at[1], place.y_peer())
        edge.start()
        small = vector_sums(layer)

        late = [mixing, expand[1]]
        launch = late

        def during_one():
            for copy in sent + back:
                copy.wait_send()
            for k in range(cfg.bits):
                for i in range(place.group(k)):
                    pass_part(k, place.given(k, i)).wait_send()
            edge.wait()
            r.vectors[4:6, :] = r.vys[0:2, :] + r.vyr[0:2, :]
            small.start()

        partial = one_grad
        one_grad = y_sum(
            place, r, 1, lambda at: partial[:, at], during_one, [job.multiply for job in launch]
        )
        dx = norm_back(xhat, scale, r.attention_gain[one, :], one_grad)
        r.second_out[...] = second_grad[...] + dx
        small = small.fold()
        next(small)
        if layer > 0 and fetch is not None:
            fetch(layer - 1)
    for job in late:
        job.relay()
    next(last)
    next(small)
    for job in late:
        job.finish()
    next(last)
    next(small)


def grad_shapes(cfg):
    tok, feats = cfg.tok, cfg.feats
    share = feats // cfg.seq
    return Grads(
        first_out=(tok, feats),
        second_out=(tok, feats),
        out_wq=(LAYERS, share, cfg.width),
        out_wv=(LAYERS, share, cfg.width),
        out_wm=(LAYERS, cfg.width // cfg.seq, feats),
        out_we=(LAYERS, share, cfg.hid),
        out_ws=(LAYERS, cfg.hid // cfg.seq, feats),
        out_small=(LAYERS, 8, LANES),
    )


def backward_call(cfg, params, cotangents, saved):
    scratch = common_scratch(cfg) | backward_scratch(cfg)
    shapes = grad_shapes(cfg)
    whole = pl.BlockSpec(memory_space=pltpu.VMEM)
    apart = pl.BlockSpec(memory_space=pl.ANY)
    specs = Params(*[apart] * len(params))._replace(attention_gain=whole, forward_gain=whole)
    held = [pltpu.VMEM(*shape) for shape in saved_shapes(cfg)] * slots_of(cfg)
    outs = pl.pallas_call(
        functools.partial(backward_kernel, cfg, list(scratch)),
        out_shape=[jax.ShapeDtypeStruct(shape, F32) for shape in shapes],
        in_specs=list(specs) + [whole] * 2 + [apart] * (LAYERS * len(Kept._fields)),
        out_specs=[whole] * len(shapes),
        scratch_shapes=held + list(scratch.values()),
        compiler_params=pltpu.CompilerParams(
            collective_id=LAYERS, has_side_effects=True, vmem_limit_bytes=VMEM_LIMIT
        ),
        name="backward",
    )(*params, *cotangents, *[array for kept in saved for array in kept])
    return Grads(*outs)


def whole_kernel(cfg, common, forth, sems, back, *refs):
    sources, refs = refs[: IN_COUNT + 2], refs[IN_COUNT + 2 :]
    targets, refs = refs[: 2 + len(Grads._fields)], refs[2 + len(Grads._fields) :]
    inputs, refs = list(refs[: IN_COUNT + 2]), refs[IN_COUNT + 2 :]
    result_two, out = refs[0], Grads(*refs[1 : 1 + len(Grads._fields)])
    refs = refs[1 + len(Grads._fields) :]
    in_sem, out_sem, refs = refs[0], refs[1], refs[2:]
    held = []
    for _ in range(LAYERS):
        held.append(Kept(*refs[: len(Kept._fields)]))
        refs = refs[len(Kept._fields) :]
    shared, refs = dict(zip(common, refs)), refs[len(common) :]
    ahead, refs = dict(zip(forth, refs)), refs[len(forth) :]
    signals, refs = dict(zip(sems, refs)), refs[len(sems) :]
    loads = []
    for i, source in enumerate(sources):
        if i in apart_inputs():
            inputs[i] = source
        else:
            loads.append((i, pltpu.make_async_copy(source, inputs[i], in_sem.at[i])))
    streams, params = Streams(*inputs[:3]), Params(*inputs[3:IN_COUNT])
    early = (streams.second, params.attention_gain, params.attention_shift)
    early = [i for i, ref in enumerate(inputs) if any(ref is other for other in early)]
    loads = {i: load for i, load in loads}
    for i in early:
        loads[i].start()

    def fetch_rest():
        for i in loads:
            if i not in early:
                loads[i].start()

    def need_rest():
        for i in loads:
            if i not in early:
                loads[i].wait()

    place = Place(cfg)
    weights, before = None, None
    first, second = streams.first, streams.second
    held[0] = held[0]._replace(second=second)
    for layer in range(LAYERS):
        r = gathered(held[layer], params, **shared, **ahead)
        vars(r).update({name: ref.at[layer] for name, ref in signals.items()})
        r.first, r.buckets = first, streams.buckets
        r.renewed = result_two if layer == LAYERS - 1 else held[layer + 1].second
        if weights is None:
            weights = Weights(r, [0, 1, 0])
            weights.fetch(0, 1)
            weights.rest = fetch_rest, need_rest
            for i in early:
                loads[i].wait()
        before = forward_layer(cfg, place, layer, r, weights, layer == 0, before)
        first, second = r.mixed, r.renewed
    stores = [
        pltpu.make_async_copy(source, target, out_sem.at[i])
        for i, (source, target) in enumerate(zip((first, second) + tuple(out), targets))
    ]
    for store in stores[:2]:
        store.start()
    r = gathered(params, out, **shared, **dict(zip(back, refs, strict=True)))
    backward_layers(cfg, place, r, weights, held, None, None, *inputs[IN_COUNT:], before)
    for store in stores[2:]:
        store.start()
    for store in stores:
        store.wait()


def apart_inputs():
    names = Streams._fields + Params._fields
    return [i for i, name in enumerate(names) if name.endswith("_hbm")]


def whole_call(cfg, streams, cotangents, params):
    common, forth, back = common_scratch(cfg), forward_scratch(cfg), backward_scratch(cfg)
    sems = forward_sems(cfg, LAYERS)
    apart = pl.BlockSpec(memory_space=pl.ANY)
    unused, shapes = ((8, LANES), F32), saved_shapes(cfg)
    held = [shapes._replace(second=unused)] + [shapes] * (LAYERS - 1)
    held = [pltpu.VMEM(*shape) for kept in held for shape in kept]
    operands = (*streams, *params, *cotangents)
    inputs = [
        pltpu.VMEM(*(unused if i in apart_inputs() else (array.shape, array.dtype)))
        for i, array in enumerate(operands)
    ]
    results = [(cfg.tok, cfg.feats)] * 2 + list(grad_shapes(cfg))
    dma = pltpu.SemaphoreType.DMA
    scratch = inputs + [pltpu.VMEM(shape, F32) for shape in results[1:]]
    scratch += [dma((len(inputs),)), dma((len(results),))] + held
    scratch += [value for part in (common, forth, sems, back) for value in part.values()]
    outs = pl.pallas_call(
        functools.partial(whole_kernel, cfg, list(common), list(forth), list(sems), list(back)),
        out_shape=[jax.ShapeDtypeStruct(shape, F32) for shape in results],
        in_specs=[apart] * len(operands),
        out_specs=[apart] * len(results),
        scratch_shapes=scratch,
        compiler_params=pltpu.CompilerParams(
            collective_id=0, has_side_effects=True, vmem_limit_bytes=VMEM_LIMIT
        ),
        name="whole",
    )(*operands)
    return outs[0], outs[1], Grads(*outs[2:])


def finish_kernel(cfg, count, *refs):
    sources, refs = refs[: count + 1], refs[count + 1 :]
    targets, refs = refs[: count + 7], refs[count + 7 :]
    halfway, refs = refs[: count + 1], refs[count + 1 :]
    pieces, sem = refs[:7], refs[7]

    def leg(number, i):
        ends = (sources[i], halfway[i]) if number == 0 else (halfway[i], targets[i])
        return pltpu.make_async_copy(*ends, sem.at[number, i])

    def small_leg(line):
        return pltpu.make_async_copy(pieces[line], targets[count + line], sem.at[1, count + line])

    for i in reversed(range(count + 1)):
        leg(0, i).start()
    leg(0, count).wait()
    index = lax.axis_index("seq")
    for line, piece in enumerate(pieces):
        share = piece.shape[1]
        tile = halfway[count][:, line, :]
        found = jnp.zeros(piece.shape, F32)
        for k in range(LANES // share):
            here = index % (LANES // share) == k
            found = jnp.where(here, tile[:, k * share : (k + 1) * share], found)
        piece[...] = found
        small_leg(line).start()
    for i in reversed(range(count)):
        leg(0, i).wait()
        leg(1, i).start()
    for line in range(7):
        small_leg(line).wait()
    for i in range(count):
        leg(1, i).wait()


def finish_call(cfg, small, arrays):
    apart = pl.BlockSpec(memory_space=pl.ANY)
    count = len(arrays)
    shapes = [(LAYERS, cfg.feats // cfg.seq)] * 6 + [(LAYERS, cfg.hid // cfg.seq)]
    halfway = [array.shape for array in arrays] + [small.shape]
    outs = pl.pallas_call(
        functools.partial(finish_kernel, cfg, count),
        out_shape=[jax.ShapeDtypeStruct(shape, F32) for shape in halfway[:-1] + shapes],
        in_specs=[apart] * (count + 1),
        out_specs=[apart] * (count + 7),
        scratch_shapes=[pltpu.VMEM(shape, F32) for shape in halfway + shapes]
        + [pltpu.SemaphoreType.DMA((2, count + 7))],
        compiler_params=pltpu.CompilerParams(vmem_limit_bytes=VMEM_LIMIT),
        name="finish",
    )(*arrays, small)
    return outs[:count], outs[count:]


def shards(stream_one, stream_two, cotangent_one, cotangent_two, bucket_numbers, *params):
    cfg = sizes_of(lax.axis_size("seq"), stream_one, params[0], params[4])
    params = Params(*params)
    first, second = stream_one, stream_two
    if cfg.parts == 1:
        streams = Streams(first, second, bucket_numbers)
        first, second, out = whole_call(cfg, streams, (cotangent_one, cotangent_two), params)
    else:
        saved = []
        for layer in range(LAYERS):
            kept = forward_call(cfg, layer, Streams(first, second, bucket_numbers), params)
            saved.append(kept._replace(second=second))
            first, second = kept.mixed, kept.second
        out = backward_call(cfg, params, (cotangent_one, cotangent_two), saved)
    arrays = (first, second) + tuple(out)[:-1]
    (first, second, one, two, wq, wv, wm, we, ws), small = finish_call(cfg, out.out_small, arrays)
    return (
        first,
        second,
        one,
        two,
        wq,
        wv,
        wm,
        small[1],
        we,
        small[6],
        ws,
        small[0],
        small[4],
        small[5],
        small[2],
        small[3],
    )


def solution(mesh):
    in_specs = (
        P("seq", None),
        P("seq", None),
        P("seq", None),
        P("seq", None),
        P(None, None, "mp", None),
        P(None, None, "mp"),
        P(None, None, "mp"),
        P(None, "mp", None),
        P(),
        P(None, None, "mp"),
        P(None, "mp"),
        P(None, "mp", None),
        P(),
        P(),
        P(),
        P(),
        P(),
    )
    out_specs = (
        P("seq", None),
        P("seq", None),
        P("seq", None),
        P("seq", None),
        P(None, "seq", "mp"),
        P(None, "seq", "mp"),
        P(None, ("mp", "seq"), None),
        P(None, "seq"),
        P(None, "seq", "mp"),
        P(None, ("mp", "seq")),
        P(None, ("mp", "seq"), None),
        P(None, "seq"),
        P(None, "seq"),
        P(None, "seq"),
        P(None, "seq"),
        P(None, "seq"),
    )
    return jax.shard_map(shards, mesh=mesh, in_specs=in_specs, out_specs=out_specs, check_vma=False)
```
